256 devices in a mesh: gx: 8 (over y_lo, x), gy: 32 (over z, y_hi, core).
Axes of the slice: x: 4, y: 4 (y_hi: 2, y_lo: 2; y = y_hi * 2 + y_lo), z: 8, core: 2. Of those that a mesh axis runs over, the one named last changes fastest.
Arguments:
- segments: float32 [9, 2097152], P(None, ('gx', 'gy')), as said below
- pair_list: int32 [131072, 2], P(('gx', 'gy')), may hold values from 0 to 127, as said below
- pair_count: int32 [256], P(('gx', 'gy')), may hold values from 64 to 512
- send_list: int32 [1024, 16], P(('gx', 'gy')), may hold values from 0 to 63, as said below
- cell_ids: int32 [2097152], P(('gx', 'gy')), may hold values from 0 to 511, as said below
Outputs:
- forces: float32 [3, 2097152], P(None, ('gx', 'gy'))
The draws below stay inside these ranges and needn't reach their ends.
Inputs may be any that keep to these rules, and one draw needn't show every extreme that they name: `pair_list`: column 0 names a block below 64. Column 1 names another block of the same device (below 64, never equal to column 0), or a received block 64 + k*16 + j only where the neighbour of side k exists. `send_list`: each row names 16 different blocks of the sending device. `cell_ids`: segments of device d lie in cells d*2 to d*2 + 1. `segments`: the midpoints of device d (gx index ix, gy index iy) lie in [ix, ix + 1) x [iy, iy + 1) x [0, 1).
All inputs are finite; a program needn't handle non-finite values.
Results may differ from the reference program's by a relative error of at most 0.0001.
Values sent between devices are 32-bit elements; how exact they have to be, the bound alone decides.
A program may use at most 64 MiB of HBM per device.

```python
import math
import jax
import jax.numpy as jnp
from jax import lax

BLOCK = 128
BLK_DEV = 64
PAIRS_DEV = 512
GHOST = 16
CELL_DEV = 2
SEG_DEV = 8192
SEGS = 2097152
CELLS = 512
N_GX = 8
N_GY = 32


def draw_segments(key, part):
    key = jax.random.fold_in(key, 53)
    key_pos, key_line, key_burgers = jax.random.split(key, 3)
    device = jnp.arange(SEGS, dtype=jnp.int32) // SEG_DEV
    slab_x = (device // N_GY).astype(jnp.float32)
    slab_y = (device % N_GY).astype(jnp.float32)
    unit = jax.random.uniform(key_pos, (3, SEGS), jnp.float32)
    position = jnp.stack([slab_x + unit[0], slab_y + unit[1], unit[2]])
    lines = 0.3 * jax.random.normal(key_line, (3, SEGS), jnp.float32)
    burgers = jax.random.normal(key_burgers, (3, SEGS), jnp.float32)
    return jnp.concatenate([position, lines, burgers], axis=0).astype(jnp.float32)


def draw_pair_list(key, part):
    key = jax.random.fold_in(key, 23)
    keys = jax.random.split(key, 5)
    pair_total = N_GX * N_GY * PAIRS_DEV
    row_index = jnp.arange(pair_total, dtype=jnp.int32)
    device = row_index // PAIRS_DEV
    slab_x = device // N_GY
    slab_y = device % N_GY
    first = jax.random.randint(keys[0], (pair_total,), 0, BLK_DEV)
    other = (first + 1 + jax.random.randint(keys[1], (pair_total,), 0, BLK_DEV - 1)) % BLK_DEV
    side = jax.random.randint(keys[2], (pair_total,), 0, 4)
    kind = jax.random.randint(keys[3], (pair_total,), 0, 2)
    slot_index = jax.random.randint(keys[4], (pair_total,), 0, GHOST)
    present = jnp.where(side == 0, slab_x > 0, jnp.where(side == 1, slab_x < N_GX - 1, jnp.where(side == 2, slab_y > 0, slab_y < N_GY - 1)))
    ghost_id = BLK_DEV + side * GHOST + slot_index
    second = jnp.where((kind == 1) & present, ghost_id, other)
    first = jnp.where(row_index == 0, 0, first)
    second = jnp.where(row_index == 0, BLK_DEV + 4 * GHOST - 1, second)
    return jnp.stack([first, second], axis=1).astype(jnp.int32)


def draw_pair_count(key, part):
    key = jax.random.fold_in(key, 37)
    key_count, key_busy = jax.random.split(key)
    devices = N_GX * N_GY
    counts = jax.random.randint(key_count, (devices,), PAIRS_DEV // 8, PAIRS_DEV // 2 + 1)
    busiest = jax.random.randint(key_busy, (), 0, devices)
    return jnp.where(jnp.arange(devices, dtype=jnp.int32) == busiest, PAIRS_DEV, counts).astype(jnp.int32)


def draw_send_list(key, part):
    key = jax.random.fold_in(key, 61)
    row_total = N_GX * N_GY * 4
    column = jnp.arange(BLK_DEV, dtype=jnp.int32)[None, :]
    row_index = jnp.arange(row_total, dtype=jnp.int32)[:, None]
    scores = jax.random.randint(key, (row_total, BLK_DEV), 0, 1 << 20) * BLK_DEV + column
    scores = jnp.where(row_index == 0, BLK_DEV - 1 - column, jnp.where(row_index == 1, column, scores))
    order = jnp.argsort(scores, axis=1, stable=True)
    return order[:, :GHOST].astype(jnp.int32)


def draw_cell_ids(key, part):
    key = jax.random.fold_in(key, 41)
    seg_index = jnp.arange(SEGS, dtype=jnp.int32)
    device = seg_index // SEG_DEV
    offset = jax.random.randint(key, (SEGS,), 0, CELL_DEV)
    offset = jnp.where(seg_index == 0, 0, jnp.where(seg_index == SEGS - 1, CELL_DEV - 1, offset))
    return (device * CELL_DEV + offset).astype(jnp.int32)


def setup_inputs(seed: int = 0) -> dict:
    seeds = jax.random.split(jax.random.key(seed), 6)
    return {
        "segments": draw_segments(jax.random.fold_in(seeds[5], 71), 0),
        "pair_list": draw_pair_list(jax.random.fold_in(seeds[5], 71), 0),
        "pair_count": draw_pair_count(jax.random.fold_in(seeds[5], 71), 0),
        "send_list": draw_send_list(jax.random.fold_in(seeds[5], 71), 0),
        "cell_ids": draw_cell_ids(jax.random.fold_in(seeds[5], 71), 0),
    }


strength = 0.2
core_sq = 0.05
far_gain = 0.5
far_core_sq = 0.1

def pair_terms(first, second, live_mask):
    offset = first[:, 0:3, :, None] - second[:, 0:3, None, :]
    dist_sq = lax.optimization_barrier(jnp.sum(offset * offset, axis=1)) + core_sq
    burgers_dot = lax.optimization_barrier(jnp.sum(first[:, 6:9, :, None] * second[:, 6:9, None, :], axis=1))
    line_dot = lax.optimization_barrier(jnp.sum(first[:, 3:6, :, None] * second[:, 3:6, None, :], axis=1))
    coupling = strength * burgers_dot * line_dot / (dist_sq * jnp.sqrt(dist_sq)) * live_mask[:, None, None]
    pushed = coupling[:, None] * offset
    return (lax.optimization_barrier(jnp.sum(pushed, axis=3)), -lax.optimization_barrier(jnp.sum(pushed, axis=2)))

def cell_centers(cell_total, per_device, span_y):
    cell_index = jnp.arange(cell_total, dtype=jnp.int32)
    device = cell_index // per_device
    sub_cell = (cell_index % per_device).astype(jnp.float32)
    centre_x = (device // span_y).astype(jnp.float32) + 0.5
    centre_y = (device % span_y).astype(jnp.float32) + (sub_cell + 0.5) / per_device
    centre_z = jnp.full((cell_total,), 0.5, jnp.float32)
    return jnp.stack([centre_x, centre_y, centre_z])

def far_terms(position, weight, moments, centers):
    offset = position[:, :, None] - centers[:, None, :]
    dist_sq = lax.optimization_barrier(jnp.sum(offset * offset, axis=0)) + far_core_sq
    falloff = moments[None, :] / (dist_sq * jnp.sqrt(dist_sq))
    return far_gain * weight[None, :] * lax.optimization_barrier(jnp.sum(falloff[None] * offset, axis=2))

def reference(segments, pair_list, pair_count, send_list, cell_ids):
    devices = N_GX * N_GY
    block_total = devices * BLK_DEV
    blocks = segments.reshape(9, block_total, BLOCK).transpose(1, 0, 2)
    pair_rows = jnp.arange(devices * PAIRS_DEV, dtype=jnp.int32)
    device = pair_rows // PAIRS_DEV
    is_live = (pair_rows % PAIRS_DEV < pair_count[device]).astype(jnp.float32)
    first_id = device * BLK_DEV + pair_list[:, 0]
    second_local = pair_list[:, 1]
    is_ghost = second_local >= BLK_DEV
    ghost_pos = jnp.maximum(second_local - BLK_DEV, 0)
    side = jnp.clip(ghost_pos // GHOST, 0, 3)
    slot_index = ghost_pos % GHOST
    neighbour_step = jnp.array([-N_GY, N_GY, -1, 1], jnp.int32)
    sender_dir = jnp.array([1, 0, 3, 2], jnp.int32)
    sender = jnp.clip(device + neighbour_step[side], 0, devices - 1)
    sent_block = send_list[sender * 4 + sender_dir[side], slot_index]
    second_id = jnp.where(is_ghost, sender * BLK_DEV + sent_block, device * BLK_DEV + second_local)
    batch_size = math.gcd(devices * PAIRS_DEV, 256)

    def add_pairs(forces, items):
        first_ids, second_ids, live = items
        force_first, force_second = pair_terms(blocks[first_ids], blocks[second_ids], live)
        return (forces.at[first_ids].add(force_first).at[second_ids].add(force_second), None)
    forces = jnp.zeros((block_total, 3, BLOCK), jnp.float32)
    forces, _ = lax.scan(add_pairs, forces, (first_id.reshape(-1, batch_size), second_id.reshape(-1, batch_size), is_live.reshape(-1, batch_size)))
    self_size = math.gcd(block_total, 256)

    def add_self(forces, block_ids):
        group = blocks[block_ids]
        force_first, _ = pair_terms(group, group, jnp.ones((self_size,), jnp.float32))
        return (forces.at[block_ids].add(force_first), None)
    forces, _ = lax.scan(add_self, forces, jnp.arange(block_total, dtype=jnp.int32).reshape(-1, self_size))
    pair_force = forces.transpose(1, 0, 2).reshape(3, SEGS)
    weight = lax.optimization_barrier(jnp.sum(segments[3:6] * segments[6:9], axis=0))
    moments = jax.ops.segment_sum(weight, cell_ids, CELLS)
    centers = cell_centers(CELLS, CELL_DEV, N_GY)
    far_size = math.gcd(SEGS, 2048)
    positions = segments[0:3].reshape(3, -1, far_size).transpose(1, 0, 2)
    weights = weight.reshape(-1, far_size)
    far_force = lax.map(lambda items: far_terms(items[0], items[1], moments, centers), (positions, weights))
    far_force = far_force.transpose(1, 0, 2).reshape(3, SEGS)
    return pair_force + far_force
```

```python
import functools

import jax
import jax.numpy as jnp
from jax import lax
from jax.experimental import pallas as pl
from jax.experimental.pallas import tpu as pltpu
from jax.sharding import PartitionSpec as P

f32, bf16, i32 = jnp.float32, jnp.bfloat16, jnp.int32
MESH = pl.DeviceIdType.MESH
BLOCK = 128
OWN = 64
GHOST = 16
ALL = OWN + 4 * GHOST
TRASH = ALL
PAIRS = 512
NX, NY = 8, 32
GROUP = 8
KDIM = 96
ROWS = 9 * GHOST

strength = 0.2
core_sq = 0.05
far_gain = 0.5
far_core_sq = 0.1


def mm(a, b, nt=False):
    dims = (((1,), (1 if nt else 0,)), ((), ()))
    return lax.dot_general(a, b, dims, preferred_element_type=f32)


def split3(x):
    h = x.astype(bf16)
    r = x - h.astype(f32)
    m = r.astype(bf16)
    return h, m, (r - m.astype(f32)).astype(bf16)


def rows16(parts):
    missing = 16 - sum(p.shape[0] for p in parts)
    if missing:
        parts = parts + [jnp.zeros((missing, BLOCK), f32)]
    return jnp.concatenate(parts, axis=0)


def eye128():
    shape = (BLOCK, BLOCK)
    return (lax.broadcasted_iota(i32, shape, 0) == lax.broadcasted_iota(i32, shape, 1)).astype(bf16)


def neighbours(ix, iy):
    return (
        (lax.rem(ix + NX - 1, NX), iy),
        (lax.rem(ix + 1, NX), iy),
        (ix, lax.rem(iy + NY - 1, NY)),
        (ix, lax.rem(iy + 1, NY)),
    )


def exchange(send_list, seg, cells, ghost_out, mom_out, main, last, out_buf, in_buf, row, part, row2, table,
             s_sem, r_sem, s1, r1, s2, r2):
    ix, iy = lax.axis_index("gx"), lax.axis_index("gy")
    barrier = pltpu.get_barrier_semaphore()

    def greet_y(o, _):
        pl.semaphore_signal(barrier, inc=1, device_id=(ix, lax.rem(iy + o, NY)), device_id_type=MESH)
        return 0

    def greet_x(o, _):
        pl.semaphore_signal(barrier, inc=1, device_id=(lax.rem(ix + o, NX), iy), device_id_type=MESH)
        return 0

    lax.fori_loop(1, NY, greet_y, 0)
    lax.fori_loop(1, NX, greet_x, 0)
    for k in range(OWN):
        main[k] = seg[0:8, k * BLOCK : (k + 1) * BLOCK]
        last[k] = seg[8:9, k * BLOCK : (k + 1) * BLOCK]
    for q in range(4):
        for j in range(GHOST):
            k = send_list[q, j]
            out_buf[q, 8 * j : 8 * j + 8, :] = main[k]
            out_buf[q, 8 * GHOST + j : 8 * GHOST + j + 1, :] = last[k]
    c = jnp.sum(seg[3:6, :] * seg[6:9, :], axis=0, keepdims=True)
    first = 2 * (ix * NY + iy)
    ids = cells[...]
    m0 = jnp.sum(jnp.where(ids == first, c, 0.0))
    m1 = jnp.sum(jnp.where(ids == first + 1, c, 0.0))
    lane = lax.broadcasted_iota(i32, (1, BLOCK), 1)
    mine = jnp.where(lane == 2 * iy, m0, jnp.where(lane == 2 * iy + 1, m1, 0.0))
    row[...] = mine
    part[NY - 1 : NY, :] = mine
    pl.semaphore_wait(barrier, NY - 1 + NX - 1)
    copies = []
    for q, dev in enumerate(neighbours(ix, iy)):
        copies.append(
            pltpu.make_async_remote_copy(
                src_ref=out_buf.at[q], dst_ref=in_buf.at[q ^ 1], send_sem=s_sem.at[q],
                recv_sem=r_sem.at[q ^ 1], device_id=dev, device_id_type=MESH,
            )
        )
        copies[-1].start()

    def send_y(o, _):
        pltpu.make_async_remote_copy(
            src_ref=row, dst_ref=part.at[pl.ds(o - 1, 1)], send_sem=s1, recv_sem=r1,
            device_id=(ix, lax.rem(iy + o, NY)), device_id_type=MESH,
        ).start()
        return 0

    lax.fori_loop(1, NY, send_y, 0)
    pltpu.make_async_copy(part.at[0 : NY - 1], part.at[0 : NY - 1], r1).wait()
    slab = jnp.sum(part[...], axis=0, keepdims=True)
    row2[...] = slab
    table[pl.ds(NX - 1, 1), :] = slab

    def send_x(o, _):
        pltpu.make_async_remote_copy(
            src_ref=row2, dst_ref=table.at[pl.ds(o - 1, 1)], send_sem=s2, recv_sem=r2,
            device_id=(lax.rem(ix + o, NX), iy), device_id_type=MESH,
        ).start()
        return 0

    lax.fori_loop(1, NX, send_x, 0)
    for cp in copies:
        cp.wait()
    ghost_out[...] = in_buf[...]
    pltpu.make_async_copy(table.at[0 : NX - 1], table.at[0 : NX - 1], r2).wait()
    mom_out[...] = table[...]
    pltpu.make_async_copy(part.at[0 : NY - 1], part.at[0 : NY - 1], s1).wait()
    pltpu.make_async_copy(table.at[0 : NX - 1], table.at[0 : NX - 1], s2).wait()


def features(raw, cx, cy, eye, a_ref, b_ref, p_ref, k, with_a):
    x, y, z = raw[0:1] - cx, raw[1:2] - cy, raw[2:3] - 0.5
    l, b = raw[3:6], raw[6:9]
    u = [b[0:1] * l, b[1:2] * l, b[2:3] * l]
    norm = x * x + y * y + z * z
    one = jnp.ones((1, BLOCK), f32)
    bq = split3(rows16(u))
    bd = split3(rows16([jnp.zeros((9, BLOCK), f32), x, y, z, norm, one]))
    order = (0, 1, 0, 1, 2, 0)
    b_ref[k, :, 0:BLOCK] = jnp.concatenate([bq[o] for o in order], axis=0)
    b_ref[k, :, BLOCK:] = jnp.concatenate([bd[o] for o in order], axis=0)
    pos = [t.astype(f32) for t in split3(x) + split3(y) + split3(z)]
    px = rows16(pos + [one]).astype(bf16)
    p_ref[k] = jnp.concatenate([px, px], axis=1)
    if with_a:
        fa = split3(
            rows16([strength * t for t in u] + [-2.0 * x, -2.0 * y, -2.0 * z, one, norm + core_sq])
        )
        at = jnp.concatenate([fa[o] for o in (0, 0, 1, 1, 0, 2)], axis=0)
        at = jnp.concatenate([at, jnp.zeros((BLOCK - KDIM, BLOCK), bf16)], axis=0)
        a_ref[k] = mm(eye, at, nt=True).astype(bf16)


def finish(acc, x, y, z):
    s = acc[9:10]
    return jnp.concatenate(
        [
            x * s - (acc[0:1] + acc[1:2] + acc[2:3]),
            y * s - (acc[3:4] + acc[4:5] + acc[5:6]),
            z * s - (acc[6:7] + acc[7:8] + acc[8:9]),
        ],
        axis=0,
    )


def pairs(count, rows, send_list, seg, ghost, own_out, ghost_out, inv_out, a_ref, b_ref, p_ref,
          qd, ww, rr, acc_a, acc_b):
    ix, iy = lax.axis_index("gx"), lax.axis_index("gy")
    cx, cy = ix.astype(f32) + 0.5, iy.astype(f32) + 0.5
    eye = eye128()

    def own_block(k):
        return seg[:, pl.ds(pl.multiple_of(k * BLOCK, BLOCK), BLOCK)]

    def ghost_block(q, j):
        return jnp.concatenate(
            [ghost[q, pl.ds(pl.multiple_of(8 * j, 8), 8), :], ghost[q, pl.ds(8 * GHOST + j, 1), :]], axis=0
        )

    def build_own(k, _):
        features(own_block(k), cx, cy, eye, a_ref, b_ref, p_ref, k, True)
        return 0

    def build_ghost(j, _):
        for q in range(4):
            features(ghost_block(q, j), cx, cy, eye, a_ref, b_ref, p_ref, OWN + GHOST * q + j, False)
        return 0

    lax.fori_loop(0, OWN, build_own, 0, unroll=4)
    lax.fori_loop(0, GHOST, build_ghost, 0)
    for acc in (acc_a, acc_b):
        acc[...] = jnp.zeros_like(acc)

    def step(t, _):
        for s in range(GROUP):
            o = t * (4 * GROUP) + 4 * s
            acc_a[rows[o + 2]] += rr[s, 0]
            acc_b[rows[o + 3]] += rr[s, 1]
            o = o + 4 * GROUP
            rr[s, 0] = mm(p_ref[rows[o + 1]], jnp.concatenate([ww[s, 0:BLOCK], ww[s, BLOCK:]], axis=1), nt=True)
            rr[s, 1] = mm(p_ref[rows[o]], ww[s])
            r = lax.rsqrt(qd[s, :, BLOCK:])
            w = (qd[s, :, 0:BLOCK] * r) * (r * r)
            wh = w.astype(bf16)
            ww[s, 0:BLOCK] = wh
            ww[s, BLOCK:] = (w - wh.astype(f32)).astype(bf16)
            o = o + 8 * GROUP
            qd[s] = mm(a_ref[rows[o], :, 0:KDIM], b_ref[rows[o + 1]])
        return 0

    lax.fori_loop(0, (count[0] + OWN + GROUP - 1) // GROUP + 3, step, 0)

    def finish_own(k, _):
        raw = own_block(k)
        own_out[k] = finish(acc_a[k] + acc_b[k], raw[0:1] - cx, raw[1:2] - cy, raw[2:3] - 0.5)
        return 0

    def finish_ghost(j, _):
        for q in range(4):
            raw = ghost_block(q, j)
            f = finish(acc_b[OWN + GHOST * q + j], raw[0:1] - cx, raw[1:2] - cy, raw[2:3] - 0.5)
            ghost_out[q, j] = jnp.concatenate([f, jnp.zeros((1, BLOCK), f32)], axis=0)
        return 0

    lax.fori_loop(0, OWN, finish_own, 0, unroll=4)
    lax.fori_loop(0, GHOST, finish_ghost, 0)

    def clear(k, _):
        for q in range(4):
            inv_out[q, k] = GHOST
        return 0

    lax.fori_loop(0, OWN, clear, 0, unroll=8)
    for q in range(4):
        for j in range(GHOST):
            inv_out[q, send_list[q, j]] = j


def finale(inv, seg, mom, own, ghost, out, back_in, mb, s_sem, r_sem):
    ix, iy = lax.axis_index("gx"), lax.axis_index("gy")
    barrier = pltpu.get_barrier_semaphore()
    near = neighbours(ix, iy)
    for dev in near:
        pl.semaphore_signal(barrier, inc=1, device_id=dev, device_id_type=MESH)
    wide = jnp.concatenate([mom[...], jnp.zeros((BLOCK - NX, BLOCK), f32)], axis=0).T
    for s in range(NX):
        mb[s] = jnp.broadcast_to(wide[0 : 2 * NY, s : s + 1], (2 * NY, BLOCK))
    pl.semaphore_wait(barrier, 4)
    copies = []
    for q, dev in enumerate(near):
        copies.append(
            pltpu.make_async_remote_copy(
                src_ref=ghost.at[q], dst_ref=back_in.at[q ^ 1, 0:GHOST], send_sem=s_sem.at[q],
                recv_sem=r_sem.at[q ^ 1], device_id=dev, device_id_type=MESH,
            )
        )
        copies[-1].start()
    for q in range(4):
        back_in[q, GHOST] = jnp.zeros((4, BLOCK), f32)
    groups = 2 * NY // 8
    sub = lax.broadcasted_iota(i32, (8, BLOCK), 0).astype(f32)
    centre_x = []
    for s in range(NX):
        src = lax.rem(ix + (2 * NX - 1 - s), NX)
        centre_x.append(src.astype(f32) + 0.5)

    def far(k, _):
        blk = seg[:, pl.ds(pl.multiple_of(k * BLOCK, BLOCK), BLOCK)]
        x, y, z = blk[0:1], blk[1:2], blk[2:3] - 0.5
        wide_y = jnp.broadcast_to(y, (8, BLOCK))
        base = z * z + far_core_sq
        dx = [jnp.broadcast_to(x - cx, (8, BLOCK)) for cx in centre_x]
        dx2 = [d * d for d in dx]
        hx = [None] * NX
        fy = total = None
        for g in range(groups):
            dy = wide_y - (0.5 * sub + (4.0 * g + 0.25))
            by = dy * dy + base
            gy = None
            for s in range(NX):
                r = lax.rsqrt(by + dx2[s])
                w = (mb[s, 8 * g : 8 * g + 8, :] * r) * (r * r)
                hx[s] = w if hx[s] is None else hx[s] + w
                gy = w if gy is None else gy + w
            total = gy if total is None else total + gy
            fy = dy * gy if fy is None else fy + dy * gy
        fx = dx[0] * hx[0]
        for s in range(1, NX):
            fx = fx + dx[s] * hx[s]
        weight = far_gain * jnp.sum(blk[3:6] * blk[6:9], axis=0, keepdims=True)
        add = lambda t: jnp.sum(t, axis=0, keepdims=True)
        f = jnp.concatenate([add(fx), add(fy), z * add(total)], axis=0)
        out[:, pl.ds(pl.multiple_of(k * BLOCK, BLOCK), BLOCK)] = own[k] + weight * f
        return 0

    lax.fori_loop(0, OWN, far, 0)
    for cp in copies:
        cp.wait()

    def combine(k, _):
        f = back_in[0, inv[0, k]]
        for q in range(1, 4):
            f = f + back_in[q, inv[q, k]]
        where = pl.ds(pl.multiple_of(k * BLOCK, BLOCK), BLOCK)
        out[:, where] = out[:, where] + f[0:3]
        return 0

    lax.fori_loop(0, OWN, combine, 0, unroll=4)


def index_rows(pair_list, pair_count):
    live = (jnp.arange(PAIRS, dtype=i32) < pair_count[0])[:, None]
    own = jnp.arange(OWN, dtype=i32)
    idle = jnp.array([[0, 0, TRASH, TRASH]], i32)
    pad = lambda n: jnp.broadcast_to(idle, (n, 4))
    self_rows = jnp.stack([own, own, jnp.full((OWN,), TRASH, i32), own], axis=1)
    pair_rows = jnp.where(live, jnp.concatenate([pair_list, pair_list], axis=1), idle)
    return jnp.concatenate([pad(3 * GROUP), self_rows, pair_rows, pad(5 * GROUP)], axis=0).reshape(-1)


VM, SM = pl.BlockSpec(memory_space=pltpu.VMEM), pl.BlockSpec(memory_space=pltpu.SMEM)
SDS = jax.ShapeDtypeStruct
DMA = pltpu.SemaphoreType.DMA


def body(segments, pair_list, pair_count, send_list, cell_ids):
    ghost, mom = pl.pallas_call(
        exchange,
        name="exchange",
        out_shape=(SDS((4, ROWS, BLOCK), f32), SDS((NX, BLOCK), f32)),
        in_specs=[SM, VM, VM],
        out_specs=(VM, VM),
        scratch_shapes=[
            pltpu.VMEM((OWN, 8, BLOCK), f32),
            pltpu.VMEM((OWN, 1, BLOCK), f32),
            pltpu.VMEM((4, ROWS, BLOCK), f32),
            pltpu.VMEM((4, ROWS, BLOCK), f32),
            pltpu.VMEM((1, BLOCK), f32),
            pltpu.VMEM((NY, BLOCK), f32),
            pltpu.VMEM((1, BLOCK), f32),
            pltpu.VMEM((NX, BLOCK), f32),
            DMA((4,)), DMA((4,)), DMA, DMA, DMA, DMA,
        ],
        compiler_params=pltpu.CompilerParams(
            collective_id=0, has_side_effects=True, vmem_limit_bytes=32 * 2**20
        ),
    )(send_list, segments, cell_ids.reshape(1, -1))
    own_force, ghost_force, inv = pl.pallas_call(
        pairs,
        name="pairs",
        out_shape=(SDS((OWN, 3, BLOCK), f32), SDS((4, GHOST, 4, BLOCK), f32), SDS((4, OWN), i32)),
        in_specs=[SM, SM, SM, VM, VM],
        out_specs=(VM, VM, SM),
        scratch_shapes=[
            pltpu.VMEM((OWN, BLOCK, BLOCK), bf16),
            pltpu.VMEM((ALL, KDIM, 2 * BLOCK), bf16),
            pltpu.VMEM((ALL, 16, 2 * BLOCK), bf16),
            pltpu.VMEM((GROUP, BLOCK, 2 * BLOCK), f32),
            pltpu.VMEM((GROUP, 2 * BLOCK, BLOCK), bf16),
            pltpu.VMEM((GROUP, 2, 16, BLOCK), f32),
            pltpu.VMEM((ALL + 1, 16, BLOCK), f32),
            pltpu.VMEM((ALL + 1, 16, BLOCK), f32),
        ],
        compiler_params=pltpu.CompilerParams(vmem_limit_bytes=40 * 2**20),
    )(pair_count, index_rows(pair_list, pair_count), send_list, segments, ghost)
    return pl.pallas_call(
        finale,
        name="finale",
        out_shape=SDS((3, OWN * BLOCK), f32),
        in_specs=[SM, VM, VM, VM, VM],
        out_specs=VM,
        scratch_shapes=[
            pltpu.VMEM((4, GHOST + 1, 4, BLOCK), f32),
            pltpu.VMEM((NX, 2 * NY, BLOCK), f32),
            DMA((4,)), DMA((4,)),
        ],
        compiler_params=pltpu.CompilerParams(
            collective_id=1, has_side_effects=True, vmem_limit_bytes=32 * 2**20
        ),
    )(inv, segments, mom, own_force, ghost_force)


def solution(mesh):
    in_specs = (
        P(None, ("gx", "gy")),
        P(("gx", "gy"), None),
        P(("gx", "gy")),
        P(("gx", "gy"), None),
        P(("gx", "gy")),
    )
    out_specs = P(None, ("gx", "gy"))
    return jax.shard_map(body, mesh=mesh, in_specs=in_specs, out_specs=out_specs, check_vma=False)
```

```python
import functools

import jax
import jax.numpy as jnp
from jax import lax
from jax.experimental import pallas as pl
from jax.experimental.pallas import tpu as pltpu
from jax.sharding import PartitionSpec as P

f32, bf16, i32 = jnp.float32, jnp.bfloat16, jnp.int32
MESH = pl.DeviceIdType.MESH
BLOCK = 128
OWN = 64
GHOST = 16
ALL = OWN + 4 * GHOST
TRASH = ALL
PAIRS = 512
NX, NY = 8, 32
GROUP = 8
KDIM = 96
ROWS = 9 * GHOST

strength = 0.2
core_sq = 0.05
far_gain = 0.5
far_core_sq = 0.1


def mm(a, b, nt=False):
    dims = (((1,), (1 if nt else 0,)), ((), ()))
    return lax.dot_general(a, b, dims, preferred_element_type=f32)


def split3(x):
    h = x.astype(bf16)
    r = x - h.astype(f32)
    m = r.astype(bf16)
    return h, m, (r - m.astype(f32)).astype(bf16)


def rows16(parts):
    missing = 16 - sum(p.shape[0] for p in parts)
    if missing:
        parts = parts + [jnp.zeros((missing, BLOCK), f32)]
    return jnp.concatenate(parts, axis=0)


def eye128():
    shape = (BLOCK, BLOCK)
    return (lax.broadcasted_iota(i32, shape, 0) == lax.broadcasted_iota(i32, shape, 1)).astype(bf16)


def neighbours(ix, iy):
    return (
        (lax.rem(ix + NX - 1, NX), iy),
        (lax.rem(ix + 1, NX), iy),
        (ix, lax.rem(iy + NY - 1, NY)),
        (ix, lax.rem(iy + 1, NY)),
    )


def features(raw, cx, cy, eye, a_ref, b_ref, p_ref, k, with_a):
    x, y, z = raw[0:1] - cx, raw[1:2] - cy, raw[2:3] - 0.5
    l, b = raw[3:6], raw[6:9]
    u = [b[0:1] * l, b[1:2] * l, b[2:3] * l]
    norm = x * x + y * y + z * z
    one = jnp.ones((1, BLOCK), f32)
    bq = split3(rows16(u))
    bd = split3(rows16([jnp.zeros((9, BLOCK), f32), x, y, z, norm, one]))
    b_ref[k, :, 0:BLOCK] = jnp.concatenate(bq, axis=0)
    b_ref[k, :, BLOCK:] = jnp.concatenate(bd, axis=0)
    pos = [t.astype(f32) for t in split3(x) + split3(y) + split3(z)]
    p_ref[k] = rows16(pos + [one]).astype(bf16)
    if with_a:
        fa = split3(
            rows16([strength * t for t in u] + [-2.0 * x, -2.0 * y, -2.0 * z, one, norm + core_sq])
        )
        at = jnp.concatenate([fa[o] for o in (0, 0, 1, 1, 0, 2)], axis=0)
        at = jnp.concatenate([at, jnp.zeros((BLOCK - KDIM, BLOCK), bf16)], axis=0)
        a_ref[k] = mm(eye, at, nt=True).astype(bf16)


def twice(p):
    return jnp.concatenate([p, p], axis=1)


def spread(b):
    h, m, l = b[0:16], b[16:32], b[32:48]
    return jnp.concatenate([h, m, h, m, l, h], axis=0)


def twice_w(ww, s):
    return jnp.concatenate([ww[s, 0:BLOCK], ww[s, BLOCK:]], axis=1)


def weigh(qd, ww, s):
    r = lax.rsqrt(qd[s, :, BLOCK:])
    w = (qd[s, :, 0:BLOCK] * r) * (r * r)
    wh = w.astype(bf16)
    ww[s, 0:BLOCK] = wh
    ww[s, BLOCK:] = (w - wh.astype(f32)).astype(bf16)


def exchange(send_list, seg, cells, a_ref, b_ref, p_ref, self_ref, mom_out, main, last, out_buf, in_buf,
             row, part, row2, table, qd, ww, s_sem, r_sem, s1, r1, s2, r2):
    ix, iy = lax.axis_index("gx"), lax.axis_index("gy")
    barrier = pltpu.get_barrier_semaphore()

    def greet_y(o, _):
        pl.semaphore_signal(barrier, inc=1, device_id=(ix, lax.rem(iy + o, NY)), device_id_type=MESH)
        return 0

    def greet_x(o, _):
        pl.semaphore_signal(barrier, inc=1, device_id=(lax.rem(ix + o, NX), iy), device_id_type=MESH)
        return 0

    lax.fori_loop(1, NY, greet_y, 0)
    lax.fori_loop(1, NX, greet_x, 0)
    for k in range(OWN):
        main[k] = seg[0:8, k * BLOCK : (k + 1) * BLOCK]
        last[k] = seg[8:9, k * BLOCK : (k + 1) * BLOCK]
    for q in range(4):
        for j in range(GHOST):
            k = send_list[q, j]
            out_buf[q, 8 * j : 8 * j + 8, :] = main[k]
            out_buf[q, 8 * GHOST + j : 8 * GHOST + j + 1, :] = last[k]
    c = jnp.sum(seg[3:6, :] * seg[6:9, :], axis=0, keepdims=True)
    first = 2 * (ix * NY + iy)
    ids = cells[...]
    m0 = jnp.sum(jnp.where(ids == first, c, 0.0))
    m1 = jnp.sum(jnp.where(ids == first + 1, c, 0.0))
    lane = lax.broadcasted_iota(i32, (1, BLOCK), 1)
    mine = jnp.where(lane == 2 * iy, m0, jnp.where(lane == 2 * iy + 1, m1, 0.0))
    row[...] = mine
    part[NY - 1 : NY, :] = mine
    pl.semaphore_wait(barrier, NY - 1 + NX - 1)
    copies = []
    for q, dev in enumerate(neighbours(ix, iy)):
        copies.append(
            pltpu.make_async_remote_copy(
                src_ref=out_buf.at[q], dst_ref=in_buf.at[q ^ 1], send_sem=s_sem.at[q],
                recv_sem=r_sem.at[q ^ 1], device_id=dev, device_id_type=MESH,
            )
        )
        copies[-1].start()

    def send_y(o, _):
        pltpu.make_async_remote_copy(
            src_ref=row, dst_ref=part.at[pl.ds(o - 1, 1)], send_sem=s1, recv_sem=r1,
            device_id=(ix, lax.rem(iy + o, NY)), device_id_type=MESH,
        ).start()
        return 0

    lax.fori_loop(1, NY, send_y, 0)
    cx, cy = ix.astype(f32) + 0.5, iy.astype(f32) + 0.5
    eye = eye128()

    def build_own(k, _):
        raw = jnp.concatenate([main[k], last[k]], axis=0)
        features(raw, cx, cy, eye, a_ref, b_ref, p_ref, k, True)
        return 0

    lax.fori_loop(0, OWN, build_own, 0, unroll=4)
    pltpu.make_async_copy(part.at[0 : NY - 1], part.at[0 : NY - 1], r1).wait()
    slab = jnp.sum(part[...], axis=0, keepdims=True)
    row2[...] = slab
    table[pl.ds(NX - 1, 1), :] = slab

    def send_x(o, _):
        pltpu.make_async_remote_copy(
            src_ref=row2, dst_ref=table.at[pl.ds(o - 1, 1)], send_sem=s2, recv_sem=r2,
            device_id=(lax.rem(ix + o, NX), iy), device_id_type=MESH,
        ).start()
        return 0

    lax.fori_loop(1, NX, send_x, 0)

    def step(t, _):
        for s in range(GROUP):
            k = (t - 2) * GROUP + s
            k = jnp.minimum(jnp.maximum(k, 0), OWN - 1)
            self_ref[k] = mm(twice(p_ref[k]), ww[s])
            weigh(qd, ww, s)
            k = jnp.minimum(t * GROUP + s, OWN - 1)
            qd[s] = mm(a_ref[k, :, 0:KDIM], spread(b_ref[k]))
        return 0

    lax.fori_loop(0, OWN // GROUP + 2, step, 0)
    for cp in copies:
        cp.wait()

    def build_ghost(j, _):
        for q in range(4):
            raw = jnp.concatenate(
                [in_buf[q, pl.ds(pl.multiple_of(8 * j, 8), 8), :], in_buf[q, pl.ds(8 * GHOST + j, 1), :]], axis=0
            )
            features(raw, cx, cy, eye, a_ref, b_ref, p_ref, OWN + GHOST * q + j, False)
        return 0

    lax.fori_loop(0, GHOST, build_ghost, 0)
    pltpu.make_async_copy(table.at[0 : NX - 1], table.at[0 : NX - 1], r2).wait()
    mom_out[...] = table[...]
    pltpu.make_async_copy(part.at[0 : NY - 1], part.at[0 : NY - 1], s1).wait()
    pltpu.make_async_copy(table.at[0 : NX - 1], table.at[0 : NX - 1], s2).wait()


def finish(acc, p):
    p = p.astype(f32)
    f = []
    for c in range(3):
        x = p[3 * c : 3 * c + 1] + p[3 * c + 1 : 3 * c + 2] + p[3 * c + 2 : 3 * c + 3]
        f.append(x * acc[9:10] - (acc[3 * c : 3 * c + 1] + acc[3 * c + 1 : 3 * c + 2] + acc[3 * c + 2 : 3 * c + 3]))
    return f


def pairs(count, rows, send_list, seg, mom, a_ref, b_ref, p_ref, self_ref, own_out, ghost_out, inv_out,
          qd, ww, rr, acc_a, acc_b, mb, far_out):
    ix = lax.axis_index("gx")
    acc_a[...] = jnp.zeros_like(acc_a)
    acc_b[0:OWN] = self_ref[...]
    acc_b[OWN:] = jnp.zeros((ALL + 1 - OWN, 16, BLOCK), f32)
    wide = jnp.concatenate([mom[...], jnp.zeros((BLOCK - NX, BLOCK), f32)], axis=0).T
    for s in range(NX):
        mb[s] = jnp.broadcast_to(wide[0 : 2 * NY, s : s + 1], (2 * NY, BLOCK))
    centre_x = [lax.rem(ix + (2 * NX - 1 - s), NX).astype(f32) + 0.5 for s in range(NX)]
    sub = lax.broadcasted_iota(i32, (8, BLOCK), 0).astype(f32)

    class Far:
        def __init__(self, k):
            self.k = k
            blk = seg[:, pl.ds(pl.multiple_of(jnp.minimum(k, OWN - 1) * BLOCK, BLOCK), BLOCK)]
            self.blk = blk
            self.y = jnp.broadcast_to(blk[1:2], (8, BLOCK))
            z = blk[2:3] - 0.5
            self.base = z * z + far_core_sq
            x = jnp.broadcast_to(blk[0:1], (8, BLOCK))
            self.dx2 = [(x - cx) * (x - cx) for cx in centre_x]
            self.hx, self.fy, self.total = [None] * NX, None, None

        def group(self, g):
            dy = self.y - (0.5 * sub + (4.0 * g + 0.25))
            by = dy * dy + self.base
            gy = None
            for s in range(NX):
                r = lax.rsqrt(by + self.dx2[s])
                w = (mb[s, 8 * g : 8 * g + 8, :] * r) * (r * r)
                self.hx[s] = w if g == 0 else self.hx[s] + w
                gy = w if gy is None else gy + w
            self.total = gy if g == 0 else self.total + gy
            self.fy = dy * gy if g == 0 else self.fy + dy * gy

        def store(self):
            blk = self.blk
            x = jnp.broadcast_to(blk[0:1], (8, BLOCK))
            fx = (x - centre_x[0]) * self.hx[0]
            for s in range(1, NX):
                fx = fx + (x - centre_x[s]) * self.hx[s]
            weight = far_gain * jnp.sum(blk[3:6] * blk[6:9], axis=0, keepdims=True)
            add = lambda t: jnp.sum(t, axis=0, keepdims=True)
            f = jnp.concatenate([add(fx), add(self.fy), (blk[2:3] - 0.5) * add(self.total)], axis=0)
            far_out[self.k] = weight * f

    def step(t, _):
        far = Far(jnp.minimum(t, OWN))
        for s in range(GROUP):
            o = t * (4 * GROUP) + 4 * s
            acc_a[rows[o + 2]] += rr[s, 0]
            acc_b[rows[o + 3]] += rr[s, 1]
            o = o + 4 * GROUP
            rr[s, 0] = mm(twice(p_ref[rows[o + 1]]), twice_w(ww, s), nt=True)
            rr[s, 1] = mm(twice(p_ref[rows[o]]), ww[s])
            weigh(qd, ww, s)
            far.group(s)
            o = o + 8 * GROUP
            qd[s] = mm(a_ref[rows[o], :, 0:KDIM], spread(b_ref[rows[o + 1]]))
        far.store()
        return 0

    steps = (count[0] + GROUP - 1) // GROUP + 3
    lax.fori_loop(0, steps, step, 0)

    def rest(k, _):
        far = Far(k)
        for g in range(GROUP):
            far.group(g)
        far.store()
        return 0

    lax.fori_loop(jnp.minimum(steps, OWN), OWN, rest, 0)

    def finish_own(k, _):
        own_out[k] = jnp.concatenate(finish(acc_a[k] + acc_b[k], p_ref[k]), axis=0) + far_out[k]
        return 0

    def finish_ghost(k, _):
        f = finish(acc_b[OWN + k], p_ref[OWN + k])
        ghost_out[k] = jnp.concatenate(f + [jnp.zeros((1, BLOCK), f32)], axis=0)
        return 0

    lax.fori_loop(0, OWN, finish_own, 0, unroll=4)
    lax.fori_loop(0, 4 * GHOST, finish_ghost, 0, unroll=4)

    def clear(k, _):
        for q in range(4):
            inv_out[q, k] = GHOST
        return 0

    lax.fori_loop(0, OWN, clear, 0, unroll=8)
    for q in range(4):
        for j in range(GHOST):
            inv_out[q, send_list[q, j]] = j


def finale(inv, own, ghost, out, back_in, s_sem, r_sem):
    ix, iy = lax.axis_index("gx"), lax.axis_index("gy")
    barrier = pltpu.get_barrier_semaphore()
    near = neighbours(ix, iy)
    for dev in near:
        pl.semaphore_signal(barrier, inc=1, device_id=dev, device_id_type=MESH)
    pl.semaphore_wait(barrier, 4)
    copies = []
    for q, dev in enumerate(near):
        copies.append(
            pltpu.make_async_remote_copy(
                src_ref=ghost.at[GHOST * q : GHOST * q + GHOST], dst_ref=back_in.at[q ^ 1, 0:GHOST], send_sem=s_sem.at[q],
                recv_sem=r_sem.at[q ^ 1], device_id=dev, device_id_type=MESH,
            )
        )
        copies[-1].start()
    for q in range(4):
        back_in[q, GHOST] = jnp.zeros((4, BLOCK), f32)
    for cp in copies:
        cp.wait()

    def combine(k, _):
        f = back_in[0, inv[0, k]]
        for q in range(1, 4):
            f = f + back_in[q, inv[q, k]]
        where = pl.ds(pl.multiple_of(k * BLOCK, BLOCK), BLOCK)
        out[:, where] = own[k] + f[0:3]
        return 0

    lax.fori_loop(0, OWN, combine, 0, unroll=4)


def index_rows(pair_list, pair_count):
    live = (jnp.arange(PAIRS, dtype=i32) < pair_count[0])[:, None]
    idle = jnp.array([[0, 0, TRASH, TRASH]], i32)
    pad = lambda n: jnp.broadcast_to(idle, (n, 4))
    pair_rows = jnp.where(live, jnp.concatenate([pair_list, pair_list], axis=1), idle)
    return jnp.concatenate([pad(3 * GROUP), pair_rows, pad(5 * GROUP)], axis=0).reshape(-1)


VM, SM = pl.BlockSpec(memory_space=pltpu.VMEM), pl.BlockSpec(memory_space=pltpu.SMEM)
SDS = jax.ShapeDtypeStruct
DMA = pltpu.SemaphoreType.DMA


def body(segments, pair_list, pair_count, send_list, cell_ids):
    a, b, p, own_sums, mom = pl.pallas_call(
        exchange,
        name="exchange",
        out_shape=(
            SDS((OWN, BLOCK, BLOCK), bf16),
            SDS((ALL, 48, 2 * BLOCK), bf16),
            SDS((ALL, 16, BLOCK), bf16),
            SDS((OWN, 16, BLOCK), f32),
            SDS((NX, BLOCK), f32),
        ),
        in_specs=[SM, VM, VM],
        out_specs=(VM,) * 5,
        scratch_shapes=[
            pltpu.VMEM((OWN, 8, BLOCK), f32),
            pltpu.VMEM((OWN, 1, BLOCK), f32),
            pltpu.VMEM((4, ROWS, BLOCK), f32),
            pltpu.VMEM((4, ROWS, BLOCK), f32),
            pltpu.VMEM((1, BLOCK), f32),
            pltpu.VMEM((NY, BLOCK), f32),
            pltpu.VMEM((1, BLOCK), f32),
            pltpu.VMEM((NX, BLOCK), f32),
            pltpu.VMEM((GROUP, BLOCK, 2 * BLOCK), f32),
            pltpu.VMEM((GROUP, 2 * BLOCK, BLOCK), bf16),
            DMA((4,)), DMA((4,)), DMA, DMA, DMA, DMA,
        ],
        compiler_params=pltpu.CompilerParams(
            collective_id=0, has_side_effects=True, vmem_limit_bytes=20 * 2**20
        ),
    )(send_list, segments, cell_ids.reshape(1, -1))
    own_force, ghost_force, inv = pl.pallas_call(
        pairs,
        name="pairs",
        out_shape=(SDS((OWN, 3, BLOCK), f32), SDS((4 * GHOST, 4, BLOCK), f32), SDS((4, OWN), i32)),
        in_specs=[SM, SM, SM] + [VM] * 6,
        out_specs=(VM, VM, SM),
        scratch_shapes=[
            pltpu.VMEM((GROUP, BLOCK, 2 * BLOCK), f32),
            pltpu.VMEM((GROUP, 2 * BLOCK, BLOCK), bf16),
            pltpu.VMEM((GROUP, 2, 16, BLOCK), f32),
            pltpu.VMEM((ALL + 1, 16, BLOCK), f32),
            pltpu.VMEM((ALL + 1, 16, BLOCK), f32),
            pltpu.VMEM((NX, 2 * NY, BLOCK), f32),
            pltpu.VMEM((OWN + 1, 3, BLOCK), f32),
        ],
        compiler_params=pltpu.CompilerParams(vmem_limit_bytes=24 * 2**20),
    )(pair_count, index_rows(pair_list, pair_count), send_list, segments, mom, a, b, p, own_sums)
    return pl.pallas_call(
        finale,
        name="finale",
        out_shape=SDS((3, OWN * BLOCK), f32),
        in_specs=[SM, VM, VM],
        out_specs=VM,
        scratch_shapes=[pltpu.VMEM((4, GHOST + 1, 4, BLOCK), f32), DMA((4,)), DMA((4,))],
        compiler_params=pltpu.CompilerParams(
            collective_id=1, has_side_effects=True, vmem_limit_bytes=16 * 2**20
        ),
    )(inv, own_force, ghost_force)


def solution(mesh):
    in_specs = (
        P(None, ("gx", "gy")),
        P(("gx", "gy"), None),
        P(("gx", "gy")),
        P(("gx", "gy"), None),
        P(("gx", "gy")),
    )
    out_specs = P(None, ("gx", "gy"))
    return jax.shard_map(body, mesh=mesh, in_specs=in_specs, out_specs=out_specs, check_vma=False)
```

```python
import functools

import jax
import jax.numpy as jnp
from jax import lax
from jax.experimental import pallas as pl
from jax.experimental.pallas import tpu as pltpu
from jax.sharding import PartitionSpec as P

f32, bf16, i32 = jnp.float32, jnp.bfloat16, jnp.int32
MESH = pl.DeviceIdType.MESH
BLOCK = 128
OWN = 64
GHOST = 16
ALL = OWN + 4 * GHOST
SIB = ALL
TRASH = 2 * ALL
SURE = 64
PAIRS = 512
NX, NY = 8, 32
GROUP = 8
KDIM = 96
ROWS = 9 * GHOST

strength = 0.2
core_sq = 0.05
far_gain = 0.5
far_core_sq = 0.1


def mm(a, b, nt=False):
    dims = (((1,), (1 if nt else 0,)), ((), ()))
    return lax.dot_general(a, b, dims, preferred_element_type=f32)


def split3(x):
    h = x.astype(bf16)
    r = x - h.astype(f32)
    m = r.astype(bf16)
    return h, m, (r - m.astype(f32)).astype(bf16)


def rows16(parts):
    missing = 16 - sum(p.shape[0] for p in parts)
    if missing:
        parts = parts + [jnp.zeros((missing, BLOCK), f32)]
    return jnp.concatenate(parts, axis=0)


def eye128():
    shape = (BLOCK, BLOCK)
    return (lax.broadcasted_iota(i32, shape, 0) == lax.broadcasted_iota(i32, shape, 1)).astype(bf16)


def neighbours(ix, iy):
    return (
        (lax.rem(ix + NX - 1, NX), iy),
        (lax.rem(ix + 1, NX), iy),
        (ix, lax.rem(iy + NY - 1, NY)),
        (ix, lax.rem(iy + 1, NY)),
    )


def features(raw, cx, cy, eye, a_ref, b_ref, p_ref, k, with_a):
    k = jnp.int32(k) if isinstance(k, int) else k
    x, y, z = raw[0:1] - cx, raw[1:2] - cy, raw[2:3] - 0.5
    l, b = raw[3:6], raw[6:9]
    u = [b[0:1] * l, b[1:2] * l, b[2:3] * l]
    norm = x * x + y * y + z * z
    one = jnp.ones((1, BLOCK), f32)
    bq = split3(rows16(u))
    bd = split3(rows16([jnp.zeros((9, BLOCK), f32), x, y, z, norm, one]))
    b_ref[k, :, 0:BLOCK] = jnp.concatenate(bq, axis=0)
    b_ref[k, :, BLOCK:] = jnp.concatenate(bd, axis=0)
    pos = [t.astype(f32) for t in split3(x) + split3(y) + split3(z)]
    p_ref[k] = rows16(pos + [one]).astype(bf16)
    if with_a:
        fa = split3(
            rows16([strength * t for t in u] + [-2.0 * x, -2.0 * y, -2.0 * z, one, norm + core_sq])
        )
        at = jnp.concatenate([fa[o] for o in (0, 0, 1, 1, 0, 2)], axis=0)
        at = jnp.concatenate([at, jnp.zeros((BLOCK - KDIM, BLOCK), bf16)], axis=0)
        a_ref[k] = mm(eye, at, nt=True).astype(bf16)


def twice(p):
    return jnp.concatenate([p, p], axis=1)


def spread(b):
    h, m, l = b[0:16], b[16:32], b[32:48]
    return jnp.concatenate([h, m, h, m, l, h], axis=0)


def twice_w(ww, s):
    return jnp.concatenate([ww[s, 0:BLOCK], ww[s, BLOCK:]], axis=1)


def weigh(qd, ww, s):
    r = lax.rsqrt(qd[s, :, BLOCK:])
    w = (qd[s, :, 0:BLOCK] * r) * (r * r)
    wh = w.astype(bf16)
    ww[s, 0:BLOCK] = wh
    ww[s, BLOCK:] = (w - wh.astype(f32)).astype(bf16)


def exchange(seg_in, cells_in, send_in, list_in, count, a_ref, b_ref, p_ref, self_ref, sure_ref, far_ref, mom_out,
             idx_out, inv_out, seg, cells, send_list, plist, ids, cnt, sib_seg, sib_ids, sib_cnt, sib_ghost,
             main, last, out_buf, in_buf, row, part, row2, table, qd, ww, l_sem, s_sem, r_sem, ss, sr,
             s1, r1, s2, r2):
    ix, iy = lax.axis_index("gx"), lax.axis_index("gy")
    sib = (ix, iy + 1 - 2 * lax.rem(iy, 2))
    loads = [
        pltpu.make_async_copy(src, dst, l_sem.at[n])
        for n, (src, dst) in enumerate(
            ((seg_in, seg), (send_in, send_list), (cells_in, cells), (list_in, plist), (list_in, ids))
        )
    ]
    for cp in loads:
        cp.start()
    barrier = pltpu.get_barrier_semaphore()

    def greet_y(o, _):
        pl.semaphore_signal(barrier, inc=1, device_id=(ix, lax.rem(iy + o, NY)), device_id_type=MESH)
        return 0

    def greet_x(o, _):
        pl.semaphore_signal(barrier, inc=1, device_id=(lax.rem(ix + o, NX), iy), device_id_type=MESH)
        return 0

    lax.fori_loop(1, NY, greet_y, 0)
    lax.fori_loop(1, NX, greet_x, 0)
    cnt[...] = jnp.full((1, BLOCK), count[0], i32)
    for cp in loads:
        cp.wait()
    for k in range(OWN):
        main[k] = seg[0:8, k * BLOCK : (k + 1) * BLOCK]
        last[k] = seg[8:9, k * BLOCK : (k + 1) * BLOCK]
    lanes = lax.broadcasted_iota(i32, (1, BLOCK), 1)
    for q in range(4):
        where = jnp.full((1, BLOCK), GHOST, i32)
        for j in range(GHOST):
            k = send_list[q, j]
            out_buf[q, 8 * j : 8 * j + 8, :] = main[k]
            out_buf[q, 8 * GHOST + j : 8 * GHOST + j + 1, :] = last[k]
            where = jnp.where(lanes == k, j, where)
        inv_out[q : q + 1, :] = where
    c = jnp.sum(seg[3:6, :] * seg[6:9, :], axis=0, keepdims=True)
    first = 2 * (ix * NY + iy)
    m0 = jnp.sum(jnp.where(cells[...] == first, c, 0.0))
    m1 = jnp.sum(jnp.where(cells[...] == first + 1, c, 0.0))
    mine = jnp.where(lanes == 2 * iy, m0, jnp.where(lanes == 2 * iy + 1, m1, 0.0))
    row[...] = mine
    part[NY - 1 : NY, :] = mine
    cx, cy = ix.astype(f32) + 0.5, iy.astype(f32) + 0.5
    sy = sib[1].astype(f32) + 0.5
    eye = eye128()

    def build_own(k, _):
        raw = jnp.concatenate([main[k], last[k]], axis=0)
        features(raw, cx, cy, eye, a_ref, b_ref, p_ref, k, True)
        weight = far_gain * jnp.sum(raw[3:6] * raw[6:9], axis=0, keepdims=True)
        far_ref[k] = jnp.concatenate([raw[0:2], raw[2:3] - 0.5, weight], axis=0)
        return 0

    lax.fori_loop(0, OWN, build_own, 0, unroll=4)
    pl.semaphore_wait(barrier, NY - 1 + NX - 1)
    copies = []
    for q, dev in enumerate(neighbours(ix, iy)):
        copies.append(
            pltpu.make_async_remote_copy(
                src_ref=out_buf.at[q], dst_ref=in_buf.at[q ^ 1], send_sem=s_sem.at[q],
                recv_sem=r_sem.at[q ^ 1], device_id=dev, device_id_type=MESH,
            )
        )
        copies[-1].start()

    def send_y(o, _):
        pltpu.make_async_remote_copy(
            src_ref=row, dst_ref=part.at[pl.ds(o - 1, 1)], send_sem=s1, recv_sem=r1,
            device_id=(ix, lax.rem(iy + o, NY)), device_id_type=MESH,
        ).start()
        return 0

    lax.fori_loop(1, NY, send_y, 0)
    shares = [
        pltpu.make_async_remote_copy(
            src_ref=src, dst_ref=dst, send_sem=ss.at[n], recv_sem=sr.at[n], device_id=sib, device_id_type=MESH
        )
        for n, (src, dst) in enumerate(((seg, sib_seg), (ids, sib_ids), (cnt, sib_cnt), (in_buf, sib_ghost)))
    ]
    for cp in shares[:3]:
        cp.start()

    def step(t, _):
        for s in range(GROUP):
            k = jnp.minimum(jnp.maximum((t - 2) * GROUP + s, 0), OWN - 1)
            self_ref[k] = mm(twice(p_ref[k]), ww[s])
            weigh(qd, ww, s)
            k = jnp.minimum(t * GROUP + s, OWN - 1)
            qd[s] = mm(a_ref[k][:, 0:KDIM], spread(b_ref[k]))
        return 0

    lax.fori_loop(0, OWN // GROUP + 2, step, 0)
    for cp in copies:
        cp.wait()
    shares[3].start()
    pltpu.make_async_copy(part.at[0 : NY - 1], part.at[0 : NY - 1], r1).wait()
    slab = jnp.sum(part[...], axis=0, keepdims=True)
    row2[...] = slab
    table[pl.ds(NX - 1, 1), :] = slab

    def send_x(o, _):
        pltpu.make_async_remote_copy(
            src_ref=row2, dst_ref=table.at[pl.ds(o - 1, 1)], send_sem=s2, recv_sem=r2,
            device_id=(lax.rem(ix + o, NX), iy), device_id_type=MESH,
        ).start()
        return 0

    lax.fori_loop(1, NX, send_x, 0)

    def ghosts_of(buf, cy, base):
        def build(j, _):
            for q in range(4):
                raw = jnp.concatenate(
                    [buf[q, pl.ds(pl.multiple_of(8 * j, 8), 8), :], buf[q, pl.ds(8 * GHOST + j, 1), :]], axis=0
                )
                features(raw, cx, cy, eye, a_ref, b_ref, p_ref, base + GHOST * q + j, False)
            return 0

        lax.fori_loop(0, GHOST, build, 0)

    ghosts_of(in_buf, cy, OWN)

    def sure_step(t, _):
        for s in range(GROUP):
            k = jnp.minimum(jnp.maximum((t - 2) * GROUP + s, 0), SURE - 1)
            i, j = plist[0, k], plist[1, k]
            sure_ref[k, 0] = mm(twice(p_ref[j]), twice_w(ww, s), nt=True)
            sure_ref[k, 1] = mm(twice(p_ref[i]), ww[s])
            weigh(qd, ww, s)
            k = jnp.minimum(t * GROUP + s, SURE - 1)
            i, j = plist[0, k], plist[1, k]
            qd[s] = mm(a_ref[i][:, 0:KDIM], spread(b_ref[j]))
        return 0

    lax.fori_loop(0, SURE // GROUP + 2, sure_step, 0)
    for cp in shares[:3]:
        cp.wait()

    def build_sib(k, _):
        raw = sib_seg[:, pl.ds(pl.multiple_of(k * BLOCK, BLOCK), BLOCK)]
        features(raw, cx, sy, eye, a_ref, b_ref, p_ref, SIB + k, True)
        return 0

    lax.fori_loop(0, OWN, build_sib, 0, unroll=4)
    idx_out[0:2, :] = ids[...]
    idx_out[2:4, :] = sib_ids[...] + SIB
    idx_out[4:5, :] = jnp.concatenate([cnt[...]] * (PAIRS // BLOCK), axis=1)
    idx_out[5:6, :] = jnp.concatenate([sib_cnt[...]] * (PAIRS // BLOCK), axis=1)
    shares[3].wait()
    ghosts_of(sib_ghost, sy, SIB + OWN)
    pltpu.make_async_copy(table.at[0 : NX - 1], table.at[0 : NX - 1], r2).wait()
    mom_out[...] = table[...]
    pltpu.make_async_copy(part.at[0 : NY - 1], part.at[0 : NY - 1], s1).wait()
    pltpu.make_async_copy(table.at[0 : NX - 1], table.at[0 : NX - 1], s2).wait()


def finish(acc, p):
    p = p.astype(f32)
    f = []
    for c in range(3):
        x = p[3 * c : 3 * c + 1] + p[3 * c + 1 : 3 * c + 2] + p[3 * c + 2 : 3 * c + 3]
        f.append(x * acc[9:10] - (acc[3 * c : 3 * c + 1] + acc[3 * c + 1 : 3 * c + 2] + acc[3 * c + 2 : 3 * c + 3]))
    return f


def pairs(idx, a_ref, b_ref, p_ref, self_ref, sure_ref, out, qd, ww, rr, acc_a, acc_b):
    own_rows, sib_rows = idx[4, 0] - SURE, idx[5, 0] - SURE
    half = (own_rows + sib_rows + 1) // 2
    n_own = jnp.minimum(own_rows, half)
    n_help = jnp.maximum(sib_rows - half, 0)
    total = n_own + n_help
    acc_a[0:OWN] = jnp.zeros((OWN, 16, BLOCK), f32)
    acc_b[0:OWN] = self_ref[...]
    acc_b[OWN:ALL] = jnp.zeros((ALL - OWN, 16, BLOCK), f32)

    @pl.when(n_help > 0)
    def _():
        acc_a[SIB : SIB + OWN] = jnp.zeros((OWN, 16, BLOCK), f32)
        acc_b[SIB : SIB + ALL] = jnp.zeros((ALL, 16, BLOCK), f32)

    def add_sure(k, _):
        acc_a[idx[0, k]] += sure_ref[k, 0]
        acc_b[idx[1, k]] += sure_ref[k, 1]
        return 0

    lax.fori_loop(0, SURE, add_sure, 0, unroll=8)

    def pick(r):
        r = jnp.maximum(jnp.minimum(r, total - 1), 0)
        own = r < n_own
        at = r + jnp.where(own, SURE, SURE + half - n_own)
        which = jnp.where(own, 0, 2)
        return idx[which, at], idx[which + 1, at]

    def step(t, _):
        for s in range(GROUP):
            r = (t - 3) * GROUP + s
            i, j = pick(r)
            live = jnp.logical_and(r >= 0, r < total)
            acc_a[jnp.where(live, i, TRASH)] += rr[s, 0]
            acc_b[jnp.where(live, j, TRASH)] += rr[s, 1]
            i, j = pick((t - 2) * GROUP + s)
            rr[s, 0] = mm(twice(p_ref[j]), twice_w(ww, s), nt=True)
            rr[s, 1] = mm(twice(p_ref[i]), ww[s])
            weigh(qd, ww, s)
            i, j = pick(t * GROUP + s)
            qd[s] = mm(a_ref[i][:, 0:KDIM], spread(b_ref[j]))
        return 0

    @pl.when(total > 0)
    def _():
        lax.fori_loop(0, (total + GROUP - 1) // GROUP + 3, step, 0)

    zero = jnp.zeros((1, BLOCK), f32)

    def finish_own(k, _):
        out[k] = jnp.concatenate(finish(acc_a[k] + acc_b[k], p_ref[k]) + [zero], axis=0)
        return 0

    def finish_other(k, _):
        out[k] = jnp.concatenate(finish(acc_b[k], p_ref[k]) + [zero], axis=0)
        return 0

    lax.fori_loop(0, OWN, finish_own, 0, unroll=4)
    lax.fori_loop(OWN, ALL, finish_other, 0, unroll=4)

    @pl.when(n_help > 0)
    def _():
        lax.fori_loop(SIB, SIB + OWN, finish_own, 0, unroll=4)
        lax.fori_loop(SIB + OWN, SIB + ALL, finish_other, 0, unroll=4)

    @pl.when(n_help == 0)
    def _():
        out[SIB:] = jnp.zeros((ALL, 4, BLOCK), f32)


def finale(inv, far_ref, mom, force, out, sib_in, gsum, back_in, mb, ss, sr, s_sem, r_sem):
    ix, iy = lax.axis_index("gx"), lax.axis_index("gy")
    sib = (ix, iy + 1 - 2 * lax.rem(iy, 2))
    barrier = pltpu.get_barrier_semaphore()
    near = neighbours(ix, iy)
    for dev in near:
        pl.semaphore_signal(barrier, inc=1, device_id=dev, device_id_type=MESH)
    for q in range(4):
        back_in[q, GHOST] = jnp.zeros((4, BLOCK), f32)
    pl.semaphore_wait(barrier, 4)
    share = pltpu.make_async_remote_copy(
        src_ref=force.at[SIB : SIB + ALL], dst_ref=sib_in, send_sem=ss, recv_sem=sr, device_id=sib,
        device_id_type=MESH,
    )
    share.start()
    wide = jnp.concatenate([mom[...], jnp.zeros((BLOCK - NX, BLOCK), f32)], axis=0).T
    for s in range(NX):
        mb[s] = jnp.broadcast_to(wide[0 : 2 * NY, s : s + 1], (2 * NY, BLOCK))
    centre_x = [lax.rem(ix + (2 * NX - 1 - s), NX).astype(f32) + 0.5 for s in range(NX)]
    sub = lax.broadcasted_iota(i32, (8, BLOCK), 0).astype(f32)
    share.wait()
    gsum[...] = force[OWN:ALL] + sib_in[OWN:ALL]
    copies = []
    for q, dev in enumerate(near):
        copies.append(
            pltpu.make_async_remote_copy(
                src_ref=gsum.at[GHOST * q : GHOST * q + GHOST], dst_ref=back_in.at[q ^ 1, 0:GHOST],
                send_sem=s_sem.at[q], recv_sem=r_sem.at[q ^ 1], device_id=dev, device_id_type=MESH,
            )
        )
        copies[-1].start()

    def far(k, _):
        blk = far_ref[k]
        x, y, z = jnp.broadcast_to(blk[0:1], (8, BLOCK)), jnp.broadcast_to(blk[1:2], (8, BLOCK)), blk[2:3]
        base = z * z + far_core_sq
        dx = [x - cx for cx in centre_x]
        dx2 = [d * d for d in dx]
        hx = [None] * NX
        fy = total = None
        for g in range(2 * NY // 8):
            dy = y - (0.5 * sub + (4.0 * g + 0.25))
            by = dy * dy + base
            gy = None
            for s in range(NX):
                r = lax.rsqrt(by + dx2[s])
                w = (mb[s, 8 * g : 8 * g + 8, :] * r) * (r * r)
                hx[s] = w if g == 0 else hx[s] + w
                gy = w if s == 0 else gy + w
            total = gy if g == 0 else total + gy
            fy = dy * gy if g == 0 else fy + dy * gy
        fx = dx[0] * hx[0]
        for s in range(1, NX):
            fx = fx + dx[s] * hx[s]
        add = lambda t: jnp.sum(t, axis=0, keepdims=True)
        f = jnp.concatenate([add(fx), add(fy), z * add(total)], axis=0)
        where = pl.ds(pl.multiple_of(k * BLOCK, BLOCK), BLOCK)
        out[:, where] = blk[3:4] * f + (force[k] + sib_in[k])[0:3]
        return 0

    lax.fori_loop(0, OWN, far, 0)
    for cp in copies:
        cp.wait()

    def combine(k, _):
        f = back_in[0, inv[0, k]]
        for q in range(1, 4):
            f = f + back_in[q, inv[q, k]]
        where = pl.ds(pl.multiple_of(k * BLOCK, BLOCK), BLOCK)
        out[:, where] = out[:, where] + f[0:3]
        return 0

    lax.fori_loop(0, OWN, combine, 0, unroll=4)


VM, SM = pl.BlockSpec(memory_space=pltpu.VMEM), pl.BlockSpec(memory_space=pltpu.SMEM)
HB = pl.BlockSpec(memory_space=pltpu.HBM)
SDS = jax.ShapeDtypeStruct
DMA = pltpu.SemaphoreType.DMA


def body(segments, pair_list, pair_count, send_list, cell_ids):
    segs = segments.shape[1]
    a, b, p, own_sums, sure, far, mom, idx, inv = pl.pallas_call(
        exchange,
        name="exchange",
        out_shape=(
            SDS((SIB + OWN, BLOCK, BLOCK), bf16),
            SDS((2 * ALL, 48, 2 * BLOCK), bf16),
            SDS((2 * ALL, 16, BLOCK), bf16),
            SDS((OWN, 16, BLOCK), f32),
            SDS((SURE, 2, 16, BLOCK), f32),
            SDS((OWN, 4, BLOCK), f32),
            SDS((NX, BLOCK), f32),
            SDS((6, PAIRS), i32),
            SDS((4, BLOCK), i32),
        ),
        in_specs=[HB, HB, HB, HB, SM],
        out_specs=(VM,) * 9,
        scratch_shapes=[
            pltpu.VMEM((9, segs), f32),
            pltpu.VMEM((1, segs), i32),
            pltpu.SMEM((4, GHOST), i32),
            pltpu.SMEM((2, PAIRS), i32),
            pltpu.VMEM((2, PAIRS), i32),
            pltpu.VMEM((1, BLOCK), i32),
            pltpu.VMEM((9, segs), f32),
            pltpu.VMEM((2, PAIRS), i32),
            pltpu.VMEM((1, BLOCK), i32),
            pltpu.VMEM((4, ROWS, BLOCK), f32),
            pltpu.VMEM((OWN, 8, BLOCK), f32),
            pltpu.VMEM((OWN, 1, BLOCK), f32),
            pltpu.VMEM((4, ROWS, BLOCK), f32),
            pltpu.VMEM((4, ROWS, BLOCK), f32),
            pltpu.VMEM((1, BLOCK), f32),
            pltpu.VMEM((NY, BLOCK), f32),
            pltpu.VMEM((1, BLOCK), f32),
            pltpu.VMEM((NX, BLOCK), f32),
            pltpu.VMEM((GROUP, BLOCK, 2 * BLOCK), f32),
            pltpu.VMEM((GROUP, 2 * BLOCK, BLOCK), bf16),
            DMA((5,)), DMA((4,)), DMA((4,)), DMA((4,)), DMA((4,)), DMA, DMA, DMA, DMA,
        ],
        compiler_params=pltpu.CompilerParams(
            collective_id=0, has_side_effects=True, vmem_limit_bytes=24 * 2**20
        ),
    )(segments, cell_ids.reshape(1, -1), send_list, pair_list.T, pair_count)
    force = pl.pallas_call(
        pairs,
        name="pairs",
        out_shape=SDS((2 * ALL, 4, BLOCK), f32),
        in_specs=[SM] + [VM] * 5,
        out_specs=VM,
        scratch_shapes=[
            pltpu.VMEM((GROUP, BLOCK, 2 * BLOCK), f32),
            pltpu.VMEM((GROUP, 2 * BLOCK, BLOCK), bf16),
            pltpu.VMEM((GROUP, 2, 16, BLOCK), f32),
            pltpu.VMEM((2 * ALL + 1, 16, BLOCK), f32),
            pltpu.VMEM((2 * ALL + 1, 16, BLOCK), f32),
        ],
        compiler_params=pltpu.CompilerParams(vmem_limit_bytes=24 * 2**20),
    )(idx, a, b, p, own_sums, sure)
    return pl.pallas_call(
        finale,
        name="finale",
        out_shape=SDS((3, segs), f32),
        in_specs=[SM, VM, VM, VM],
        out_specs=VM,
        scratch_shapes=[
            pltpu.VMEM((ALL, 4, BLOCK), f32),
            pltpu.VMEM((4 * GHOST, 4, BLOCK), f32),
            pltpu.VMEM((4, GHOST + 1, 4, BLOCK), f32),
            pltpu.VMEM((NX, 2 * NY, BLOCK), f32),
            DMA, DMA, DMA((4,)), DMA((4,)),
        ],
        compiler_params=pltpu.CompilerParams(
            collective_id=1, has_side_effects=True, vmem_limit_bytes=16 * 2**20
        ),
    )(inv, far, mom, force)


def solution(mesh):
    in_specs = (
        P(None, ("gx", "gy")),
        P(("gx", "gy"), None),
        P(("gx", "gy")),
        P(("gx", "gy"), None),
        P(("gx", "gy")),
    )
    out_specs = P(None, ("gx", "gy"))
    return jax.shard_map(body, mesh=mesh, in_specs=in_specs, out_specs=out_specs, check_vma=False)
```

```python
import functools

import jax
import jax.numpy as jnp
from jax import lax
from jax.experimental import pallas as pl
from jax.experimental.pallas import tpu as pltpu
from jax.sharding import PartitionSpec as P

f32, bf16, i32 = jnp.float32, jnp.bfloat16, jnp.int32
MESH = pl.DeviceIdType.MESH
BLOCK = 128
OWN = 64
GHOST = 16
ALL = OWN + 4 * GHOST
SIB = ALL
TRASH = 2 * ALL
SURE = 64
PAIRS = 512
NX, NY = 8, 32
GROUP = 16
KDIM = 96
ROWS = 9 * GHOST

strength = 0.2
core_sq = 0.05
far_gain = 0.5
far_core_sq = 0.1


def mm(a, b, nt=False):
    dims = (((1,), (1 if nt else 0,)), ((), ()))
    return lax.dot_general(a, b, dims, preferred_element_type=f32)


def split3(x):
    h = x.astype(bf16)
    r = x - h.astype(f32)
    m = r.astype(bf16)
    return h, m, (r - m.astype(f32)).astype(bf16)


def rows16(parts):
    missing = 16 - sum(p.shape[0] for p in parts)
    return jnp.concatenate(parts + [jnp.zeros((missing, BLOCK), f32)], axis=0)


def eye128():
    shape = (BLOCK, BLOCK)
    return (lax.broadcasted_iota(i32, shape, 0) == lax.broadcasted_iota(i32, shape, 1)).astype(bf16)


def neighbours(ix, iy):
    return (
        (lax.rem(ix + NX - 1, NX), iy),
        (lax.rem(ix + 1, NX), iy),
        (ix, lax.rem(iy + NY - 1, NY)),
        (ix, lax.rem(iy + 1, NY)),
    )


def features(raw, centre, eye, a_ref, b_ref, p_ref, k, with_a):
    pos = raw[0:3] - centre
    l, b = raw[3:6], raw[6:9]
    u = jnp.concatenate([b[0:1] * l, b[1:2] * l, b[2:3] * l], axis=0)
    norm = jnp.sum(pos * pos, axis=0, keepdims=True)
    one = jnp.ones((1, BLOCK), f32)
    zero9 = jnp.zeros((9, BLOCK), f32)
    b_ref[k, :, 0:BLOCK] = jnp.concatenate(split3(rows16([u])), axis=0)
    b_ref[k, :, BLOCK:] = jnp.concatenate(split3(rows16([zero9, pos, norm, one])), axis=0)
    p_ref[k] = rows16([t.astype(f32) for t in split3(pos)] + [one]).astype(bf16)
    if with_a:
        h, m, l = split3(rows16([strength * u, -2.0 * pos, one, norm + core_sq]))
        at = jnp.concatenate([h, h, m, m, h, l, jnp.zeros((BLOCK - KDIM, BLOCK), bf16)], axis=0)
        a_ref[k] = mm(eye, at, nt=True).astype(bf16)


def centre_of(ix, iy):
    r = lax.broadcasted_iota(i32, (3, BLOCK), 0)
    return jnp.where(r == 0, ix.astype(f32), jnp.where(r == 1, iy.astype(f32), 0.0)) + 0.5


def twice(p):
    return jnp.concatenate([p, p], axis=1)


def spread(b):
    h, m, l = b[0:16], b[16:32], b[32:48]
    return jnp.concatenate([h, m, h, m, l, h], axis=0)


def weigh(qd, ww, s):
    r = lax.rsqrt(qd[s, :, BLOCK:])
    w = (qd[s, :, 0:BLOCK] * r) * (r * r)
    wh = w.astype(bf16)
    half = slice(0, BLOCK) if s % 2 == 0 else slice(BLOCK, 2 * BLOCK)
    ww[s // 2, 0:BLOCK, half] = wh
    ww[s // 2, BLOCK:, half] = (w - wh.astype(f32)).astype(bf16)


def sums_over(w, p0, p1):
    f = mm(jnp.concatenate([twice(p0), twice(p1)], axis=0), w)
    return f[0:16, 0:BLOCK], f[16:32, BLOCK:]


def second_sums(ww, s, p0, p1):
    return sums_over(ww[s], p0, p1)


def first_sums(ww, s, p0, p1):
    w = ww[s]
    turned = [
        jnp.concatenate([w[r : r + BLOCK, 0:BLOCK].T, w[r : r + BLOCK, BLOCK:].T], axis=1) for r in (0, BLOCK)
    ]
    return sums_over(jnp.concatenate(turned, axis=0), p0, p1)


def exchange(seg_in, cells_in, send_in, list_in, count, a_ref, b_ref, p_ref, self_ref, sure_ref, far_ref, mom_out,
             idx_out, cnt_out, inv_out, seg, cells, send_list, plist, ids, cnt, sib_seg, sib_ids, sib_cnt, sib_ghost,
             main, last, out_buf, in_buf, row, part, row2, table, qd, ww, l_sem, s_sem, r_sem, ss, sr,
             s1, r1, s2, r2):
    ix, iy = lax.axis_index("gx"), lax.axis_index("gy")
    sib = (ix, iy + 1 - 2 * lax.rem(iy, 2))
    loads = [
        pltpu.make_async_copy(src, dst, l_sem.at[n])
        for n, (src, dst) in enumerate(
            ((seg_in, seg), (send_in, send_list), (cells_in, cells), (list_in, plist), (list_in, ids))
        )
    ]
    for cp in loads:
        cp.start()
    barrier = pltpu.get_barrier_semaphore()

    def greet_y(o, _):
        pl.semaphore_signal(barrier, inc=1, device_id=(ix, lax.rem(iy + o, NY)), device_id_type=MESH)
        return 0

    def greet_x(o, _):
        pl.semaphore_signal(barrier, inc=1, device_id=(lax.rem(ix + o, NX), iy), device_id_type=MESH)
        return 0

    lax.fori_loop(1, NY, greet_y, 0)
    lax.fori_loop(1, NX, greet_x, 0)
    cnt[...] = jnp.full((1, BLOCK), count[0], i32)
    for cp in loads:
        cp.wait()
    for k in range(OWN):
        main[k] = seg[0:8, k * BLOCK : (k + 1) * BLOCK]
        last[k] = seg[8:9, k * BLOCK : (k + 1) * BLOCK]
    lanes = lax.broadcasted_iota(i32, (1, BLOCK), 1)
    for q in range(4):
        where = jnp.full((1, BLOCK), GHOST, i32)
        for j in range(GHOST):
            k = send_list[q, j]
            out_buf[q, 8 * j : 8 * j + 8, :] = main[k]
            out_buf[q, 8 * GHOST + j : 8 * GHOST + j + 1, :] = last[k]
            where = jnp.where(lanes == k, j, where)
        inv_out[q : q + 1, :] = where
    c = jnp.sum(seg[3:6, :] * seg[6:9, :], axis=0, keepdims=True)
    first = 2 * (ix * NY + iy)
    m0 = jnp.sum(jnp.where(cells[...] == first, c, 0.0))
    m1 = jnp.sum(jnp.where(cells[...] == first + 1, c, 0.0))
    mine = jnp.where(lanes == 2 * iy, m0, jnp.where(lanes == 2 * iy + 1, m1, 0.0))
    row[...] = mine
    part[NY - 1 : NY, :] = mine
    centre, sib_centre = centre_of(ix, iy), centre_of(ix, sib[1])
    eye = eye128()

    def build_own(k, _):
        raw = jnp.concatenate([main[k], last[k]], axis=0)
        features(raw, centre, eye, a_ref, b_ref, p_ref, k, True)
        weight = far_gain * jnp.sum(raw[3:6] * raw[6:9], axis=0, keepdims=True)
        far_ref[k] = jnp.concatenate([raw[0:2], raw[2:3] - 0.5, weight], axis=0)
        return 0

    lax.fori_loop(0, OWN, build_own, 0, unroll=4)
    pl.semaphore_wait(barrier, NY - 1 + NX - 1)
    copies = []
    for q, dev in enumerate(neighbours(ix, iy)):
        copies.append(
            pltpu.make_async_remote_copy(
                src_ref=out_buf.at[q], dst_ref=in_buf.at[q ^ 1], send_sem=s_sem.at[q],
                recv_sem=r_sem.at[q ^ 1], device_id=dev, device_id_type=MESH,
            )
        )
        copies[-1].start()

    def send_y(o, _):
        pltpu.make_async_remote_copy(
            src_ref=row, dst_ref=part.at[pl.ds(o - 1, 1)], send_sem=s1, recv_sem=r1,
            device_id=(ix, lax.rem(iy + o, NY)), device_id_type=MESH,
        ).start()
        return 0

    lax.fori_loop(1, NY, send_y, 0)
    shares = [
        pltpu.make_async_remote_copy(
            src_ref=src, dst_ref=dst, send_sem=ss.at[n], recv_sem=sr.at[n], device_id=sib, device_id_type=MESH
        )
        for n, (src, dst) in enumerate(((seg, sib_seg), (ids, sib_ids), (cnt, sib_cnt), (in_buf, sib_ghost)))
    ]
    for cp in shares[:3]:
        cp.start()

    def step(t, _):
        for s in range(0, GROUP, 2):
            k = jnp.minimum(jnp.maximum((t - 2) * GROUP + s, 0), OWN - 2)
            self_ref[k], self_ref[k + 1] = second_sums(ww, s // 2, p_ref[k], p_ref[k + 1])
            weigh(qd, ww, s)
            weigh(qd, ww, s + 1)
            k = jnp.minimum(t * GROUP + s, OWN - 2)
            qd[s] = mm(a_ref[k][:, 0:KDIM], spread(b_ref[k]))
            qd[s + 1] = mm(a_ref[k + 1][:, 0:KDIM], spread(b_ref[k + 1]))
        return 0

    lax.fori_loop(0, OWN // GROUP + 2, step, 0)
    for cp in shares[:3]:
        cp.wait()

    def build_sib(k, _):
        raw = sib_seg[:, pl.ds(pl.multiple_of(k * BLOCK, BLOCK), BLOCK)]
        features(raw, sib_centre, eye, a_ref, b_ref, p_ref, SIB + k, True)
        return 0

    lax.fori_loop(0, OWN, build_sib, 0, unroll=4)
    for cp in copies:
        cp.wait()
    shares[3].start()
    pltpu.make_async_copy(part.at[0 : NY - 1], part.at[0 : NY - 1], r1).wait()
    slab = jnp.sum(part[...], axis=0, keepdims=True)
    row2[...] = slab
    table[pl.ds(NX - 1, 1), :] = slab

    def send_x(o, _):
        pltpu.make_async_remote_copy(
            src_ref=row2, dst_ref=table.at[pl.ds(o - 1, 1)], send_sem=s2, recv_sem=r2,
            device_id=(lax.rem(ix + o, NX), iy), device_id_type=MESH,
        ).start()
        return 0

    lax.fori_loop(1, NX, send_x, 0)

    def ghosts_of(buf, cen, base):
        def build(j, _):
            for q in range(4):
                raw = jnp.concatenate(
                    [buf[q, pl.ds(pl.multiple_of(8 * j, 8), 8), :], buf[q, pl.ds(8 * GHOST + j, 1), :]], axis=0
                )
                features(raw, cen, eye, a_ref, b_ref, p_ref, base + GHOST * q + j, False)
            return 0

        lax.fori_loop(0, GHOST, build, 0)

    ghosts_of(in_buf, centre, OWN)

    def sure_step(t, _):
        for s in range(0, GROUP, 2):
            k = jnp.minimum(jnp.maximum((t - 2) * GROUP + s, 0), SURE - 2)
            sure_ref[k, 0], sure_ref[k + 1, 0] = first_sums(ww, s // 2, p_ref[plist[1, k]], p_ref[plist[1, k + 1]])
            sure_ref[k, 1], sure_ref[k + 1, 1] = second_sums(ww, s // 2, p_ref[plist[0, k]], p_ref[plist[0, k + 1]])
            weigh(qd, ww, s)
            weigh(qd, ww, s + 1)
            k = jnp.minimum(t * GROUP + s, SURE - 2)
            for d in range(2):
                qd[s + d] = mm(a_ref[plist[0, k + d]][:, 0:KDIM], spread(b_ref[plist[1, k + d]]))
        return 0

    lax.fori_loop(0, SURE // GROUP + 2, sure_step, 0)
    idx_out[0:2, :] = ids[...]
    idx_out[2:4, :] = sib_ids[...] + SIB
    idx_out[4:8, :] = jnp.zeros((4, PAIRS), i32)
    cnt_out[0:1, :] = cnt[...]
    cnt_out[1:2, :] = sib_cnt[...]
    shares[3].wait()
    ghosts_of(sib_ghost, sib_centre, SIB + OWN)
    pltpu.make_async_copy(table.at[0 : NX - 1], table.at[0 : NX - 1], r2).wait()
    mom_out[...] = table[...]
    pltpu.make_async_copy(part.at[0 : NY - 1], part.at[0 : NY - 1], s1).wait()
    pltpu.make_async_copy(table.at[0 : NX - 1], table.at[0 : NX - 1], s2).wait()


def finish(acc, p):
    p = p.astype(f32)
    f = (p[0:3] + p[3:6] + p[6:9]) * acc[9:10] - (acc[0:3] + acc[3:6] + acc[6:9])
    return jnp.concatenate([f, jnp.zeros((1, BLOCK), f32)], axis=0)


def pairs(counts, lists, a_ref, b_ref, p_ref, self_ref, sure_ref, out, merged, rows, qd, ww, rr, acc_a, acc_b, sem):
    own_rows, sib_rows = counts[0, 0] - SURE, counts[1, 0] - SURE
    half = (own_rows + sib_rows + 1) // 2
    n_own = jnp.minimum(own_rows, half)
    n_help = jnp.maximum(sib_rows - half, 0)
    total = n_own + n_help
    r = lax.broadcasted_iota(i32, (1, PAIRS), 1) - 2 * GROUP
    skip = SURE - 2 * GROUP
    own_list = pltpu.roll(lists[...], PAIRS - skip, 1)
    sib_list = pltpu.roll(lists[...], PAIRS - (skip + half - n_own), 1)
    live = jnp.logical_and(r >= 0, r < total)
    i = jnp.where(r < n_own, own_list[0:1], sib_list[2:3])
    j = jnp.where(r < n_own, own_list[1:2], sib_list[3:4])
    merged[0:1, :] = jnp.where(live, i, 0)
    merged[1:2, :] = jnp.where(live, j, 0)
    merged[2:3, :] = jnp.where(live, i, TRASH)
    merged[3:4, :] = jnp.where(live, j, TRASH)
    merged[4:6, :] = lists[0:2, :]
    merged[6:8, :] = jnp.zeros((2, PAIRS), i32)
    fetch = pltpu.make_async_copy(merged, rows, sem)
    fetch.start()
    acc_a[0:OWN] = jnp.zeros((OWN, 16, BLOCK), f32)
    acc_b[0:OWN] = self_ref[...]
    acc_b[OWN:ALL] = jnp.zeros((ALL - OWN, 16, BLOCK), f32)

    @pl.when(n_help > 0)
    def _():
        acc_a[SIB : SIB + OWN] = jnp.zeros((OWN, 16, BLOCK), f32)
        acc_b[SIB : SIB + ALL] = jnp.zeros((ALL, 16, BLOCK), f32)

    fetch.wait()

    def add_sure(k, _):
        acc_a[rows[4, k]] += sure_ref[k, 0]
        acc_b[rows[5, k]] += sure_ref[k, 1]
        return 0

    lax.fori_loop(0, SURE, add_sure, 0, unroll=8)

    def step(t, _):
        for s in range(0, GROUP, 2):
            c = t * GROUP + s
            rr[s, 0], rr[s + 1, 0] = first_sums(ww, s // 2, p_ref[rows[1, c]], p_ref[rows[1, c + 1]])
            rr[s, 1], rr[s + 1, 1] = second_sums(ww, s // 2, p_ref[rows[0, c]], p_ref[rows[0, c + 1]])
            weigh(qd, ww, s)
            weigh(qd, ww, s + 1)
            c = c + 2 * GROUP
            for d in range(2):
                qd[s + d] = mm(a_ref[rows[0, c + d]][:, 0:KDIM], spread(b_ref[rows[1, c + d]]))
        for s in range(GROUP):
            c = t * GROUP + s
            acc_a[rows[2, c]] += rr[s, 0]
            acc_b[rows[3, c]] += rr[s, 1]
        return 0

    @pl.when(total > 0)
    def _():
        lax.fori_loop(0, (total + GROUP - 1) // GROUP + 2, step, 0)

    def finish_own(k, _):
        out[k] = finish(acc_a[k] + acc_b[k], p_ref[k])
        return 0

    def finish_other(k, _):
        out[k] = finish(acc_b[k], p_ref[k])
        return 0

    lax.fori_loop(0, OWN, finish_own, 0, unroll=4)
    lax.fori_loop(OWN, ALL, finish_other, 0, unroll=4)

    @pl.when(n_help > 0)
    def _():
        lax.fori_loop(SIB, SIB + OWN, finish_own, 0, unroll=4)
        lax.fori_loop(SIB + OWN, SIB + ALL, finish_other, 0, unroll=4)

    @pl.when(n_help == 0)
    def _():
        out[SIB:] = jnp.zeros((ALL, 4, BLOCK), f32)


def finale(inv, far_ref, mom, force, out, sib_in, gsum, back_in, mb, ss, sr, s_sem, r_sem):
    ix, iy = lax.axis_index("gx"), lax.axis_index("gy")
    sib = (ix, iy + 1 - 2 * lax.rem(iy, 2))
    barrier = pltpu.get_barrier_semaphore()
    near = neighbours(ix, iy)
    for dev in near:
        pl.semaphore_signal(barrier, inc=1, device_id=dev, device_id_type=MESH)
    for q in range(4):
        back_in[q, GHOST] = jnp.zeros((4, BLOCK), f32)
    pl.semaphore_wait(barrier, 4)
    share = pltpu.make_async_remote_copy(
        src_ref=force.at[SIB : SIB + ALL], dst_ref=sib_in, send_sem=ss, recv_sem=sr, device_id=sib,
        device_id_type=MESH,
    )
    share.start()
    wide = jnp.concatenate([mom[...], jnp.zeros((BLOCK - NX, BLOCK), f32)], axis=0).T
    for s in range(NX):
        mb[s] = jnp.broadcast_to(wide[0 : 2 * NY, s : s + 1], (2 * NY, BLOCK))
    centre_x = [lax.rem(ix + (2 * NX - 1 - s), NX).astype(f32) + 0.5 for s in range(NX)]
    sub = lax.broadcasted_iota(i32, (8, BLOCK), 0).astype(f32)
    def far(k, _):
        blk = far_ref[k]
        x, y, z = jnp.broadcast_to(blk[0:1], (8, BLOCK)), jnp.broadcast_to(blk[1:2], (8, BLOCK)), blk[2:3]
        base = z * z + far_core_sq
        dx = [x - cx for cx in centre_x]
        dx2 = [d * d for d in dx]
        hx = [None] * NX
        fy = total = None
        for g in range(2 * NY // 8):
            dy = y - (0.5 * sub + (4.0 * g + 0.25))
            by = dy * dy + base
            gy = None
            for s in range(NX):
                r = lax.rsqrt(by + dx2[s])
                w = (mb[s, 8 * g : 8 * g + 8, :] * r) * (r * r)
                hx[s] = w if g == 0 else hx[s] + w
                gy = w if s == 0 else gy + w
            total = gy if g == 0 else total + gy
            fy = dy * gy if g == 0 else fy + dy * gy
        fx = dx[0] * hx[0]
        for s in range(1, NX):
            fx = fx + dx[s] * hx[s]
        add = lambda t: jnp.sum(t, axis=0, keepdims=True)
        f = jnp.concatenate([add(fx), add(fy), z * add(total)], axis=0)
        where = pl.ds(pl.multiple_of(k * BLOCK, BLOCK), BLOCK)
        out[:, where] = blk[3:4] * f
        return 0

    lax.fori_loop(0, OWN // 4, far, 0)
    share.wait()
    gsum[...] = force[OWN:ALL] + sib_in[OWN:ALL]
    copies = []
    for q, dev in enumerate(near):
        copies.append(
            pltpu.make_async_remote_copy(
                src_ref=gsum.at[GHOST * q : GHOST * q + GHOST], dst_ref=back_in.at[q ^ 1, 0:GHOST],
                send_sem=s_sem.at[q], recv_sem=r_sem.at[q ^ 1], device_id=dev, device_id_type=MESH,
            )
        )
        copies[-1].start()

    lax.fori_loop(OWN // 4, OWN, far, 0)
    for cp in copies:
        cp.wait()

    def combine(k, _):
        f = force[k] + sib_in[k]
        for q in range(4):
            f = f + back_in[q, inv[q, k]]
        where = pl.ds(pl.multiple_of(k * BLOCK, BLOCK), BLOCK)
        out[:, where] = out[:, where] + f[0:3]
        return 0

    lax.fori_loop(0, OWN, combine, 0, unroll=4)


VM, SM = pl.BlockSpec(memory_space=pltpu.VMEM), pl.BlockSpec(memory_space=pltpu.SMEM)
HB = pl.BlockSpec(memory_space=pltpu.HBM)
SDS = jax.ShapeDtypeStruct
DMA = pltpu.SemaphoreType.DMA


def body(segments, pair_list, pair_count, send_list, cell_ids):
    segs = segments.shape[1]
    a, b, p, own_sums, sure, far, mom, idx, cnt, inv = pl.pallas_call(
        exchange,
        name="exchange",
        out_shape=(
            SDS((SIB + OWN, BLOCK, BLOCK), bf16),
            SDS((2 * ALL, 48, 2 * BLOCK), bf16),
            SDS((2 * ALL, 16, BLOCK), bf16),
            SDS((OWN, 16, BLOCK), f32),
            SDS((SURE, 2, 16, BLOCK), f32),
            SDS((OWN, 4, BLOCK), f32),
            SDS((NX, BLOCK), f32),
            SDS((8, PAIRS), i32),
            SDS((2, BLOCK), i32),
            SDS((4, BLOCK), i32),
        ),
        in_specs=[HB, HB, HB, HB, SM],
        out_specs=(VM,) * 10,
        scratch_shapes=[
            pltpu.VMEM((9, segs), f32),
            pltpu.VMEM((1, segs), i32),
            pltpu.SMEM((4, GHOST), i32),
            pltpu.SMEM((2, PAIRS), i32),
            pltpu.VMEM((2, PAIRS), i32),
            pltpu.VMEM((1, BLOCK), i32),
            pltpu.VMEM((9, segs), f32),
            pltpu.VMEM((2, PAIRS), i32),
            pltpu.VMEM((1, BLOCK), i32),
            pltpu.VMEM((4, ROWS, BLOCK), f32),
            pltpu.VMEM((OWN, 8, BLOCK), f32),
            pltpu.VMEM((OWN, 1, BLOCK), f32),
            pltpu.VMEM((4, ROWS, BLOCK), f32),
            pltpu.VMEM((4, ROWS, BLOCK), f32),
            pltpu.VMEM((1, BLOCK), f32),
            pltpu.VMEM((NY, BLOCK), f32),
            pltpu.VMEM((1, BLOCK), f32),
            pltpu.VMEM((NX, BLOCK), f32),
            pltpu.VMEM((GROUP, BLOCK, 2 * BLOCK), f32),
            pltpu.VMEM((GROUP // 2, 2 * BLOCK, 2 * BLOCK), bf16),
            DMA((5,)), DMA((4,)), DMA((4,)), DMA((4,)), DMA((4,)), DMA, DMA, DMA, DMA,
        ],
        compiler_params=pltpu.CompilerParams(
            collective_id=0, has_side_effects=True, vmem_limit_bytes=24 * 2**20
        ),
    )(*[pltpu.with_memory_space_constraint(x, pltpu.HBM) for x in (segments, cell_ids.reshape(1, -1), send_list, pair_list.T)], pair_count)
    force = pl.pallas_call(
        pairs,
        name="pairs",
        out_shape=SDS((2 * ALL, 4, BLOCK), f32),
        in_specs=[SM] + [VM] * 6,
        out_specs=VM,
        scratch_shapes=[
            pltpu.VMEM((8, PAIRS), i32),
            pltpu.SMEM((8, PAIRS), i32),
            pltpu.VMEM((GROUP, BLOCK, 2 * BLOCK), f32),
            pltpu.VMEM((GROUP // 2, 2 * BLOCK, 2 * BLOCK), bf16),
            pltpu.VMEM((GROUP, 2, 16, BLOCK), f32),
            pltpu.VMEM((2 * ALL + 1, 16, BLOCK), f32),
            pltpu.VMEM((2 * ALL + 1, 16, BLOCK), f32),
            DMA,
        ],
        compiler_params=pltpu.CompilerParams(vmem_limit_bytes=24 * 2**20),
    )(cnt, idx, a, b, p, own_sums, sure)
    return pl.pallas_call(
        finale,
        name="finale",
        out_shape=SDS((3, segs), f32),
        in_specs=[SM, VM, VM, VM],
        out_specs=VM,
        scratch_shapes=[
            pltpu.VMEM((ALL, 4, BLOCK), f32),
            pltpu.VMEM((4 * GHOST, 4, BLOCK), f32),
            pltpu.VMEM((4, GHOST + 1, 4, BLOCK), f32),
            pltpu.VMEM((NX, 2 * NY, BLOCK), f32),
            DMA, DMA, DMA((4,)), DMA((4,)),
        ],
        compiler_params=pltpu.CompilerParams(
            collective_id=1, has_side_effects=True, vmem_limit_bytes=16 * 2**20
        ),
    )(inv, far, mom, force)


def solution(mesh):
    in_specs = (
        P(None, ("gx", "gy")),
        P(("gx", "gy"), None),
        P(("gx", "gy")),
        P(("gx", "gy"), None),
        P(("gx", "gy")),
    )
    out_specs = P(None, ("gx", "gy"))
    return jax.shard_map(body, mesh=mesh, in_specs=in_specs, out_specs=out_specs, check_vma=False)
```

```python
import functools

import jax
import jax.numpy as jnp
from jax import lax
from jax.experimental import pallas as pl
from jax.experimental.pallas import tpu as pltpu
from jax.sharding import PartitionSpec as P

f32, bf16, i32 = jnp.float32, jnp.bfloat16, jnp.int32
MESH = pl.DeviceIdType.MESH
BLOCK = 128
OWN = 64
GHOST = 16
ALL = OWN + 4 * GHOST
SIB = ALL
TRASH = 2 * ALL
SURE = 64
PAIRS = 512
NX, NY = 8, 32
GROUP = 16
KDIM = 96
ROWS = 9 * GHOST

strength = 0.2
core_sq = 0.05
far_gain = 0.5
far_core_sq = 0.1


def mm(a, b, nt=False):
    dims = (((1,), (1 if nt else 0,)), ((), ()))
    return lax.dot_general(a, b, dims, preferred_element_type=f32)


def split3(x):
    h = x.astype(bf16)
    r = x - h.astype(f32)
    m = r.astype(bf16)
    return h, m, (r - m.astype(f32)).astype(bf16)


def rows16(parts):
    missing = 16 - sum(p.shape[0] for p in parts)
    return jnp.concatenate(parts + [jnp.zeros((missing, BLOCK), f32)], axis=0)


def eye128():
    shape = (BLOCK, BLOCK)
    return (lax.broadcasted_iota(i32, shape, 0) == lax.broadcasted_iota(i32, shape, 1)).astype(bf16)


def neighbours(ix, iy):
    return (
        (lax.rem(ix + NX - 1, NX), iy),
        (lax.rem(ix + 1, NX), iy),
        (ix, lax.rem(iy + NY - 1, NY)),
        (ix, lax.rem(iy + 1, NY)),
    )


def features(raw, centre, eye, a_ref, b_ref, p_ref, k, with_a):
    pos = raw[0:3] - centre
    l, b = raw[3:6], raw[6:9]
    u = jnp.concatenate([b[0:1] * l, b[1:2] * l, b[2:3] * l], axis=0)
    norm = jnp.sum(pos * pos, axis=0, keepdims=True)
    one = jnp.ones((1, BLOCK), f32)
    zero9 = jnp.zeros((9, BLOCK), f32)
    b_ref[k, :, 0:BLOCK] = jnp.concatenate(split3(rows16([u])), axis=0)
    b_ref[k, :, BLOCK:] = jnp.concatenate(split3(rows16([zero9, pos, norm, one])), axis=0)
    p_ref[k] = rows16([t.astype(f32) for t in split3(pos)] + [one]).astype(bf16)
    if with_a:
        h, m, l = split3(rows16([strength * u, -2.0 * pos, one, norm + core_sq]))
        at = jnp.concatenate([h, h, m, m, h, l, jnp.zeros((BLOCK - KDIM, BLOCK), bf16)], axis=0)
        a_ref[k] = mm(eye, at, nt=True).astype(bf16)


def centre_of(ix, iy):
    r = lax.broadcasted_iota(i32, (3, BLOCK), 0)
    return jnp.where(r == 0, ix.astype(f32), jnp.where(r == 1, iy.astype(f32), 0.0)) + 0.5


def twice(p):
    return jnp.concatenate([p, p], axis=1)


def spread(b):
    h, m, l = b[0:16], b[16:32], b[32:48]
    return jnp.concatenate([h, m, h, m, l, h], axis=0)


def weigh(qd, ww, s):
    r = lax.rsqrt(qd[s, :, BLOCK:])
    w = (qd[s, :, 0:BLOCK] * r) * (r * r)
    wh = w.astype(bf16)
    half = slice(0, BLOCK) if s % 2 == 0 else slice(BLOCK, 2 * BLOCK)
    ww[s // 2, 0:BLOCK, half] = wh
    ww[s // 2, BLOCK:, half] = (w - wh.astype(f32)).astype(bf16)


def sums_over(w, p0, p1):
    f = mm(jnp.concatenate([twice(p0), twice(p1)], axis=0), w)
    return f[0:16, 0:BLOCK], f[16:32, BLOCK:]


def second_sums(ww, s, p0, p1):
    return sums_over(ww[s], p0, p1)


def first_sums(ww, s, p0, p1):
    w = ww[s]
    turned = [
        jnp.concatenate([w[r : r + BLOCK, 0:BLOCK].T, w[r : r + BLOCK, BLOCK:].T], axis=1) for r in (0, BLOCK)
    ]
    return sums_over(jnp.concatenate(turned, axis=0), p0, p1)


def pipeline(groups, products, sums, close=None):
    qd, ww = products.qd, products.ww

    def step(c, b, a):
        for s in range(0, GROUP, 2):
            if c is not None:
                sums(c * GROUP + s, s)
            if b:
                weigh(qd, ww, s)
                weigh(qd, ww, s + 1)
            if a is not None:
                for d in range(2):
                    products(a * GROUP + s + d, s + d)
        if c is not None and close is not None:
            close(c)

    def body(t, _):
        step(t - 2, True, t)
        return 0

    step(None, False, 0)
    step(None, True, 1)
    lax.fori_loop(2, groups, body, 0)
    step(groups - 2, True, None)
    step(groups - 1, False, None)


class Products:
    def __init__(self, qd, ww, a_ref, b_ref, pick):
        self.qd, self.ww, self.a_ref, self.b_ref, self.pick = qd, ww, a_ref, b_ref, pick

    def __call__(self, r, s):
        i, j = self.pick(r)
        self.qd[s] = mm(self.a_ref[i][:, 0:KDIM], spread(self.b_ref[j]))


def along(ix, iy, o):
    z, hi, core = iy // 4, lax.rem(iy // 2, 2), lax.rem(iy, 2)
    return ix, lax.rem(z + o % 8, 8) * 4 + hi * 2 + lax.rem(core + o // 8, 2)


def across(ix, iy, o):
    z, hi, core = iy // 4, lax.rem(iy // 2, 2), lax.rem(iy, 2)
    return lax.rem(ix + o % 8, 8), z * 4 + lax.rem(hi + o // 8, 2) * 2 + core


def exchange(seg_in, cells_in, send_in, list_in, count, a_ref, b_ref, p_ref, self_ref, sure_ref, far_ref, mom_out,
             idx_out, cnt_out, inv_out, seg, cells, send_list, plist, ids, cnt, sib_seg, sib_ids, sib_cnt, sib_ghost,
             main, last, out_buf, in_buf, row, part, row2, table, qd, ww, l_sem, s_sem, r_sem, ss, sr,
             s1, r1, s2, r2):
    ix, iy = lax.axis_index("gx"), lax.axis_index("gy")
    sib = (ix, iy + 1 - 2 * lax.rem(iy, 2))
    loads = [
        pltpu.make_async_copy(src, dst, l_sem.at[n])
        for n, (src, dst) in enumerate(
            ((seg_in, seg), (send_in, send_list), (cells_in, cells), (list_in, plist), (list_in, ids))
        )
    ]
    for cp in loads:
        cp.start()
    barrier = pltpu.get_barrier_semaphore()

    other_y = (ix, lax.rem(iy + 2 * lax.rem(iy, 2) + NY - 1, NY))
    for dev in [along(ix, iy, o) for o in range(1, 16)] + [across(ix, iy, o) for o in range(1, 16)] + [other_y]:
        pl.semaphore_signal(barrier, inc=1, device_id=dev, device_id_type=MESH)
    cnt[...] = jnp.full((1, BLOCK), count[0], i32)
    for cp in loads:
        cp.wait()
    for k in range(OWN):
        main[k] = seg[0:8, k * BLOCK : (k + 1) * BLOCK]
        last[k] = seg[8:9, k * BLOCK : (k + 1) * BLOCK]
    lanes = lax.broadcasted_iota(i32, (1, BLOCK), 1)
    for q in range(4):
        where = jnp.full((1, BLOCK), GHOST, i32)
        for j in range(GHOST):
            k = send_list[q, j]
            out_buf[q, 8 * j : 8 * j + 8, :] = main[k]
            out_buf[q, 8 * GHOST + j : 8 * GHOST + j + 1, :] = last[k]
            where = jnp.where(lanes == k, j, where)
        inv_out[q : q + 1, :] = where
    c = jnp.sum(seg[3:6, :] * seg[6:9, :], axis=0, keepdims=True)
    first = 2 * (ix * NY + iy)
    m0 = jnp.sum(jnp.where(cells[...] == first, c, 0.0))
    m1 = jnp.sum(jnp.where(cells[...] == first + 1, c, 0.0))
    mine = jnp.where(lanes == 2 * iy, m0, jnp.where(lanes == 2 * iy + 1, m1, 0.0))
    row[...] = mine
    part[15:16, :] = mine
    centre, sib_centre = centre_of(ix, iy), centre_of(ix, sib[1])
    eye = eye128()

    def build_own(k, _):
        raw = jnp.concatenate([main[k], last[k]], axis=0)
        features(raw, centre, eye, a_ref, b_ref, p_ref, k, True)
        weight = far_gain * jnp.sum(raw[3:6] * raw[6:9], axis=0, keepdims=True)
        far_ref[k] = jnp.concatenate([raw[0:2], raw[2:3] - 0.5, weight], axis=0)
        return 0

    lax.fori_loop(0, OWN, build_own, 0, unroll=4)
    pl.semaphore_wait(barrier, 31)
    copies = []
    for q, dev in enumerate(neighbours(ix, iy)):
        copies.append(
            pltpu.make_async_remote_copy(
                src_ref=out_buf.at[q], dst_ref=in_buf.at[q ^ 1], send_sem=s_sem.at[q],
                recv_sem=r_sem.at[q ^ 1], device_id=dev, device_id_type=MESH,
            )
        )
        copies[-1].start()

    for o in range(1, 16):
        pltpu.make_async_remote_copy(
            src_ref=row, dst_ref=part.at[o - 1 : o], send_sem=s1, recv_sem=r1,
            device_id=along(ix, iy, o), device_id_type=MESH,
        ).start()
    shares = [
        pltpu.make_async_remote_copy(
            src_ref=src, dst_ref=dst, send_sem=ss.at[n], recv_sem=sr.at[n], device_id=sib, device_id_type=MESH
        )
        for n, (src, dst) in enumerate(((seg, sib_seg), (ids, sib_ids), (cnt, sib_cnt), (in_buf, sib_ghost)))
    ]
    for cp in shares[:3]:
        cp.start()

    def own_sums(k, s):
        self_ref[k], self_ref[k + 1] = second_sums(ww, s // 2, p_ref[k], p_ref[k + 1])

    pipeline(OWN // GROUP, Products(qd, ww, a_ref, b_ref, lambda k: (k, k)), own_sums)
    for cp in shares[:3]:
        cp.wait()

    def build_sib(k, _):
        raw = sib_seg[:, pl.ds(pl.multiple_of(k * BLOCK, BLOCK), BLOCK)]
        features(raw, sib_centre, eye, a_ref, b_ref, p_ref, SIB + k, True)
        return 0

    lax.fori_loop(0, OWN, build_sib, 0, unroll=4)
    for cp in copies:
        cp.wait()
    shares[3].start()
    pltpu.make_async_copy(part.at[0:15], part.at[0:15], r1).wait()
    slab = jnp.sum(part[...], axis=0, keepdims=True)
    row2[...] = slab
    table[15:16, :] = slab
    for o in range(1, 16):
        pltpu.make_async_remote_copy(
            src_ref=row2, dst_ref=table.at[o - 1 : o], send_sem=s2, recv_sem=r2,
            device_id=across(ix, iy, o), device_id_type=MESH,
        ).start()

    def ghosts_of(buf, cen, base):
        def build(j, _):
            for q in range(4):
                raw = jnp.concatenate(
                    [buf[q, pl.ds(pl.multiple_of(8 * j, 8), 8), :], buf[q, pl.ds(8 * GHOST + j, 1), :]], axis=0
                )
                features(raw, cen, eye, a_ref, b_ref, p_ref, base + GHOST * q + j, False)
            return 0

        lax.fori_loop(0, GHOST, build, 0)

    ghosts_of(in_buf, centre, OWN)

    def sure_sums(k, s):
        sure_ref[k, 0], sure_ref[k + 1, 0] = first_sums(ww, s // 2, p_ref[plist[1, k]], p_ref[plist[1, k + 1]])
        sure_ref[k, 1], sure_ref[k + 1, 1] = second_sums(ww, s // 2, p_ref[plist[0, k]], p_ref[plist[0, k + 1]])

    pipeline(SURE // GROUP, Products(qd, ww, a_ref, b_ref, lambda k: (plist[0, k], plist[1, k])), sure_sums)
    idx_out[0:2, :] = ids[...]
    idx_out[2:4, :] = sib_ids[...] + SIB
    idx_out[4:8, :] = jnp.zeros((4, PAIRS), i32)
    cnt_out[0:1, :] = cnt[...]
    cnt_out[1:2, :] = sib_cnt[...]
    shares[3].wait()
    ghosts_of(sib_ghost, sib_centre, SIB + OWN)
    pltpu.make_async_copy(table.at[0:15], table.at[0:15], r2).wait()
    mom_out[...] = table[0:NX, :] + table[NX:, :]
    pltpu.make_async_copy(part.at[0:15], part.at[0:15], s1).wait()
    pltpu.make_async_copy(table.at[0:15], table.at[0:15], s2).wait()


def finish(acc, p):
    p = p.astype(f32)
    f = (p[0:3] + p[3:6] + p[6:9]) * acc[9:10] - (acc[0:3] + acc[3:6] + acc[6:9])
    return jnp.concatenate([f, jnp.zeros((1, BLOCK), f32)], axis=0)


def pairs(counts, lists, a_ref, b_ref, p_ref, self_ref, sure_ref, out, merged, rows, qd, ww, rr, acc_a, acc_b, sem):
    own_rows, sib_rows = counts[0, 0] - SURE, counts[1, 0] - SURE
    half = (own_rows + sib_rows + 1) // 2
    n_own = jnp.minimum(own_rows, half)
    n_help = jnp.maximum(sib_rows - half, 0)
    total = n_own + n_help
    r = lax.broadcasted_iota(i32, (1, PAIRS), 1)
    own_list = pltpu.roll(lists[...], PAIRS - SURE, 1)
    sib_list = pltpu.roll(lists[...], PAIRS - (SURE + half - n_own), 1)
    live = r < total
    i = jnp.where(r < n_own, own_list[0:1], sib_list[2:3])
    j = jnp.where(r < n_own, own_list[1:2], sib_list[3:4])
    merged[0:1, :] = jnp.where(live, i, 0)
    merged[1:2, :] = jnp.where(live, j, 0)
    merged[2:3, :] = jnp.where(live, i, TRASH)
    merged[3:4, :] = jnp.where(live, j, TRASH)
    merged[4:6, :] = lists[0:2, :]
    merged[6:8, :] = jnp.zeros((2, PAIRS), i32)
    fetch = pltpu.make_async_copy(merged, rows, sem)
    fetch.start()
    acc_a[0:OWN] = jnp.zeros((OWN, 16, BLOCK), f32)
    acc_b[0:OWN] = self_ref[...]
    acc_b[OWN:ALL] = jnp.zeros((ALL - OWN, 16, BLOCK), f32)

    @pl.when(n_help > 0)
    def _():
        acc_a[SIB : SIB + OWN] = jnp.zeros((OWN, 16, BLOCK), f32)
        acc_b[SIB : SIB + ALL] = jnp.zeros((ALL, 16, BLOCK), f32)

    fetch.wait()

    def add_sure(k, _):
        acc_a[rows[4, k]] += sure_ref[k, 0]
        acc_b[rows[5, k]] += sure_ref[k, 1]
        return 0

    lax.fori_loop(0, SURE, add_sure, 0, unroll=8)

    def sums(c, s):
        rr[s, 0], rr[s + 1, 0] = first_sums(ww, s // 2, p_ref[rows[1, c]], p_ref[rows[1, c + 1]])
        rr[s, 1], rr[s + 1, 1] = second_sums(ww, s // 2, p_ref[rows[0, c]], p_ref[rows[0, c + 1]])

    def close(t):
        for s in range(GROUP):
            acc_a[rows[2, t * GROUP + s]] += rr[s, 0]
            acc_b[rows[3, t * GROUP + s]] += rr[s, 1]

    products = Products(qd, ww, a_ref, b_ref, lambda c: (rows[0, c], rows[1, c]))
    pipeline(jnp.maximum((total + GROUP - 1) // GROUP, 2), products, sums, close)

    def finish_own(k, _):
        out[k] = finish(acc_a[k] + acc_b[k], p_ref[k])
        return 0

    def finish_other(k, _):
        out[k] = finish(acc_b[k], p_ref[k])
        return 0

    lax.fori_loop(0, OWN, finish_own, 0, unroll=4)
    lax.fori_loop(OWN, ALL, finish_other, 0, unroll=4)

    @pl.when(n_help > 0)
    def _():
        lax.fori_loop(SIB, SIB + OWN, finish_own, 0, unroll=4)
        lax.fori_loop(SIB + OWN, SIB + ALL, finish_other, 0, unroll=4)

    @pl.when(n_help == 0)
    def _():
        out[SIB:] = jnp.zeros((ALL, 4, BLOCK), f32)


def finale(inv, far_ref, mom, force, out, sib_in, gsum, back_in, mb, ss, sr, s_sem, r_sem):
    ix, iy = lax.axis_index("gx"), lax.axis_index("gy")
    sib = (ix, iy + 1 - 2 * lax.rem(iy, 2))
    barrier = pltpu.get_barrier_semaphore()
    near = neighbours(ix, iy)
    for dev in near:
        pl.semaphore_signal(barrier, inc=1, device_id=dev, device_id_type=MESH)
    for q in range(4):
        back_in[q, GHOST] = jnp.zeros((4, BLOCK), f32)
    pl.semaphore_wait(barrier, 4)
    share = pltpu.make_async_remote_copy(
        src_ref=force.at[SIB : SIB + ALL], dst_ref=sib_in, send_sem=ss, recv_sem=sr, device_id=sib,
        device_id_type=MESH,
    )
    share.start()
    wide = jnp.concatenate([mom[...], jnp.zeros((BLOCK - NX, BLOCK), f32)], axis=0).T
    for s in range(NX):
        mb[s] = jnp.broadcast_to(wide[0 : 2 * NY, s : s + 1], (2 * NY, BLOCK))
    centre_x = [lax.rem(ix + (2 * NX - 1 - s), NX).astype(f32) + 0.5 for s in range(NX)]
    sub = lax.broadcasted_iota(i32, (8, BLOCK), 0).astype(f32)
    def far(k, _):
        blk = far_ref[k]
        x, y, z = jnp.broadcast_to(blk[0:1], (8, BLOCK)), jnp.broadcast_to(blk[1:2], (8, BLOCK)), blk[2:3]
        base = z * z + far_core_sq
        dx = [x - cx for cx in centre_x]
        dx2 = [d * d for d in dx]
        hx = [None] * NX
        fy = total = None
        for g in range(2 * NY // 8):
            dy = y - (0.5 * sub + (4.0 * g + 0.25))
            by = dy * dy + base
            gy = None
            for s in range(NX):
                r = lax.rsqrt(by + dx2[s])
                w = (mb[s, 8 * g : 8 * g + 8, :] * r) * (r * r)
                hx[s] = w if g == 0 else hx[s] + w
                gy = w if s == 0 else gy + w
            total = gy if g == 0 else total + gy
            fy = dy * gy if g == 0 else fy + dy * gy
        fx = dx[0] * hx[0]
        for s in range(1, NX):
            fx = fx + dx[s] * hx[s]
        add = lambda t: jnp.sum(t, axis=0, keepdims=True)
        f = jnp.concatenate([add(fx), add(fy), z * add(total)], axis=0)
        where = pl.ds(pl.multiple_of(k * BLOCK, BLOCK), BLOCK)
        out[:, where] = blk[3:4] * f
        return 0

    lax.fori_loop(0, OWN // 4, far, 0)
    share.wait()
    gsum[...] = force[OWN:ALL] + sib_in[OWN:ALL]
    copies = []
    for q, dev in enumerate(near):
        copies.append(
            pltpu.make_async_remote_copy(
                src_ref=gsum.at[GHOST * q : GHOST * q + GHOST], dst_ref=back_in.at[q ^ 1, 0:GHOST],
                send_sem=s_sem.at[q], recv_sem=r_sem.at[q ^ 1], device_id=dev, device_id_type=MESH,
            )
        )
        copies[-1].start()

    lax.fori_loop(OWN // 4, OWN, far, 0)
    for cp in copies:
        cp.wait()

    def combine(k, _):
        f = force[k] + sib_in[k]
        for q in range(4):
            f = f + back_in[q, inv[q, k]]
        where = pl.ds(pl.multiple_of(k * BLOCK, BLOCK), BLOCK)
        out[:, where] = out[:, where] + f[0:3]
        return 0

    lax.fori_loop(0, OWN, combine, 0, unroll=4)


VM, SM = pl.BlockSpec(memory_space=pltpu.VMEM), pl.BlockSpec(memory_space=pltpu.SMEM)
HB = pl.BlockSpec(memory_space=pltpu.HBM)
SDS = jax.ShapeDtypeStruct
DMA = pltpu.SemaphoreType.DMA


def body(segments, pair_list, pair_count, send_list, cell_ids):
    segs = segments.shape[1]
    a, b, p, own_sums, sure, far, mom, idx, cnt, inv = pl.pallas_call(
        exchange,
        name="exchange",
        out_shape=(
            SDS((SIB + OWN, BLOCK, BLOCK), bf16),
            SDS((2 * ALL, 48, 2 * BLOCK), bf16),
            SDS((2 * ALL, 16, BLOCK), bf16),
            SDS((OWN, 16, BLOCK), f32),
            SDS((SURE, 2, 16, BLOCK), f32),
            SDS((OWN, 4, BLOCK), f32),
            SDS((NX, BLOCK), f32),
            SDS((8, PAIRS), i32),
            SDS((2, BLOCK), i32),
            SDS((4, BLOCK), i32),
        ),
        in_specs=[HB, HB, HB, HB, SM],
        out_specs=(VM,) * 10,
        scratch_shapes=[
            pltpu.VMEM((9, segs), f32),
            pltpu.VMEM((1, segs), i32),
            pltpu.SMEM((4, GHOST), i32),
            pltpu.SMEM((2, PAIRS), i32),
            pltpu.VMEM((2, PAIRS), i32),
            pltpu.VMEM((1, BLOCK), i32),
            pltpu.VMEM((9, segs), f32),
            pltpu.VMEM((2, PAIRS), i32),
            pltpu.VMEM((1, BLOCK), i32),
            pltpu.VMEM((4, ROWS, BLOCK), f32),
            pltpu.VMEM((OWN, 8, BLOCK), f32),
            pltpu.VMEM((OWN, 1, BLOCK), f32),
            pltpu.VMEM((4, ROWS, BLOCK), f32),
            pltpu.VMEM((4, ROWS, BLOCK), f32),
            pltpu.VMEM((1, BLOCK), f32),
            pltpu.VMEM((16, BLOCK), f32),
            pltpu.VMEM((1, BLOCK), f32),
            pltpu.VMEM((16, BLOCK), f32),
            pltpu.VMEM((GROUP, BLOCK, 2 * BLOCK), f32),
            pltpu.VMEM((GROUP // 2, 2 * BLOCK, 2 * BLOCK), bf16),
            DMA((5,)), DMA((4,)), DMA((4,)), DMA((4,)), DMA((4,)), DMA, DMA, DMA, DMA,
        ],
        compiler_params=pltpu.CompilerParams(
            collective_id=0, has_side_effects=True, vmem_limit_bytes=24 * 2**20
        ),
    )(*[pltpu.with_memory_space_constraint(x, pltpu.HBM) for x in (segments, cell_ids.reshape(1, -1), send_list, pair_list.T)], pair_count)
    force = pl.pallas_call(
        pairs,
        name="pairs",
        out_shape=SDS((2 * ALL, 4, BLOCK), f32),
        in_specs=[SM] + [VM] * 6,
        out_specs=VM,
        scratch_shapes=[
            pltpu.VMEM((8, PAIRS), i32),
            pltpu.SMEM((8, PAIRS), i32),
            pltpu.VMEM((GROUP, BLOCK, 2 * BLOCK), f32),
            pltpu.VMEM((GROUP // 2, 2 * BLOCK, 2 * BLOCK), bf16),
            pltpu.VMEM((GROUP, 2, 16, BLOCK), f32),
            pltpu.VMEM((2 * ALL + 1, 16, BLOCK), f32),
            pltpu.VMEM((2 * ALL + 1, 16, BLOCK), f32),
            DMA,
        ],
        compiler_params=pltpu.CompilerParams(vmem_limit_bytes=24 * 2**20),
    )(cnt, idx, a, b, p, own_sums, sure)
    return pl.pallas_call(
        finale,
        name="finale",
        out_shape=SDS((3, segs), f32),
        in_specs=[SM, VM, VM, VM],
        out_specs=VM,
        scratch_shapes=[
            pltpu.VMEM((ALL, 4, BLOCK), f32),
            pltpu.VMEM((4 * GHOST, 4, BLOCK), f32),
            pltpu.VMEM((4, GHOST + 1, 4, BLOCK), f32),
            pltpu.VMEM((NX, 2 * NY, BLOCK), f32),
            DMA, DMA, DMA((4,)), DMA((4,)),
        ],
        compiler_params=pltpu.CompilerParams(
            collective_id=1, has_side_effects=True, vmem_limit_bytes=16 * 2**20
        ),
    )(inv, far, mom, force)


def solution(mesh):
    in_specs = (
        P(None, ("gx", "gy")),
        P(("gx", "gy"), None),
        P(("gx", "gy")),
        P(("gx", "gy"), None),
        P(("gx", "gy")),
    )
    out_specs = P(None, ("gx", "gy"))
    return jax.shard_map(body, mesh=mesh, in_specs=in_specs, out_specs=out_specs, check_vma=False)
```

```python
import functools

import jax
import jax.numpy as jnp
from jax import lax
from jax.experimental import pallas as pl
from jax.experimental.pallas import tpu as pltpu
from jax.sharding import PartitionSpec as P

f32, bf16, i32 = jnp.float32, jnp.bfloat16, jnp.int32
MESH = pl.DeviceIdType.MESH
BLOCK = 128
OWN = 64
GHOST = 16
ALL = OWN + 4 * GHOST
SIB = ALL
TRASH = 2 * ALL
SURE = 64
PAIRS = 512
NX, NY = 8, 32
GROUP = 16
KDIM = 96
ROWS = 9 * GHOST

strength = 0.2
core_sq = 0.05
far_gain = 0.5
far_core_sq = 0.1


def mm(a, b, nt=False):
    dims = (((1,), (1 if nt else 0,)), ((), ()))
    return lax.dot_general(a, b, dims, preferred_element_type=f32)


def split3(x):
    h = x.astype(bf16)
    r = x - h.astype(f32)
    m = r.astype(bf16)
    return h, m, (r - m.astype(f32)).astype(bf16)


def rows16(parts):
    missing = 16 - sum(p.shape[0] for p in parts)
    return jnp.concatenate(parts + [jnp.zeros((missing, BLOCK), f32)], axis=0)


def eye128():
    shape = (BLOCK, BLOCK)
    return (lax.broadcasted_iota(i32, shape, 0) == lax.broadcasted_iota(i32, shape, 1)).astype(bf16)


def neighbours(ix, iy):
    return (
        (lax.rem(ix + NX - 1, NX), iy),
        (lax.rem(ix + 1, NX), iy),
        (ix, lax.rem(iy + NY - 1, NY)),
        (ix, lax.rem(iy + 1, NY)),
    )


def features(raw, centre, eye, a_ref, b_ref, p_ref, k, with_a):
    pos = raw[0:3] - centre
    l, b = raw[3:6], raw[6:9]
    u = jnp.concatenate([b[0:1] * l, b[1:2] * l, b[2:3] * l], axis=0)
    norm = jnp.sum(pos * pos, axis=0, keepdims=True)
    one = jnp.ones((1, BLOCK), f32)
    zero9 = jnp.zeros((9, BLOCK), f32)
    b_ref[k, :, 0:BLOCK] = jnp.concatenate(split3(rows16([u])), axis=0)
    b_ref[k, :, BLOCK:] = jnp.concatenate(split3(rows16([zero9, pos, norm, one])), axis=0)
    p_ref[k] = rows16([t.astype(f32) for t in split3(pos)] + [one]).astype(bf16)
    if with_a:
        h, m, l = split3(rows16([strength * u, -2.0 * pos, one, norm + core_sq]))
        at = jnp.concatenate([h, h, m, m, h, l, jnp.zeros((BLOCK - KDIM, BLOCK), bf16)], axis=0)
        a_ref[k] = mm(eye, at, nt=True).astype(bf16)


def centre_of(ix, iy):
    r = lax.broadcasted_iota(i32, (3, BLOCK), 0)
    return jnp.where(r == 0, ix.astype(f32), jnp.where(r == 1, iy.astype(f32), 0.0)) + 0.5


def twice(p):
    return jnp.concatenate([p, p], axis=1)


def spread(b):
    h, m, l = b[0:16], b[16:32], b[32:48]
    return jnp.concatenate([h, m, h, m, l, h], axis=0)


def weigh(qd, ww, s):
    r = lax.rsqrt(qd[s, :, BLOCK:])
    w = (qd[s, :, 0:BLOCK] * r) * (r * r)
    wh = w.astype(bf16)
    half = slice(0, BLOCK) if s % 2 == 0 else slice(BLOCK, 2 * BLOCK)
    ww[s // 2, 0:BLOCK, half] = wh
    ww[s // 2, BLOCK:, half] = (w - wh.astype(f32)).astype(bf16)


def sums_over(w, p0, p1):
    f = mm(jnp.concatenate([twice(p0), twice(p1)], axis=0), w)
    return f[0:16, 0:BLOCK], f[16:32, BLOCK:]


def second_sums(ww, s, p0, p1):
    return sums_over(ww[s], p0, p1)


def first_sums(ww, s, p0, p1):
    w = ww[s]
    turned = [
        jnp.concatenate([w[r : r + BLOCK, 0:BLOCK].T, w[r : r + BLOCK, BLOCK:].T], axis=1) for r in (0, BLOCK)
    ]
    return sums_over(jnp.concatenate(turned, axis=0), p0, p1)


def pipeline(groups, products, sums, close=None):
    qd, ww = products.qd, products.ww

    def step(c, b, a):
        for s in range(0, GROUP, 2):
            if c is not None:
                sums(c * GROUP + s, s)
            if b:
                weigh(qd, ww, s)
                weigh(qd, ww, s + 1)
            if a is not None:
                for d in range(2):
                    products(a * GROUP + s + d, s + d)
        if c is not None and close is not None:
            close(c)

    def body(t, _):
        step(t - 2, True, t)
        return 0

    step(None, False, 0)
    step(None, True, 1)
    lax.fori_loop(2, groups, body, 0)
    step(groups - 2, True, None)
    step(groups - 1, False, None)


class Products:
    def __init__(self, qd, ww, a_ref, b_ref, pick):
        self.qd, self.ww, self.a_ref, self.b_ref, self.pick = qd, ww, a_ref, b_ref, pick

    def __call__(self, r, s):
        i, j = self.pick(r)
        self.qd[s] = mm(self.a_ref[i][:, 0:KDIM], spread(self.b_ref[j]))


def along(ix, iy, o):
    z, hi, core = iy // 4, lax.rem(iy // 2, 2), lax.rem(iy, 2)
    return ix, lax.rem(z + o % 8, 8) * 4 + hi * 2 + lax.rem(core + o // 8, 2)


def across(ix, iy, o):
    z, hi, core = iy // 4, lax.rem(iy // 2, 2), lax.rem(iy, 2)
    return lax.rem(ix + o % 8, 8), z * 4 + lax.rem(hi + o // 8, 2) * 2 + core


def exchange(seg_in, cells_in, send_in, list_in, count, a_ref, b_ref, p_ref, self_ref, sure_ref, far_ref, mom_out,
             idx_out, cnt_out, inv_out, seg, cells, send_list, plist, ids, cnt, sib_seg, sib_ids, sib_cnt, sib_ghost,
             main, last, out_buf, in_buf, row, part, row2, table, qd, ww, l_sem, s_sem, r_sem, ss, sr,
             s1, r1, s2, r2):
    ix, iy = lax.axis_index("gx"), lax.axis_index("gy")
    sib = (ix, iy + 1 - 2 * lax.rem(iy, 2))
    loads = [
        pltpu.make_async_copy(src, dst, l_sem.at[n])
        for n, (src, dst) in enumerate(
            ((seg_in, seg), (send_in, send_list), (cells_in, cells), (list_in, plist), (list_in, ids))
        )
    ]
    for cp in loads:
        cp.start()
    barrier = pltpu.get_barrier_semaphore()

    other_y = (ix, lax.rem(iy + 2 * lax.rem(iy, 2) + NY - 1, NY))
    for dev in [along(ix, iy, o) for o in range(1, 16)] + [across(ix, iy, o) for o in range(1, 16)] + [other_y]:
        pl.semaphore_signal(barrier, inc=1, device_id=dev, device_id_type=MESH)
    cnt[...] = jnp.full((1, BLOCK), count[0], i32)
    for cp in loads:
        cp.wait()
    for k in range(OWN):
        main[k] = seg[0:8, k * BLOCK : (k + 1) * BLOCK]
        last[k] = seg[8:9, k * BLOCK : (k + 1) * BLOCK]
    lanes = lax.broadcasted_iota(i32, (1, BLOCK), 1)
    for q in range(4):
        where = jnp.full((1, BLOCK), GHOST, i32)
        for j in range(GHOST):
            k = send_list[q, j]
            out_buf[q, 8 * j : 8 * j + 8, :] = main[k]
            out_buf[q, 8 * GHOST + j : 8 * GHOST + j + 1, :] = last[k]
            where = jnp.where(lanes == k, j, where)
        inv_out[q : q + 1, :] = where
    c = jnp.sum(seg[3:6, :] * seg[6:9, :], axis=0, keepdims=True)
    first = 2 * (ix * NY + iy)
    m0 = jnp.sum(jnp.where(cells[...] == first, c, 0.0))
    m1 = jnp.sum(jnp.where(cells[...] == first + 1, c, 0.0))
    mine = jnp.where(lanes == 2 * iy, m0, jnp.where(lanes == 2 * iy + 1, m1, 0.0))
    row[...] = mine
    part[15:16, :] = mine
    centre, sib_centre = centre_of(ix, iy), centre_of(ix, sib[1])
    eye = eye128()

    def build_own(k, _):
        raw = jnp.concatenate([main[k], last[k]], axis=0)
        features(raw, centre, eye, a_ref, b_ref, p_ref, k, True)
        weight = far_gain * jnp.sum(raw[3:6] * raw[6:9], axis=0, keepdims=True)
        far_ref[k] = jnp.concatenate([raw[0:2], raw[2:3] - 0.5, weight], axis=0)
        return 0

    lax.fori_loop(0, OWN, build_own, 0, unroll=8)
    pl.semaphore_wait(barrier, 31)
    for o in range(1, 16):
        pltpu.make_async_remote_copy(
            src_ref=row, dst_ref=part.at[o - 1 : o], send_sem=s1, recv_sem=r1,
            device_id=along(ix, iy, o), device_id_type=MESH,
        ).start()
    copies = []
    for q, dev in enumerate(neighbours(ix, iy)):
        copies.append(
            pltpu.make_async_remote_copy(
                src_ref=out_buf.at[q], dst_ref=in_buf.at[q ^ 1], send_sem=s_sem.at[q],
                recv_sem=r_sem.at[q ^ 1], device_id=dev, device_id_type=MESH,
            )
        )
        copies[-1].start()

    shares = [
        pltpu.make_async_remote_copy(
            src_ref=src, dst_ref=dst, send_sem=ss.at[n], recv_sem=sr.at[n], device_id=sib, device_id_type=MESH
        )
        for n, (src, dst) in enumerate(((seg, sib_seg), (ids, sib_ids), (cnt, sib_cnt), (in_buf, sib_ghost)))
    ]
    for cp in shares[:3]:
        cp.start()

    def own_sums(k, s):
        self_ref[k], self_ref[k + 1] = second_sums(ww, s // 2, p_ref[k], p_ref[k + 1])

    pipeline(OWN // GROUP, Products(qd, ww, a_ref, b_ref, lambda k: (k, k)), own_sums)
    for cp in shares[:3]:
        cp.wait()

    def build_sib(k, _):
        raw = sib_seg[:, pl.ds(pl.multiple_of(k * BLOCK, BLOCK), BLOCK)]
        features(raw, sib_centre, eye, a_ref, b_ref, p_ref, SIB + k, True)
        return 0

    lax.fori_loop(0, OWN, build_sib, 0, unroll=8)
    pltpu.make_async_copy(part.at[0:15], part.at[0:15], r1).wait()
    slab = jnp.sum(part[...], axis=0, keepdims=True)
    row2[...] = slab
    table[15:16, :] = slab
    for o in range(1, 16):
        pltpu.make_async_remote_copy(
            src_ref=row2, dst_ref=table.at[o - 1 : o], send_sem=s2, recv_sem=r2,
            device_id=across(ix, iy, o), device_id_type=MESH,
        ).start()

    for cp in copies:
        cp.wait()
    shares[3].start()
    def ghosts_of(buf, cen, base):
        def build(j, _):
            for q in range(4):
                raw = jnp.concatenate(
                    [buf[q, pl.ds(pl.multiple_of(8 * j, 8), 8), :], buf[q, pl.ds(8 * GHOST + j, 1), :]], axis=0
                )
                features(raw, cen, eye, a_ref, b_ref, p_ref, base + GHOST * q + j, False)
            return 0

        lax.fori_loop(0, GHOST, build, 0, unroll=2)

    ghosts_of(in_buf, centre, OWN)

    def sure_sums(k, s):
        sure_ref[k, 0], sure_ref[k + 1, 0] = first_sums(ww, s // 2, p_ref[plist[1, k]], p_ref[plist[1, k + 1]])
        sure_ref[k, 1], sure_ref[k + 1, 1] = second_sums(ww, s // 2, p_ref[plist[0, k]], p_ref[plist[0, k + 1]])

    pipeline(SURE // GROUP, Products(qd, ww, a_ref, b_ref, lambda k: (plist[0, k], plist[1, k])), sure_sums)
    idx_out[0:2, :] = ids[...]
    idx_out[2:4, :] = sib_ids[...] + SIB
    idx_out[4:8, :] = jnp.zeros((4, PAIRS), i32)
    cnt_out[0:1, :] = cnt[...]
    cnt_out[1:2, :] = sib_cnt[...]
    shares[3].wait()
    ghosts_of(sib_ghost, sib_centre, SIB + OWN)
    pltpu.make_async_copy(table.at[0:15], table.at[0:15], r2).wait()
    mom_out[...] = table[0:NX, :] + table[NX:, :]
    pltpu.make_async_copy(part.at[0:15], part.at[0:15], s1).wait()
    pltpu.make_async_copy(table.at[0:15], table.at[0:15], s2).wait()


def finish(acc, p):
    p = p.astype(f32)
    f = (p[0:3] + p[3:6] + p[6:9]) * acc[9:10] - (acc[0:3] + acc[3:6] + acc[6:9])
    return jnp.concatenate([f, jnp.zeros((1, BLOCK), f32)], axis=0)


def pairs(counts, lists, a_ref, b_ref, p_ref, self_ref, sure_ref, out, merged, rows, qd, ww, rr, acc_a, acc_b, sem):
    own_rows, sib_rows = counts[0, 0] - SURE, counts[1, 0] - SURE
    half = (own_rows + sib_rows + 1) // 2
    n_own = jnp.minimum(own_rows, half)
    n_help = jnp.maximum(sib_rows - half, 0)
    total = n_own + n_help
    r = lax.broadcasted_iota(i32, (1, PAIRS), 1)
    own_list = pltpu.roll(lists[...], PAIRS - SURE, 1)
    sib_list = pltpu.roll(lists[...], PAIRS - (SURE + half - n_own), 1)
    live = r < total
    i = jnp.where(r < n_own, own_list[0:1], sib_list[2:3])
    j = jnp.where(r < n_own, own_list[1:2], sib_list[3:4])
    merged[0:1, :] = jnp.where(live, i, 0)
    merged[1:2, :] = jnp.where(live, j, 0)
    merged[2:3, :] = jnp.where(live, i, TRASH)
    merged[3:4, :] = jnp.where(live, j, TRASH)
    merged[4:6, :] = lists[0:2, :]
    merged[6:8, :] = jnp.zeros((2, PAIRS), i32)
    fetch = pltpu.make_async_copy(merged, rows, sem)
    fetch.start()
    acc_a[0:OWN] = jnp.zeros((OWN, 16, BLOCK), f32)
    acc_b[0:OWN] = self_ref[...]
    acc_b[OWN:ALL] = jnp.zeros((ALL - OWN, 16, BLOCK), f32)

    @pl.when(n_help > 0)
    def _():
        acc_a[SIB : SIB + OWN] = jnp.zeros((OWN, 16, BLOCK), f32)
        acc_b[SIB : SIB + ALL] = jnp.zeros((ALL, 16, BLOCK), f32)

    fetch.wait()

    def add_sure(k, _):
        acc_a[rows[4, k]] += sure_ref[k, 0]
        acc_b[rows[5, k]] += sure_ref[k, 1]
        return 0

    lax.fori_loop(0, SURE, add_sure, 0, unroll=8)

    def sums(c, s):
        rr[s, 0], rr[s + 1, 0] = first_sums(ww, s // 2, p_ref[rows[1, c]], p_ref[rows[1, c + 1]])
        rr[s, 1], rr[s + 1, 1] = second_sums(ww, s // 2, p_ref[rows[0, c]], p_ref[rows[0, c + 1]])

    def close(t):
        for s in range(GROUP):
            acc_a[rows[2, t * GROUP + s]] += rr[s, 0]
            acc_b[rows[3, t * GROUP + s]] += rr[s, 1]

    products = Products(qd, ww, a_ref, b_ref, lambda c: (rows[0, c], rows[1, c]))
    pipeline(jnp.maximum((total + GROUP - 1) // GROUP, 2), products, sums, close)

    def finish_own(k, _):
        out[k] = finish(acc_a[k] + acc_b[k], p_ref[k])
        return 0

    def finish_other(k, _):
        out[k] = finish(acc_b[k], p_ref[k])
        return 0

    lax.fori_loop(0, OWN, finish_own, 0, unroll=8)
    lax.fori_loop(OWN, ALL, finish_other, 0, unroll=8)

    @pl.when(n_help > 0)
    def _():
        lax.fori_loop(SIB, SIB + OWN, finish_own, 0, unroll=4)
        lax.fori_loop(SIB + OWN, SIB + ALL, finish_other, 0, unroll=4)

    @pl.when(n_help == 0)
    def _():
        out[SIB:] = jnp.zeros((ALL, 4, BLOCK), f32)


def finale(inv, far_ref, mom, force, out, sib_in, back_in, mb, ss, sr, s_sem, r_sem):
    ix, iy = lax.axis_index("gx"), lax.axis_index("gy")
    core = lax.rem(iy, 2)
    sy = iy + 1 - 2 * core
    lower, upper = lax.rem(ix + NX - 1, NX), lax.rem(ix + 1, NX)
    step = 2 * core - 1
    beyond = lax.rem(iy + step + NY, NY)
    sib_beyond = lax.rem(sy - step + NY, NY)
    beyond_sib = lax.rem(iy + 2 * step + NY, NY)
    barrier = pltpu.get_barrier_semaphore()
    peers = [(lower, iy), (upper, iy), (ix, sy), (ix, beyond), (lower, sy), (upper, sy), (ix, sib_beyond), (ix, beyond_sib)]
    for dev in peers:
        pl.semaphore_signal(barrier, inc=1, device_id=dev, device_id_type=MESH)
    for n in range(8):
        back_in[n, GHOST] = jnp.zeros((4, BLOCK), f32)
    near_side, away_side = OWN + GHOST * (3 - core), OWN + GHOST * (2 + core)
    sib_near, sib_away = SIB + OWN + GHOST * (2 + core), SIB + OWN + GHOST * (3 - core)
    pl.semaphore_wait(barrier, 8)
    share = pltpu.make_async_remote_copy(
        src_ref=force.at[SIB : SIB + OWN], dst_ref=sib_in, send_sem=ss, recv_sem=sr, device_id=(ix, sy),
        device_id_type=MESH,
    )
    sends = (
        (OWN, 1, (lower, iy)),
        (OWN + GHOST, 0, (upper, iy)),
        (away_side, 3, (ix, beyond)),
        (SIB + OWN, 5, (lower, sy)),
        (SIB + OWN + GHOST, 4, (upper, sy)),
        (sib_away, 7, (ix, sib_beyond)),
        (near_side, 2, (ix, sy)),
    )
    copies = [
        pltpu.make_async_remote_copy(
            src_ref=force.at[pl.ds(start, GHOST)], dst_ref=back_in.at[slot, 0:GHOST], send_sem=s_sem.at[slot],
            recv_sem=r_sem.at[slot], device_id=dev, device_id_type=MESH,
        )
        for start, slot, dev in sends
    ]
    for cp in copies:
        cp.start()
    share.start()
    for j in range(GHOST):
        back_in[6, j] = force[sib_near + j]
    wide = jnp.concatenate([mom[...], jnp.zeros((BLOCK - NX, BLOCK), f32)], axis=0).T
    for s in range(NX):
        mb[s] = jnp.broadcast_to(wide[0 : 2 * NY, s : s + 1], (2 * NY, BLOCK))
    centre_x = [lax.rem(ix + (2 * NX - 1 - s), NX).astype(f32) + 0.5 for s in range(NX)]
    sub = lax.broadcasted_iota(i32, (8, BLOCK), 0).astype(f32)
    def far(k, _):
        blk = far_ref[k]
        x, y, z = jnp.broadcast_to(blk[0:1], (8, BLOCK)), jnp.broadcast_to(blk[1:2], (8, BLOCK)), blk[2:3]
        base = z * z + far_core_sq
        dx = [x - cx for cx in centre_x]
        dx2 = [d * d for d in dx]
        hx = [None] * NX
        fy = total = None
        for g in range(2 * NY // 8):
            dy = y - (0.5 * sub + (4.0 * g + 0.25))
            by = dy * dy + base
            gy = None
            for s in range(NX):
                r = lax.rsqrt(by + dx2[s])
                w = (mb[s, 8 * g : 8 * g + 8, :] * r) * (r * r)
                hx[s] = w if g == 0 else hx[s] + w
                gy = w if s == 0 else gy + w
            total = gy if g == 0 else total + gy
            fy = dy * gy if g == 0 else fy + dy * gy
        fx = dx[0] * hx[0]
        for s in range(1, NX):
            fx = fx + dx[s] * hx[s]
        add = lambda t: jnp.sum(t, axis=0, keepdims=True)
        f = jnp.concatenate([add(fx), add(fy), z * add(total)], axis=0)
        where = pl.ds(pl.multiple_of(k * BLOCK, BLOCK), BLOCK)
        out[:, where] = blk[3:4] * f
        return 0

    lax.fori_loop(0, OWN, far, 0)
    for cp in copies:
        cp.wait()
    share.wait()
    lists = (0, 1, 3 - core, 2 + core, 0, 1, 3 - core, 2 + core)

    def combine(k, _):
        f = force[k] + sib_in[k]
        for n, q in enumerate(lists):
            f = f + back_in[n, inv[q, k]]
        where = pl.ds(pl.multiple_of(k * BLOCK, BLOCK), BLOCK)
        out[:, where] = out[:, where] + f[0:3]
        return 0

    lax.fori_loop(0, OWN, combine, 0, unroll=8)


VM, SM = pl.BlockSpec(memory_space=pltpu.VMEM), pl.BlockSpec(memory_space=pltpu.SMEM)
HB = pl.BlockSpec(memory_space=pltpu.HBM)
SDS = jax.ShapeDtypeStruct
DMA = pltpu.SemaphoreType.DMA


def body(segments, pair_list, pair_count, send_list, cell_ids):
    segs = segments.shape[1]
    a, b, p, own_sums, sure, far, mom, idx, cnt, inv = pl.pallas_call(
        exchange,
        name="exchange",
        out_shape=(
            SDS((SIB + OWN, BLOCK, BLOCK), bf16),
            SDS((2 * ALL, 48, 2 * BLOCK), bf16),
            SDS((2 * ALL, 16, BLOCK), bf16),
            SDS((OWN, 16, BLOCK), f32),
            SDS((SURE, 2, 16, BLOCK), f32),
            SDS((OWN, 4, BLOCK), f32),
            SDS((NX, BLOCK), f32),
            SDS((8, PAIRS), i32),
            SDS((2, BLOCK), i32),
            SDS((4, BLOCK), i32),
        ),
        in_specs=[HB, HB, HB, HB, SM],
        out_specs=(VM,) * 10,
        scratch_shapes=[
            pltpu.VMEM((9, segs), f32),
            pltpu.VMEM((1, segs), i32),
            pltpu.SMEM((4, GHOST), i32),
            pltpu.SMEM((2, PAIRS), i32),
            pltpu.VMEM((2, PAIRS), i32),
            pltpu.VMEM((1, BLOCK), i32),
            pltpu.VMEM((9, segs), f32),
            pltpu.VMEM((2, PAIRS), i32),
            pltpu.VMEM((1, BLOCK), i32),
            pltpu.VMEM((4, ROWS, BLOCK), f32),
            pltpu.VMEM((OWN, 8, BLOCK), f32),
            pltpu.VMEM((OWN, 1, BLOCK), f32),
            pltpu.VMEM((4, ROWS, BLOCK), f32),
            pltpu.VMEM((4, ROWS, BLOCK), f32),
            pltpu.VMEM((1, BLOCK), f32),
            pltpu.VMEM((16, BLOCK), f32),
            pltpu.VMEM((1, BLOCK), f32),
            pltpu.VMEM((16, BLOCK), f32),
            pltpu.VMEM((GROUP, BLOCK, 2 * BLOCK), f32),
            pltpu.VMEM((GROUP // 2, 2 * BLOCK, 2 * BLOCK), bf16),
            DMA((5,)), DMA((4,)), DMA((4,)), DMA((4,)), DMA((4,)), DMA, DMA, DMA, DMA,
        ],
        compiler_params=pltpu.CompilerParams(
            collective_id=0, has_side_effects=True, vmem_limit_bytes=24 * 2**20
        ),
    )(*[pltpu.with_memory_space_constraint(x, pltpu.HBM) for x in (segments, cell_ids.reshape(1, -1), send_list, pair_list.T)], pair_count)
    force = pl.pallas_call(
        pairs,
        name="pairs",
        out_shape=SDS((2 * ALL, 4, BLOCK), f32),
        in_specs=[SM] + [VM] * 6,
        out_specs=VM,
        scratch_shapes=[
            pltpu.VMEM((8, PAIRS), i32),
            pltpu.SMEM((8, PAIRS), i32),
            pltpu.VMEM((GROUP, BLOCK, 2 * BLOCK), f32),
            pltpu.VMEM((GROUP // 2, 2 * BLOCK, 2 * BLOCK), bf16),
            pltpu.VMEM((GROUP, 2, 16, BLOCK), f32),
            pltpu.VMEM((2 * ALL + 1, 16, BLOCK), f32),
            pltpu.VMEM((2 * ALL + 1, 16, BLOCK), f32),
            DMA,
        ],
        compiler_params=pltpu.CompilerParams(vmem_limit_bytes=24 * 2**20),
    )(cnt, idx, a, b, p, own_sums, sure)
    return pl.pallas_call(
        finale,
        name="finale",
        out_shape=SDS((3, segs), f32),
        in_specs=[SM, VM, VM, VM],
        out_specs=VM,
        scratch_shapes=[
            pltpu.VMEM((OWN, 4, BLOCK), f32),
            pltpu.VMEM((8, GHOST + 1, 4, BLOCK), f32),
            pltpu.VMEM((NX, 2 * NY, BLOCK), f32),
            DMA, DMA, DMA((8,)), DMA((8,)),
        ],
        compiler_params=pltpu.CompilerParams(
            collective_id=1, has_side_effects=True, vmem_limit_bytes=16 * 2**20
        ),
    )(inv, far, mom, force)


def solution(mesh):
    in_specs = (
        P(None, ("gx", "gy")),
        P(("gx", "gy"), None),
        P(("gx", "gy")),
        P(("gx", "gy"), None),
        P(("gx", "gy")),
    )
    out_specs = P(None, ("gx", "gy"))
    return jax.shard_map(body, mesh=mesh, in_specs=in_specs, out_specs=out_specs, check_vma=False)
```

```python
import functools

import jax
import jax.numpy as jnp
from jax import lax
from jax.experimental import pallas as pl
from jax.experimental.pallas import tpu as pltpu
from jax.sharding import PartitionSpec as P

f32, bf16, i32 = jnp.float32, jnp.bfloat16, jnp.int32
MESH = pl.DeviceIdType.MESH
BLOCK = 128
OWN = 64
GHOST = 16
ALL = OWN + 4 * GHOST
SIB = ALL
TRASH = 2 * ALL
SURE = 64
PAIRS = 512
NX, NY = 8, 32
GROUP = 16
KDIM = 96
ROWS = 9 * GHOST

strength = 0.2
core_sq = 0.05
far_gain = 0.5
far_core_sq = 0.1


def mm(a, b, nt=False):
    dims = (((1,), (1 if nt else 0,)), ((), ()))
    return lax.dot_general(a, b, dims, preferred_element_type=f32)


def split3(x):
    h = x.astype(bf16)
    r = x - h.astype(f32)
    m = r.astype(bf16)
    return h, m, (r - m.astype(f32)).astype(bf16)


def rows16(parts):
    missing = 16 - sum(p.shape[0] for p in parts)
    return jnp.concatenate(parts + [jnp.zeros((missing, BLOCK), f32)], axis=0)


def eye128():
    shape = (BLOCK, BLOCK)
    return (lax.broadcasted_iota(i32, shape, 0) == lax.broadcasted_iota(i32, shape, 1)).astype(bf16)


def neighbours(ix, iy):
    return (
        (lax.rem(ix + NX - 1, NX), iy),
        (lax.rem(ix + 1, NX), iy),
        (ix, lax.rem(iy + NY - 1, NY)),
        (ix, lax.rem(iy + 1, NY)),
    )


def features(raw, centre, eye, a_ref, b_ref, p_ref, k, with_a):
    pos = raw[0:3] - centre
    l, b = raw[3:6], raw[6:9]
    u = jnp.concatenate([b[0:1] * l, b[1:2] * l, b[2:3] * l], axis=0)
    norm = jnp.sum(pos * pos, axis=0, keepdims=True)
    one = jnp.ones((1, BLOCK), f32)
    zero9 = jnp.zeros((9, BLOCK), f32)
    b_ref[k, :, 0:BLOCK] = jnp.concatenate(split3(rows16([u])), axis=0)
    b_ref[k, :, BLOCK:] = jnp.concatenate(split3(rows16([zero9, pos, norm, one])), axis=0)
    p_ref[k] = rows16([t.astype(f32) for t in split3(pos)] + [one]).astype(bf16)
    if with_a:
        h, m, l = split3(rows16([strength * u, -2.0 * pos, one, norm + core_sq]))
        at = jnp.concatenate([h, h, m, m, h, l, jnp.zeros((BLOCK - KDIM, BLOCK), bf16)], axis=0)
        a_ref[k] = mm(eye, at, nt=True).astype(bf16)


def centre_of(ix, iy):
    r = lax.broadcasted_iota(i32, (3, BLOCK), 0)
    return jnp.where(r == 0, ix.astype(f32), jnp.where(r == 1, iy.astype(f32), 0.0)) + 0.5


def twice(p):
    return jnp.concatenate([p, p], axis=1)


def spread(b):
    h, m, l = b[0:16], b[16:32], b[32:48]
    return jnp.concatenate([h, m, h, m, l, h], axis=0)


def weigh(qd, ww, s):
    r = lax.rsqrt(qd[s, :, BLOCK:])
    w = (qd[s, :, 0:BLOCK] * r) * (r * r)
    wh = w.astype(bf16)
    half = slice(0, BLOCK) if s % 2 == 0 else slice(BLOCK, 2 * BLOCK)
    ww[s // 2, 0:BLOCK, half] = wh
    ww[s // 2, BLOCK:, half] = (w - wh.astype(f32)).astype(bf16)


def sums_over(w, p0, p1):
    f = mm(jnp.concatenate([twice(p0), twice(p1)], axis=0), w)
    return f[0:16, 0:BLOCK], f[16:32, BLOCK:]


def second_sums(ww, s, p0, p1):
    return sums_over(ww[s], p0, p1)


def first_sums(ww, s, p0, p1):
    w = ww[s]
    turned = [
        jnp.concatenate([w[r : r + BLOCK, 0:BLOCK].T, w[r : r + BLOCK, BLOCK:].T], axis=1) for r in (0, BLOCK)
    ]
    return sums_over(jnp.concatenate(turned, axis=0), p0, p1)


def pipeline(groups, products, sums, close=None):
    qd, ww = products.qd, products.ww

    def step(c, b, a):
        for s in range(0, GROUP, 2):
            if c is not None:
                sums(c * GROUP + s, s)
            if b:
                weigh(qd, ww, s)
                weigh(qd, ww, s + 1)
            if a is not None:
                for d in range(2):
                    products(a * GROUP + s + d, s + d)
        if c is not None and close is not None:
            close(c)

    def body(t, _):
        step(t - 2, True, t)
        return 0

    step(None, False, 0)
    step(None, True, 1)
    lax.fori_loop(2, groups, body, 0)
    step(groups - 2, True, None)
    step(groups - 1, False, None)


class Products:
    def __init__(self, qd, ww, a_ref, b_ref, pick):
        self.qd, self.ww, self.a_ref, self.b_ref, self.pick = qd, ww, a_ref, b_ref, pick

    def __call__(self, r, s):
        i, j = self.pick(r)
        self.qd[s] = mm(self.a_ref[i][:, 0:KDIM], spread(self.b_ref[j]))


def along(ix, iy, o):
    z, hi, core = iy // 4, lax.rem(iy // 2, 2), lax.rem(iy, 2)
    return ix, lax.rem(z + o % 8, 8) * 4 + hi * 2 + lax.rem(core + o // 8, 2)


def across(ix, iy, o):
    z, hi, core = iy // 4, lax.rem(iy // 2, 2), lax.rem(iy, 2)
    return lax.rem(ix + o % 8, 8), z * 4 + lax.rem(hi + o // 8, 2) * 2 + core


def exchange(seg_in, cells_in, send_in, list_in, count, a_ref, b_ref, p_ref, self_ref, sure_ref, far_ref, mom_out,
             idx_out, cnt_out, inv_out, seg, cells, send_list, plist, ids, cnt, sib_seg, sib_ids, sib_cnt, sib_ghost,
             main, last, out_buf, in_buf, row, part, row2, table, qd, ww, l_sem, s_sem, r_sem, ss, sr,
             s1, r1, s2, r2):
    ix, iy = lax.axis_index("gx"), lax.axis_index("gy")
    sib = (ix, iy + 1 - 2 * lax.rem(iy, 2))
    loads = [
        pltpu.make_async_copy(src, dst, l_sem.at[n])
        for n, (src, dst) in enumerate(
            ((seg_in, seg), (send_in, send_list), (cells_in, cells), (list_in, plist), (list_in, ids))
        )
    ]
    for cp in loads:
        cp.start()
    barrier = pltpu.get_barrier_semaphore()

    other_y = (ix, lax.rem(iy + 2 * lax.rem(iy, 2) + NY - 1, NY))
    for dev in [along(ix, iy, o) for o in range(1, 16)] + [across(ix, iy, o) for o in range(1, 16)] + [other_y]:
        pl.semaphore_signal(barrier, inc=1, device_id=dev, device_id_type=MESH)
    cnt[...] = jnp.full((1, BLOCK), count[0], i32)
    for cp in loads:
        cp.wait()
    for k in range(OWN):
        main[k] = seg[0:8, k * BLOCK : (k + 1) * BLOCK]
        last[k] = seg[8:9, k * BLOCK : (k + 1) * BLOCK]
    lanes = lax.broadcasted_iota(i32, (1, BLOCK), 1)
    for q in range(4):
        where = jnp.full((1, BLOCK), GHOST, i32)
        for j in range(GHOST):
            k = send_list[q, j]
            out_buf[q, 8 * j : 8 * j + 8, :] = main[k]
            out_buf[q, 8 * GHOST + j : 8 * GHOST + j + 1, :] = last[k]
            where = jnp.where(lanes == k, j, where)
        inv_out[q : q + 1, :] = where
    c = jnp.sum(seg[3:6, :] * seg[6:9, :], axis=0, keepdims=True)
    first = 2 * (ix * NY + iy)
    m0 = jnp.sum(jnp.where(cells[...] == first, c, 0.0))
    m1 = jnp.sum(jnp.where(cells[...] == first + 1, c, 0.0))
    mine = jnp.where(lanes == 2 * iy, m0, jnp.where(lanes == 2 * iy + 1, m1, 0.0))
    row[...] = mine
    part[15:16, :] = mine
    centre, sib_centre = centre_of(ix, iy), centre_of(ix, sib[1])
    eye = eye128()

    def build_own(k, _):
        raw = jnp.concatenate([main[k], last[k]], axis=0)
        features(raw, centre, eye, a_ref, b_ref, p_ref, k, True)
        weight = far_gain * jnp.sum(raw[3:6] * raw[6:9], axis=0, keepdims=True)
        far_ref[k] = jnp.concatenate([raw[0:2], raw[2:3] - 0.5, weight], axis=0)
        return 0

    lax.fori_loop(0, OWN, build_own, 0, unroll=16)
    pl.semaphore_wait(barrier, 31)
    for o in range(1, 16):
        pltpu.make_async_remote_copy(
            src_ref=row, dst_ref=part.at[o - 1 : o], send_sem=s1, recv_sem=r1,
            device_id=along(ix, iy, o), device_id_type=MESH,
        ).start()
    copies = []
    for q, dev in enumerate(neighbours(ix, iy)):
        copies.append(
            pltpu.make_async_remote_copy(
                src_ref=out_buf.at[q], dst_ref=in_buf.at[q ^ 1], send_sem=s_sem.at[q],
                recv_sem=r_sem.at[q ^ 1], device_id=dev, device_id_type=MESH,
            )
        )
        copies[-1].start()

    shares = [
        pltpu.make_async_remote_copy(
            src_ref=src, dst_ref=dst, send_sem=ss.at[n], recv_sem=sr.at[n], device_id=sib, device_id_type=MESH
        )
        for n, (src, dst) in enumerate(((seg, sib_seg), (ids, sib_ids), (cnt, sib_cnt), (in_buf, sib_ghost)))
    ]
    for cp in shares[:3]:
        cp.start()

    def own_sums(k, s):
        self_ref[k], self_ref[k + 1] = second_sums(ww, s // 2, p_ref[k], p_ref[k + 1])

    pipeline(OWN // GROUP, Products(qd, ww, a_ref, b_ref, lambda k: (k, k)), own_sums)
    for cp in shares[:3]:
        cp.wait()

    def build_sib(k, _):
        raw = sib_seg[:, pl.ds(pl.multiple_of(k * BLOCK, BLOCK), BLOCK)]
        features(raw, sib_centre, eye, a_ref, b_ref, p_ref, SIB + k, True)
        return 0

    lax.fori_loop(0, OWN, build_sib, 0, unroll=16)
    pltpu.make_async_copy(part.at[0:15], part.at[0:15], r1).wait()
    slab = jnp.sum(part[...], axis=0, keepdims=True)
    row2[...] = slab
    table[15:16, :] = slab
    for o in range(1, 16):
        pltpu.make_async_remote_copy(
            src_ref=row2, dst_ref=table.at[o - 1 : o], send_sem=s2, recv_sem=r2,
            device_id=across(ix, iy, o), device_id_type=MESH,
        ).start()

    for cp in copies:
        cp.wait()
    shares[3].start()
    def ghosts_of(buf, cen, base):
        def build(j, _):
            for q in range(4):
                raw = jnp.concatenate(
                    [buf[q, pl.ds(pl.multiple_of(8 * j, 8), 8), :], buf[q, pl.ds(8 * GHOST + j, 1), :]], axis=0
                )
                features(raw, cen, eye, a_ref, b_ref, p_ref, base + GHOST * q + j, False)
            return 0

        lax.fori_loop(0, GHOST, build, 0, unroll=4)

    ghosts_of(in_buf, centre, OWN)

    def sure_sums(k, s):
        sure_ref[k, 0], sure_ref[k + 1, 0] = first_sums(ww, s // 2, p_ref[plist[1, k]], p_ref[plist[1, k + 1]])
        sure_ref[k, 1], sure_ref[k + 1, 1] = second_sums(ww, s // 2, p_ref[plist[0, k]], p_ref[plist[0, k + 1]])

    pipeline(SURE // GROUP, Products(qd, ww, a_ref, b_ref, lambda k: (plist[0, k], plist[1, k])), sure_sums)
    idx_out[0:2, :] = ids[...]
    idx_out[2:4, :] = sib_ids[...] + SIB
    idx_out[4:8, :] = jnp.zeros((4, PAIRS), i32)
    cnt_out[0:1, :] = cnt[...]
    cnt_out[1:2, :] = sib_cnt[...]
    shares[3].wait()
    ghosts_of(sib_ghost, sib_centre, SIB + OWN)
    pltpu.make_async_copy(table.at[0:15], table.at[0:15], r2).wait()
    mom_out[...] = table[0:NX, :] + table[NX:, :]
    pltpu.make_async_copy(part.at[0:15], part.at[0:15], s1).wait()
    pltpu.make_async_copy(table.at[0:15], table.at[0:15], s2).wait()


def finish(acc, p):
    p = p.astype(f32)
    f = (p[0:3] + p[3:6] + p[6:9]) * acc[9:10] - (acc[0:3] + acc[3:6] + acc[6:9])
    return jnp.concatenate([f, jnp.zeros((1, BLOCK), f32)], axis=0)


def pairs(counts, lists, a_ref, b_ref, p_ref, self_ref, sure_ref, out, merged, rows, qd, ww, rr, acc_a, acc_b, sem):
    own_rows, sib_rows = counts[0, 0] - SURE, counts[1, 0] - SURE
    half = (own_rows + sib_rows + 1) // 2
    n_own = jnp.minimum(own_rows, half)
    n_help = jnp.maximum(sib_rows - half, 0)
    total = n_own + n_help
    r = lax.broadcasted_iota(i32, (1, PAIRS), 1)
    own_list = pltpu.roll(lists[...], PAIRS - SURE, 1)
    sib_list = pltpu.roll(lists[...], PAIRS - (SURE + half - n_own), 1)
    live = r < total
    i = jnp.where(r < n_own, own_list[0:1], sib_list[2:3])
    j = jnp.where(r < n_own, own_list[1:2], sib_list[3:4])
    merged[0:1, :] = jnp.where(live, i, 0)
    merged[1:2, :] = jnp.where(live, j, 0)
    merged[2:3, :] = jnp.where(live, i, TRASH)
    merged[3:4, :] = jnp.where(live, j, TRASH)
    merged[4:6, :] = lists[0:2, :]
    merged[6:8, :] = jnp.zeros((2, PAIRS), i32)
    fetch = pltpu.make_async_copy(merged, rows, sem)
    fetch.start()
    acc_a[0:OWN] = jnp.zeros((OWN, 16, BLOCK), f32)
    acc_b[0:OWN] = self_ref[...]
    acc_b[OWN:ALL] = jnp.zeros((ALL - OWN, 16, BLOCK), f32)

    @pl.when(n_help > 0)
    def _():
        acc_a[SIB : SIB + OWN] = jnp.zeros((OWN, 16, BLOCK), f32)
        acc_b[SIB : SIB + ALL] = jnp.zeros((ALL, 16, BLOCK), f32)

    fetch.wait()

    def add_sure(k, _):
        acc_a[rows[4, k]] += sure_ref[k, 0]
        acc_b[rows[5, k]] += sure_ref[k, 1]
        return 0

    lax.fori_loop(0, SURE, add_sure, 0, unroll=8)

    def sums(c, s):
        rr[s, 0], rr[s + 1, 0] = first_sums(ww, s // 2, p_ref[rows[1, c]], p_ref[rows[1, c + 1]])
        rr[s, 1], rr[s + 1, 1] = second_sums(ww, s // 2, p_ref[rows[0, c]], p_ref[rows[0, c + 1]])

    def close(t):
        for s in range(GROUP):
            acc_a[rows[2, t * GROUP + s]] += rr[s, 0]
            acc_b[rows[3, t * GROUP + s]] += rr[s, 1]

    products = Products(qd, ww, a_ref, b_ref, lambda c: (rows[0, c], rows[1, c]))
    pipeline(jnp.maximum((total + GROUP - 1) // GROUP, 2), products, sums, close)

    def finish_own(k, _):
        out[k] = finish(acc_a[k] + acc_b[k], p_ref[k])
        return 0

    def finish_other(k, _):
        out[k] = finish(acc_b[k], p_ref[k])
        return 0

    lax.fori_loop(0, OWN, finish_own, 0, unroll=8)
    lax.fori_loop(OWN, ALL, finish_other, 0, unroll=8)

    @pl.when(n_help > 0)
    def _():
        lax.fori_loop(SIB, SIB + OWN, finish_own, 0, unroll=4)
        lax.fori_loop(SIB + OWN, SIB + ALL, finish_other, 0, unroll=4)

    @pl.when(n_help == 0)
    def _():
        out[SIB:] = jnp.zeros((ALL, 4, BLOCK), f32)


def finale(inv, far_ref, mom, force, out, sib_in, back_in, mb, ss, sr, s_sem, r_sem):
    ix, iy = lax.axis_index("gx"), lax.axis_index("gy")
    core = lax.rem(iy, 2)
    sy = iy + 1 - 2 * core
    lower, upper = lax.rem(ix + NX - 1, NX), lax.rem(ix + 1, NX)
    step = 2 * core - 1
    beyond = lax.rem(iy + step + NY, NY)
    sib_beyond = lax.rem(sy - step + NY, NY)
    beyond_sib = lax.rem(iy + 2 * step + NY, NY)
    barrier = pltpu.get_barrier_semaphore()
    peers = [(lower, iy), (upper, iy), (ix, sy), (ix, beyond), (lower, sy), (upper, sy), (ix, sib_beyond), (ix, beyond_sib)]
    for dev in peers:
        pl.semaphore_signal(barrier, inc=1, device_id=dev, device_id_type=MESH)
    for n in range(8):
        back_in[n, GHOST] = jnp.zeros((4, BLOCK), f32)
    near_side, away_side = OWN + GHOST * (3 - core), OWN + GHOST * (2 + core)
    sib_near, sib_away = SIB + OWN + GHOST * (2 + core), SIB + OWN + GHOST * (3 - core)
    pl.semaphore_wait(barrier, 8)
    share = pltpu.make_async_remote_copy(
        src_ref=force.at[SIB : SIB + OWN], dst_ref=sib_in, send_sem=ss, recv_sem=sr, device_id=(ix, sy),
        device_id_type=MESH,
    )
    sends = (
        (OWN, 1, (lower, iy)),
        (OWN + GHOST, 0, (upper, iy)),
        (away_side, 3, (ix, beyond)),
        (SIB + OWN, 5, (lower, sy)),
        (SIB + OWN + GHOST, 4, (upper, sy)),
        (sib_away, 7, (ix, sib_beyond)),
        (near_side, 2, (ix, sy)),
    )
    copies = [
        pltpu.make_async_remote_copy(
            src_ref=force.at[pl.ds(start, GHOST)], dst_ref=back_in.at[slot, 0:GHOST], send_sem=s_sem.at[slot],
            recv_sem=r_sem.at[slot], device_id=dev, device_id_type=MESH,
        )
        for start, slot, dev in sends
    ]
    for cp in copies:
        cp.start()
    share.start()
    for j in range(GHOST):
        back_in[6, j] = force[sib_near + j]
    wide = jnp.concatenate([mom[...], jnp.zeros((BLOCK - NX, BLOCK), f32)], axis=0).T
    for s in range(NX):
        mb[s] = jnp.broadcast_to(wide[0 : 2 * NY, s : s + 1], (2 * NY, BLOCK))
    centre_x = [lax.rem(ix + (2 * NX - 1 - s), NX).astype(f32) + 0.5 for s in range(NX)]
    sub = lax.broadcasted_iota(i32, (8, BLOCK), 0).astype(f32)
    def far(k, _):
        blk = far_ref[k]
        x, y, z = jnp.broadcast_to(blk[0:1], (8, BLOCK)), jnp.broadcast_to(blk[1:2], (8, BLOCK)), blk[2:3]
        base = z * z + far_core_sq
        dx = [x - cx for cx in centre_x]
        dx2 = [d * d for d in dx]
        hx = [None] * NX
        fy = total = None
        for g in range(2 * NY // 8):
            dy = y - (0.5 * sub + (4.0 * g + 0.25))
            by = dy * dy + base
            gy = None
            for s in range(NX):
                r = lax.rsqrt(by + dx2[s])
                w = (mb[s, 8 * g : 8 * g + 8, :] * r) * (r * r)
                hx[s] = w if g == 0 else hx[s] + w
                gy = w if s == 0 else gy + w
            total = gy if g == 0 else total + gy
            fy = dy * gy if g == 0 else fy + dy * gy
        fx = dx[0] * hx[0]
        for s in range(1, NX):
            fx = fx + dx[s] * hx[s]
        add = lambda t: jnp.sum(t, axis=0, keepdims=True)
        f = jnp.concatenate([add(fx), add(fy), z * add(total)], axis=0)
        where = pl.ds(pl.multiple_of(k * BLOCK, BLOCK), BLOCK)
        out[:, where] = blk[3:4] * f
        return 0

    lax.fori_loop(0, OWN, far, 0, unroll=2)
    for cp in copies:
        cp.wait()
    share.wait()
    lists = (0, 1, 3 - core, 2 + core, 0, 1, 3 - core, 2 + core)

    def combine(k, _):
        f = force[k] + sib_in[k]
        for n, q in enumerate(lists):
            f = f + back_in[n, inv[q, k]]
        where = pl.ds(pl.multiple_of(k * BLOCK, BLOCK), BLOCK)
        out[:, where] = out[:, where] + f[0:3]
        return 0

    lax.fori_loop(0, OWN, combine, 0, unroll=8)


VM, SM = pl.BlockSpec(memory_space=pltpu.VMEM), pl.BlockSpec(memory_space=pltpu.SMEM)
HB = pl.BlockSpec(memory_space=pltpu.HBM)
SDS = jax.ShapeDtypeStruct
DMA = pltpu.SemaphoreType.DMA


def body(segments, pair_list, pair_count, send_list, cell_ids):
    segs = segments.shape[1]
    a, b, p, own_sums, sure, far, mom, idx, cnt, inv = pl.pallas_call(
        exchange,
        name="exchange",
        out_shape=(
            SDS((SIB + OWN, BLOCK, BLOCK), bf16),
            SDS((2 * ALL, 48, 2 * BLOCK), bf16),
            SDS((2 * ALL, 16, BLOCK), bf16),
            SDS((OWN, 16, BLOCK), f32),
            SDS((SURE, 2, 16, BLOCK), f32),
            SDS((OWN, 4, BLOCK), f32),
            SDS((NX, BLOCK), f32),
            SDS((8, PAIRS), i32),
            SDS((2, BLOCK), i32),
            SDS((4, BLOCK), i32),
        ),
        in_specs=[HB, HB, HB, HB, SM],
        out_specs=(VM,) * 10,
        scratch_shapes=[
            pltpu.VMEM((9, segs), f32),
            pltpu.VMEM((1, segs), i32),
            pltpu.SMEM((4, GHOST), i32),
            pltpu.SMEM((2, PAIRS), i32),
            pltpu.VMEM((2, PAIRS), i32),
            pltpu.VMEM((1, BLOCK), i32),
            pltpu.VMEM((9, segs), f32),
            pltpu.VMEM((2, PAIRS), i32),
            pltpu.VMEM((1, BLOCK), i32),
            pltpu.VMEM((4, ROWS, BLOCK), f32),
            pltpu.VMEM((OWN, 8, BLOCK), f32),
            pltpu.VMEM((OWN, 1, BLOCK), f32),
            pltpu.VMEM((4, ROWS, BLOCK), f32),
            pltpu.VMEM((4, ROWS, BLOCK), f32),
            pltpu.VMEM((1, BLOCK), f32),
            pltpu.VMEM((16, BLOCK), f32),
            pltpu.VMEM((1, BLOCK), f32),
            pltpu.VMEM((16, BLOCK), f32),
            pltpu.VMEM((GROUP, BLOCK, 2 * BLOCK), f32),
            pltpu.VMEM((GROUP // 2, 2 * BLOCK, 2 * BLOCK), bf16),
            DMA((5,)), DMA((4,)), DMA((4,)), DMA((4,)), DMA((4,)), DMA, DMA, DMA, DMA,
        ],
        compiler_params=pltpu.CompilerParams(
            collective_id=0, has_side_effects=True, vmem_limit_bytes=24 * 2**20
        ),
    )(*[pltpu.with_memory_space_constraint(x, pltpu.HBM) for x in (segments, cell_ids.reshape(1, -1), send_list, pair_list.T)], pair_count)
    force = pl.pallas_call(
        pairs,
        name="pairs",
        out_shape=SDS((2 * ALL, 4, BLOCK), f32),
        in_specs=[SM] + [VM] * 6,
        out_specs=VM,
        scratch_shapes=[
            pltpu.VMEM((8, PAIRS), i32),
            pltpu.SMEM((8, PAIRS), i32),
            pltpu.VMEM((GROUP, BLOCK, 2 * BLOCK), f32),
            pltpu.VMEM((GROUP // 2, 2 * BLOCK, 2 * BLOCK), bf16),
            pltpu.VMEM((GROUP, 2, 16, BLOCK), f32),
            pltpu.VMEM((2 * ALL + 1, 16, BLOCK), f32),
            pltpu.VMEM((2 * ALL + 1, 16, BLOCK), f32),
            DMA,
        ],
        compiler_params=pltpu.CompilerParams(vmem_limit_bytes=24 * 2**20),
    )(cnt, idx, a, b, p, own_sums, sure)
    return pl.pallas_call(
        finale,
        name="finale",
        out_shape=SDS((3, segs), f32),
        in_specs=[SM, VM, VM, VM],
        out_specs=VM,
        scratch_shapes=[
            pltpu.VMEM((OWN, 4, BLOCK), f32),
            pltpu.VMEM((8, GHOST + 1, 4, BLOCK), f32),
            pltpu.VMEM((NX, 2 * NY, BLOCK), f32),
            DMA, DMA, DMA((8,)), DMA((8,)),
        ],
        compiler_params=pltpu.CompilerParams(
            collective_id=1, has_side_effects=True, vmem_limit_bytes=16 * 2**20
        ),
    )(inv, far, mom, force)


def solution(mesh):
    in_specs = (
        P(None, ("gx", "gy")),
        P(("gx", "gy"), None),
        P(("gx", "gy")),
        P(("gx", "gy"), None),
        P(("gx", "gy")),
    )
    out_specs = P(None, ("gx", "gy"))
    return jax.shard_map(body, mesh=mesh, in_specs=in_specs, out_specs=out_specs, check_vma=False)
```

```python
import functools

import jax
import jax.numpy as jnp
from jax import lax
from jax.experimental import pallas as pl
from jax.experimental.pallas import tpu as pltpu
from jax.sharding import PartitionSpec as P

f32, bf16, i32 = jnp.float32, jnp.bfloat16, jnp.int32
MESH = pl.DeviceIdType.MESH
BLOCK = 128
OWN = 64
GHOST = 16
ALL = OWN + 4 * GHOST
SIB = ALL
TRASH = 2 * ALL
SURE = 64
PAIRS = 512
NX, NY = 8, 32
GROUP = 16
KDIM = 96
ROWS = 9 * GHOST

strength = 0.2
core_sq = 0.05
far_gain = 0.5
far_core_sq = 0.1


def mm(a, b, nt=False):
    dims = (((1,), (1 if nt else 0,)), ((), ()))
    return lax.dot_general(a, b, dims, preferred_element_type=f32)


def split3(x):
    h = x.astype(bf16)
    r = x - h.astype(f32)
    m = r.astype(bf16)
    return h, m, (r - m.astype(f32)).astype(bf16)


def rows16(parts):
    missing = 16 - sum(p.shape[0] for p in parts)
    return jnp.concatenate(parts + [jnp.zeros((missing, BLOCK), f32)], axis=0)


def eye128():
    shape = (BLOCK, BLOCK)
    return (lax.broadcasted_iota(i32, shape, 0) == lax.broadcasted_iota(i32, shape, 1)).astype(bf16)


def neighbours(ix, iy):
    return (
        (lax.rem(ix + NX - 1, NX), iy),
        (lax.rem(ix + 1, NX), iy),
        (ix, lax.rem(iy + NY - 1, NY)),
        (ix, lax.rem(iy + 1, NY)),
    )


def features(raw, centre, eye, a_ref, b_ref, p_ref, k, with_a):
    pos = raw[0:3] - centre
    l, b = raw[3:6], raw[6:9]
    u = jnp.concatenate([b[0:1] * l, b[1:2] * l, b[2:3] * l], axis=0)
    norm = jnp.sum(pos * pos, axis=0, keepdims=True)
    one = jnp.ones((1, BLOCK), f32)
    zero9 = jnp.zeros((9, BLOCK), f32)
    b_ref[k, :, 0:BLOCK] = jnp.concatenate(split3(rows16([u])), axis=0)
    b_ref[k, :, BLOCK:] = jnp.concatenate(split3(rows16([zero9, pos, norm, one])), axis=0)
    p_ref[k] = rows16([t.astype(f32) for t in split3(pos)] + [one]).astype(bf16)
    if with_a:
        h, m, l = split3(rows16([strength * u, -2.0 * pos, one, norm + core_sq]))
        at = jnp.concatenate([h, h, m, m, h, l, jnp.zeros((BLOCK - KDIM, BLOCK), bf16)], axis=0)
        a_ref[k] = mm(eye, at, nt=True).astype(bf16)


def centre_of(ix, iy):
    r = lax.broadcasted_iota(i32, (3, BLOCK), 0)
    return jnp.where(r == 0, ix.astype(f32), jnp.where(r == 1, iy.astype(f32), 0.0)) + 0.5


def twice(p):
    return jnp.concatenate([p, p], axis=1)


def spread(b):
    h, m, l = b[0:16], b[16:32], b[32:48]
    return jnp.concatenate([h, m, h, m, l, h], axis=0)


def weigh(qd, ww, s):
    r = lax.rsqrt(qd[s, :, BLOCK:])
    w = (qd[s, :, 0:BLOCK] * r) * (r * r)
    wh = w.astype(bf16)
    half = slice(0, BLOCK) if s % 2 == 0 else slice(BLOCK, 2 * BLOCK)
    ww[s // 2, 0:BLOCK, half] = wh
    ww[s // 2, BLOCK:, half] = (w - wh.astype(f32)).astype(bf16)


def sums_over(w, p0, p1):
    f = mm(jnp.concatenate([twice(p0), twice(p1)], axis=0), w)
    return f[0:16, 0:BLOCK], f[16:32, BLOCK:]


def second_sums(ww, s, p0, p1):
    return sums_over(ww[s], p0, p1)


def first_sums(ww, s, p0, p1):
    w = ww[s]
    turned = [
        jnp.concatenate([w[r : r + BLOCK, 0:BLOCK].T, w[r : r + BLOCK, BLOCK:].T], axis=1) for r in (0, BLOCK)
    ]
    return sums_over(jnp.concatenate(turned, axis=0), p0, p1)


def pipeline(groups, products, sums, close=None):
    qd, ww = products.qd, products.ww

    def step(c, b, a):
        for s in range(0, GROUP, 2):
            if c is not None:
                sums(c * GROUP + s, s)
            if b:
                weigh(qd, ww, s)
                weigh(qd, ww, s + 1)
            if a is not None:
                for d in range(2):
                    products(a * GROUP + s + d, s + d)
        if c is not None and close is not None:
            close(c)

    def body(t, _):
        step(t - 2, True, t)
        return 0

    step(None, False, 0)
    step(None, True, 1)
    lax.fori_loop(2, groups, body, 0)
    step(groups - 2, True, None)
    step(groups - 1, False, None)


class Products:
    def __init__(self, qd, ww, a_ref, b_ref, pick):
        self.qd, self.ww, self.a_ref, self.b_ref, self.pick = qd, ww, a_ref, b_ref, pick

    def __call__(self, r, s):
        i, j = self.pick(r)
        self.qd[s] = mm(self.a_ref[i][:, 0:KDIM], spread(self.b_ref[j]))


def along(ix, iy, o):
    z, hi, core = iy // 4, lax.rem(iy // 2, 2), lax.rem(iy, 2)
    return ix, lax.rem(z + o % 8, 8) * 4 + hi * 2 + lax.rem(core + o // 8, 2)


def across(ix, iy, o):
    z, hi, core = iy // 4, lax.rem(iy // 2, 2), lax.rem(iy, 2)
    return lax.rem(ix + o % 8, 8), z * 4 + lax.rem(hi + o // 8, 2) * 2 + core


def exchange(seg_in, cells_in, send_in, list_in, count, a_ref, b_ref, p_ref, self_ref, sure_ref, far_ref, mom_out,
             idx_out, cnt_out, inv_out, seg, cells, send_list, plist, ids, cnt, sib_seg, sib_ids, sib_cnt, sib_ghost,
             main, last, out_buf, in_buf, row, part, row2, table, qd, ww, l_sem, s_sem, r_sem, ss, sr,
             s1, r1, s2, r2):
    ix, iy = lax.axis_index("gx"), lax.axis_index("gy")
    sib = (ix, iy + 1 - 2 * lax.rem(iy, 2))
    loads = [
        pltpu.make_async_copy(src, dst, l_sem.at[n])
        for n, (src, dst) in enumerate(
            ((seg_in, seg), (send_in, send_list), (cells_in, cells), (list_in, plist), (list_in, ids))
        )
    ]
    for cp in loads:
        cp.start()
    barrier = pltpu.get_barrier_semaphore()

    other_y = (ix, lax.rem(iy + 2 * lax.rem(iy, 2) + NY - 1, NY))
    for dev in [along(ix, iy, o) for o in range(1, 16)] + [across(ix, iy, o) for o in range(1, 16)] + [other_y]:
        pl.semaphore_signal(barrier, inc=1, device_id=dev, device_id_type=MESH)
    cnt[...] = jnp.full((1, BLOCK), count[0], i32)
    for cp in loads:
        cp.wait()
    for k in range(OWN):
        main[k] = seg[0:8, k * BLOCK : (k + 1) * BLOCK]
        last[k] = seg[8:9, k * BLOCK : (k + 1) * BLOCK]
    lanes = lax.broadcasted_iota(i32, (1, BLOCK), 1)
    for q in range(4):
        where = jnp.full((1, BLOCK), GHOST, i32)
        for j in range(GHOST):
            k = send_list[q, j]
            out_buf[q, 8 * j : 8 * j + 8, :] = main[k]
            out_buf[q, 8 * GHOST + j : 8 * GHOST + j + 1, :] = last[k]
            where = jnp.where(lanes == k, j, where)
        inv_out[q : q + 1, :] = where
    c = jnp.sum(seg[3:6, :] * seg[6:9, :], axis=0, keepdims=True)
    first = 2 * (ix * NY + iy)
    m0 = jnp.sum(jnp.where(cells[...] == first, c, 0.0))
    m1 = jnp.sum(jnp.where(cells[...] == first + 1, c, 0.0))
    mine = jnp.where(lanes == 2 * iy, m0, jnp.where(lanes == 2 * iy + 1, m1, 0.0))
    row[...] = mine
    part[15:16, :] = mine
    centre, sib_centre = centre_of(ix, iy), centre_of(ix, sib[1])
    eye = eye128()

    def build_own(k, _):
        raw = jnp.concatenate([main[k], last[k]], axis=0)
        features(raw, centre, eye, a_ref, b_ref, p_ref, k, True)
        weight = far_gain * jnp.sum(raw[3:6] * raw[6:9], axis=0, keepdims=True)
        far_ref[k] = jnp.concatenate([raw[0:2], raw[2:3] - 0.5, weight], axis=0)
        return 0

    lax.fori_loop(0, OWN, build_own, 0, unroll=16)
    pl.semaphore_wait(barrier, 31)
    for o in range(1, 16):
        pltpu.make_async_remote_copy(
            src_ref=row, dst_ref=part.at[o - 1 : o], send_sem=s1, recv_sem=r1,
            device_id=along(ix, iy, o), device_id_type=MESH,
        ).start()
    copies = []
    for q, dev in enumerate(neighbours(ix, iy)):
        copies.append(
            pltpu.make_async_remote_copy(
                src_ref=out_buf.at[q], dst_ref=in_buf.at[q ^ 1], send_sem=s_sem.at[q],
                recv_sem=r_sem.at[q ^ 1], device_id=dev, device_id_type=MESH,
            )
        )
        copies[-1].start()

    shares = [
        pltpu.make_async_remote_copy(
            src_ref=src, dst_ref=dst, send_sem=ss.at[n], recv_sem=sr.at[n], device_id=sib, device_id_type=MESH
        )
        for n, (src, dst) in enumerate(((seg, sib_seg), (ids, sib_ids), (cnt, sib_cnt), (in_buf, sib_ghost)))
    ]
    for cp in shares[:3]:
        cp.start()

    def own_sums(k, s):
        self_ref[k], self_ref[k + 1] = second_sums(ww, s // 2, p_ref[k], p_ref[k + 1])

    pipeline(OWN // GROUP, Products(qd, ww, a_ref, b_ref, lambda k: (k, k)), own_sums)
    for cp in shares[:3]:
        cp.wait()

    def build_sib(k, _):
        raw = sib_seg[:, pl.ds(pl.multiple_of(k * BLOCK, BLOCK), BLOCK)]
        features(raw, sib_centre, eye, a_ref, b_ref, p_ref, SIB + k, True)
        return 0

    lax.fori_loop(0, OWN, build_sib, 0, unroll=16)
    pltpu.make_async_copy(part.at[0:15], part.at[0:15], r1).wait()
    slab = jnp.sum(part[...], axis=0, keepdims=True)
    row2[...] = slab
    table[15:16, :] = slab
    for o in range(1, 16):
        pltpu.make_async_remote_copy(
            src_ref=row2, dst_ref=table.at[o - 1 : o], send_sem=s2, recv_sem=r2,
            device_id=across(ix, iy, o), device_id_type=MESH,
        ).start()

    for cp in copies:
        cp.wait()
    shares[3].start()
    def ghosts_of(buf, cen, base):
        def build(j, _):
            for q in range(4):
                raw = jnp.concatenate(
                    [buf[q, pl.ds(pl.multiple_of(8 * j, 8), 8), :], buf[q, pl.ds(8 * GHOST + j, 1), :]], axis=0
                )
                features(raw, cen, eye, a_ref, b_ref, p_ref, base + GHOST * q + j, False)
            return 0

        lax.fori_loop(0, GHOST, build, 0, unroll=8)

    ghosts_of(in_buf, centre, OWN)

    def sure_sums(k, s):
        sure_ref[k, 0], sure_ref[k + 1, 0] = first_sums(ww, s // 2, p_ref[plist[1, k]], p_ref[plist[1, k + 1]])
        sure_ref[k, 1], sure_ref[k + 1, 1] = second_sums(ww, s // 2, p_ref[plist[0, k]], p_ref[plist[0, k + 1]])

    pipeline(SURE // GROUP, Products(qd, ww, a_ref, b_ref, lambda k: (plist[0, k], plist[1, k])), sure_sums)
    idx_out[0:2, :] = ids[...]
    idx_out[2:4, :] = sib_ids[...] + SIB
    idx_out[4:8, :] = jnp.zeros((4, PAIRS), i32)
    cnt_out[0:1, :] = cnt[...]
    cnt_out[1:2, :] = sib_cnt[...]
    shares[3].wait()
    ghosts_of(sib_ghost, sib_centre, SIB + OWN)
    pltpu.make_async_copy(table.at[0:15], table.at[0:15], r2).wait()
    mom_out[...] = table[0:NX, :] + table[NX:, :]
    pltpu.make_async_copy(part.at[0:15], part.at[0:15], s1).wait()
    pltpu.make_async_copy(table.at[0:15], table.at[0:15], s2).wait()


def finish(acc, p):
    p = p.astype(f32)
    f = (p[0:3] + p[3:6] + p[6:9]) * acc[9:10] - (acc[0:3] + acc[3:6] + acc[6:9])
    return jnp.concatenate([f, jnp.zeros((1, BLOCK), f32)], axis=0)


def pairs(counts, lists, a_ref, b_ref, p_ref, self_ref, sure_ref, out, merged, rows, qd, ww, rr, acc_a, acc_b, sem):
    own_rows, sib_rows = counts[0, 0] - SURE, counts[1, 0] - SURE
    half = (own_rows + sib_rows + 1) // 2
    n_own = jnp.minimum(own_rows, half)
    n_help = jnp.maximum(sib_rows - half, 0)
    total = n_own + n_help
    r = lax.broadcasted_iota(i32, (1, PAIRS), 1)
    own_list = pltpu.roll(lists[...], PAIRS - SURE, 1)
    sib_list = pltpu.roll(lists[...], PAIRS - (SURE + half - n_own), 1)
    live = r < total
    i = jnp.where(r < n_own, own_list[0:1], sib_list[2:3])
    j = jnp.where(r < n_own, own_list[1:2], sib_list[3:4])
    merged[0:1, :] = jnp.where(live, i, 0)
    merged[1:2, :] = jnp.where(live, j, 0)
    merged[2:3, :] = jnp.where(live, i, TRASH)
    merged[3:4, :] = jnp.where(live, j, TRASH)
    merged[4:6, :] = lists[0:2, :]
    merged[6:8, :] = jnp.zeros((2, PAIRS), i32)
    fetch = pltpu.make_async_copy(merged, rows, sem)
    fetch.start()
    acc_a[0:OWN] = jnp.zeros((OWN, 16, BLOCK), f32)
    acc_b[0:OWN] = self_ref[...]
    acc_b[OWN:ALL] = jnp.zeros((ALL - OWN, 16, BLOCK), f32)

    @pl.when(n_help > 0)
    def _():
        acc_a[SIB : SIB + OWN] = jnp.zeros((OWN, 16, BLOCK), f32)
        acc_b[SIB : SIB + ALL] = jnp.zeros((ALL, 16, BLOCK), f32)

    fetch.wait()

    def add_sure(k, _):
        acc_a[rows[4, k]] += sure_ref[k, 0]
        acc_b[rows[5, k]] += sure_ref[k, 1]
        return 0

    lax.fori_loop(0, SURE, add_sure, 0, unroll=16)

    def sums(c, s):
        rr[s, 0], rr[s + 1, 0] = first_sums(ww, s // 2, p_ref[rows[1, c]], p_ref[rows[1, c + 1]])
        rr[s, 1], rr[s + 1, 1] = second_sums(ww, s // 2, p_ref[rows[0, c]], p_ref[rows[0, c + 1]])

    def close(t):
        for s in range(GROUP):
            acc_a[rows[2, t * GROUP + s]] += rr[s, 0]
            acc_b[rows[3, t * GROUP + s]] += rr[s, 1]

    products = Products(qd, ww, a_ref, b_ref, lambda c: (rows[0, c], rows[1, c]))
    pipeline(jnp.maximum((total + GROUP - 1) // GROUP, 2), products, sums, close)

    def finish_own(k, _):
        out[k] = finish(acc_a[k] + acc_b[k], p_ref[k])
        return 0

    def finish_other(k, _):
        out[k] = finish(acc_b[k], p_ref[k])
        return 0

    lax.fori_loop(0, OWN, finish_own, 0, unroll=16)
    lax.fori_loop(OWN, ALL, finish_other, 0, unroll=16)

    @pl.when(n_help > 0)
    def _():
        lax.fori_loop(SIB, SIB + OWN, finish_own, 0, unroll=4)
        lax.fori_loop(SIB + OWN, SIB + ALL, finish_other, 0, unroll=4)

    @pl.when(n_help == 0)
    def _():
        out[SIB:] = jnp.zeros((ALL, 4, BLOCK), f32)


def finale(inv, far_ref, mom, force, out, sib_in, back_in, mb, ss, sr, s_sem, r_sem):
    ix, iy = lax.axis_index("gx"), lax.axis_index("gy")
    core = lax.rem(iy, 2)
    sy = iy + 1 - 2 * core
    lower, upper = lax.rem(ix + NX - 1, NX), lax.rem(ix + 1, NX)
    step = 2 * core - 1
    beyond = lax.rem(iy + step + NY, NY)
    sib_beyond = lax.rem(sy - step + NY, NY)
    beyond_sib = lax.rem(iy + 2 * step + NY, NY)
    barrier = pltpu.get_barrier_semaphore()
    peers = [(lower, iy), (upper, iy), (ix, sy), (ix, beyond), (lower, sy), (upper, sy), (ix, sib_beyond), (ix, beyond_sib)]
    for dev in peers:
        pl.semaphore_signal(barrier, inc=1, device_id=dev, device_id_type=MESH)
    for n in range(8):
        back_in[n, GHOST] = jnp.zeros((4, BLOCK), f32)
    near_side, away_side = OWN + GHOST * (3 - core), OWN + GHOST * (2 + core)
    sib_near, sib_away = SIB + OWN + GHOST * (2 + core), SIB + OWN + GHOST * (3 - core)
    pl.semaphore_wait(barrier, 8)
    share = pltpu.make_async_remote_copy(
        src_ref=force.at[SIB : SIB + OWN], dst_ref=sib_in, send_sem=ss, recv_sem=sr, device_id=(ix, sy),
        device_id_type=MESH,
    )
    sends = (
        (OWN, 1, (lower, iy)),
        (OWN + GHOST, 0, (upper, iy)),
        (away_side, 3, (ix, beyond)),
        (SIB + OWN, 5, (lower, sy)),
        (SIB + OWN + GHOST, 4, (upper, sy)),
        (sib_away, 7, (ix, sib_beyond)),
        (near_side, 2, (ix, sy)),
    )
    copies = [
        pltpu.make_async_remote_copy(
            src_ref=force.at[pl.ds(start, GHOST)], dst_ref=back_in.at[slot, 0:GHOST], send_sem=s_sem.at[slot],
            recv_sem=r_sem.at[slot], device_id=dev, device_id_type=MESH,
        )
        for start, slot, dev in sends
    ]
    for cp in copies:
        cp.start()
    share.start()
    for j in range(GHOST):
        back_in[6, j] = force[sib_near + j]
    wide = jnp.concatenate([mom[...], jnp.zeros((BLOCK - NX, BLOCK), f32)], axis=0).T
    for s in range(NX):
        mb[s] = jnp.broadcast_to(wide[0 : 2 * NY, s : s + 1], (2 * NY, BLOCK))
    centre_x = [lax.rem(ix + (2 * NX - 1 - s), NX).astype(f32) + 0.5 for s in range(NX)]
    sub = lax.broadcasted_iota(i32, (8, BLOCK), 0).astype(f32)
    def far(k, _):
        blk = far_ref[k]
        x, y, z = jnp.broadcast_to(blk[0:1], (8, BLOCK)), jnp.broadcast_to(blk[1:2], (8, BLOCK)), blk[2:3]
        base = z * z + far_core_sq
        dx = [x - cx for cx in centre_x]
        dx2 = [d * d for d in dx]
        hx = [None] * NX
        fy = total = None
        for g in range(2 * NY // 8):
            dy = y - (0.5 * sub + (4.0 * g + 0.25))
            by = dy * dy + base
            gy = None
            for s in range(NX):
                r = lax.rsqrt(by + dx2[s])
                w = (mb[s, 8 * g : 8 * g + 8, :] * r) * (r * r)
                hx[s] = w if g == 0 else hx[s] + w
                gy = w if s == 0 else gy + w
            total = gy if g == 0 else total + gy
            fy = dy * gy if g == 0 else fy + dy * gy
        fx = dx[0] * hx[0]
        for s in range(1, NX):
            fx = fx + dx[s] * hx[s]
        add = lambda t: jnp.sum(t, axis=0, keepdims=True)
        f = jnp.concatenate([add(fx), add(fy), z * add(total)], axis=0)
        where = pl.ds(pl.multiple_of(k * BLOCK, BLOCK), BLOCK)
        out[:, where] = blk[3:4] * f
        return 0

    lax.fori_loop(0, OWN, far, 0, unroll=2)
    for cp in copies:
        cp.wait()
    share.wait()
    lists = (0, 1, 3 - core, 2 + core, 0, 1, 3 - core, 2 + core)

    def combine(k, _):
        f = force[k] + sib_in[k]
        for n, q in enumerate(lists):
            f = f + back_in[n, inv[q, k]]
        where = pl.ds(pl.multiple_of(k * BLOCK, BLOCK), BLOCK)
        out[:, where] = out[:, where] + f[0:3]
        return 0

    lax.fori_loop(0, OWN, combine, 0, unroll=16)


VM, SM = pl.BlockSpec(memory_space=pltpu.VMEM), pl.BlockSpec(memory_space=pltpu.SMEM)
HB = pl.BlockSpec(memory_space=pltpu.HBM)
SDS = jax.ShapeDtypeStruct
DMA = pltpu.SemaphoreType.DMA


def body(segments, pair_list, pair_count, send_list, cell_ids):
    segs = segments.shape[1]
    a, b, p, own_sums, sure, far, mom, idx, cnt, inv = pl.pallas_call(
        exchange,
        name="exchange",
        out_shape=(
            SDS((SIB + OWN, BLOCK, BLOCK), bf16),
            SDS((2 * ALL, 48, 2 * BLOCK), bf16),
            SDS((2 * ALL, 16, BLOCK), bf16),
            SDS((OWN, 16, BLOCK), f32),
            SDS((SURE, 2, 16, BLOCK), f32),
            SDS((OWN, 4, BLOCK), f32),
            SDS((NX, BLOCK), f32),
            SDS((8, PAIRS), i32),
            SDS((2, BLOCK), i32),
            SDS((4, BLOCK), i32),
        ),
        in_specs=[HB, HB, HB, HB, SM],
        out_specs=(VM,) * 10,
        scratch_shapes=[
            pltpu.VMEM((9, segs), f32),
            pltpu.VMEM((1, segs), i32),
            pltpu.SMEM((4, GHOST), i32),
            pltpu.SMEM((2, PAIRS), i32),
            pltpu.VMEM((2, PAIRS), i32),
            pltpu.VMEM((1, BLOCK), i32),
            pltpu.VMEM((9, segs), f32),
            pltpu.VMEM((2, PAIRS), i32),
            pltpu.VMEM((1, BLOCK), i32),
            pltpu.VMEM((4, ROWS, BLOCK), f32),
            pltpu.VMEM((OWN, 8, BLOCK), f32),
            pltpu.VMEM((OWN, 1, BLOCK), f32),
            pltpu.VMEM((4, ROWS, BLOCK), f32),
            pltpu.VMEM((4, ROWS, BLOCK), f32),
            pltpu.VMEM((1, BLOCK), f32),
            pltpu.VMEM((16, BLOCK), f32),
            pltpu.VMEM((1, BLOCK), f32),
            pltpu.VMEM((16, BLOCK), f32),
            pltpu.VMEM((GROUP, BLOCK, 2 * BLOCK), f32),
            pltpu.VMEM((GROUP // 2, 2 * BLOCK, 2 * BLOCK), bf16),
            DMA((5,)), DMA((4,)), DMA((4,)), DMA((4,)), DMA((4,)), DMA, DMA, DMA, DMA,
        ],
        compiler_params=pltpu.CompilerParams(
            collective_id=0, has_side_effects=True, vmem_limit_bytes=24 * 2**20
        ),
    )(*[pltpu.with_memory_space_constraint(x, pltpu.HBM) for x in (segments, cell_ids.reshape(1, -1), send_list, pair_list.T)], pair_count)
    force = pl.pallas_call(
        pairs,
        name="pairs",
        out_shape=SDS((2 * ALL, 4, BLOCK), f32),
        in_specs=[SM] + [VM] * 6,
        out_specs=VM,
        scratch_shapes=[
            pltpu.VMEM((8, PAIRS), i32),
            pltpu.SMEM((8, PAIRS), i32),
            pltpu.VMEM((GROUP, BLOCK, 2 * BLOCK), f32),
            pltpu.VMEM((GROUP // 2, 2 * BLOCK, 2 * BLOCK), bf16),
            pltpu.VMEM((GROUP, 2, 16, BLOCK), f32),
            pltpu.VMEM((2 * ALL + 1, 16, BLOCK), f32),
            pltpu.VMEM((2 * ALL + 1, 16, BLOCK), f32),
            DMA,
        ],
        compiler_params=pltpu.CompilerParams(vmem_limit_bytes=24 * 2**20),
    )(cnt, idx, a, b, p, own_sums, sure)
    return pl.pallas_call(
        finale,
        name="finale",
        out_shape=SDS((3, segs), f32),
        in_specs=[SM, VM, VM, VM],
        out_specs=VM,
        scratch_shapes=[
            pltpu.VMEM((OWN, 4, BLOCK), f32),
            pltpu.VMEM((8, GHOST + 1, 4, BLOCK), f32),
            pltpu.VMEM((NX, 2 * NY, BLOCK), f32),
            DMA, DMA, DMA((8,)), DMA((8,)),
        ],
        compiler_params=pltpu.CompilerParams(
            collective_id=1, has_side_effects=True, vmem_limit_bytes=16 * 2**20
        ),
    )(inv, far, mom, force)


def solution(mesh):
    in_specs = (
        P(None, ("gx", "gy")),
        P(("gx", "gy"), None),
        P(("gx", "gy")),
        P(("gx", "gy"), None),
        P(("gx", "gy")),
    )
    out_specs = P(None, ("gx", "gy"))
    return jax.shard_map(body, mesh=mesh, in_specs=in_specs, out_specs=out_specs, check_vma=False)
```
